256 devices in a mesh: node: 4 (over z_lo), tile: 8 (over x, core), slab: 8 (over y, z_hi).
Axes of the slice: x: 4, y: 4, z: 8 (z_hi: 2, z_lo: 4; z = z_hi * 4 + z_lo), core: 2. Of those that a mesh axis runs over, the one named last changes fastest.
Arguments:
- start_state: float32 [5, 128, 128, 128], P(None, 'tile', 'slab'), may hold values from -1.5 to 3.5, as said below
- iterate: float32 [4, 5, 128, 128, 128], P('node', None, 'tile', 'slab'), may hold values from -1.8 to 3.8
- wall_flags: int32 [2, 128, 128], P(None, 'tile'), may hold values 0 or 1
- reg_index: int32 [1], replicated, may hold values from 0 to 7
Outputs:
- new_iterate: float32 [4, 5, 128, 128, 128], P('node', None, 'tile', 'slab')
The draws below stay inside these ranges and needn't reach their ends.
Inputs may be any that keep to these rules, and one draw needn't show every extreme that they name: Concentration lies in 0.05 to 0.45 and shear rate is positive in start_state.
All inputs are finite; a program needn't handle non-finite values. No bound on the sum of `wall_flags` on one device may be relied on, other than what follows from the above.
Results may differ from the reference program's by a relative error of at most 0.0001.
Values sent between devices are 32-bit elements; how exact they have to be, the bound alone decides.
No kernel may reach another device: no remote copies, remote signals or barrier semaphores. Data moves between devices by JAX's collectives and lax.ppermute only.
A program may use at most 64 MiB of HBM per device.

```python
import jax
import jax.numpy as jnp
import numpy as np
from jax import lax

NODES = 4
SWEEPS = 2
NX = 128
NY = 128
NZ = 128


def shared_fields(key):
    keys = jax.random.split(key, 5)
    shape = (NX, NY, NZ)
    concen = jax.random.uniform(keys[0], shape, jnp.float32, 0.05, 0.45)
    shear = jax.random.uniform(keys[1], shape, jnp.float32, 0.5, 0.5 + 1.5)
    stream = 1.0 + 0.5 * jnp.clip(jax.random.normal(keys[2], shape, jnp.float32), -3.0, 3.0)
    normal = 0.3 * jnp.clip(jax.random.normal(keys[3], shape, jnp.float32), -3.0, 3.0)
    spanwise = 0.3 * jnp.clip(jax.random.normal(keys[4], shape, jnp.float32), -3.0, 3.0)
    return jnp.stack([concen, shear, stream, normal, spanwise])


def draw_start_state(key, part):
    return shared_fields(key)


def draw_iterate(key, part):
    base = shared_fields(key)
    key = jax.random.fold_in(key, 7)
    noise = 0.1 * jnp.clip(jax.random.normal(key, (NODES, 5, NX, NY, NZ), jnp.float32), -3.0, 3.0)
    return base[None] + noise


def touch_ends(drawn, key, least, largest):
    longest = drawn.shape.index(max(drawn.shape))
    spots = []
    for shift in (0, 1):
        where = [jax.random.randint(jax.random.fold_in(key, axis), (), 0, length) for axis, length in enumerate(drawn.shape)]
        where[longest] = (where[longest] + shift) % drawn.shape[longest]
        spots.append(tuple(where))
    return drawn.at[spots[0]].set(least).at[spots[1]].set(largest)


def setup_inputs(seed: int = 0) -> dict:
    key_list = jax.random.split(jax.random.key(seed), 5)
    return {
        "start_state": draw_start_state(jax.random.fold_in(key_list[4], 71), 0),
        "iterate": draw_iterate(jax.random.fold_in(key_list[4], 71), 0),
        "wall_flags": touch_ends((jax.random.randint(key_list[2], (2, NX, NZ), 0, 2) < 1).astype(jnp.int32), jax.random.fold_in(key_list[2], 1), 0, 1),
        "reg_index": jax.random.randint(key_list[3], (1,), 0, 8).astype(jnp.int32),
    }


step_length = 0.2

def quadrature_table():
    points = [0.25, 0.5, 0.75, 1.0]
    table = np.zeros((4, 4))
    for column in range(4):
        coeffs = [1.0]
        divisor = 1.0
        for other in range(4):
            if other != column:
                other_point = points[other]
                widened = [0.0] * (len(coeffs) + 1)
                for power, value in enumerate(coeffs):
                    widened[power + 1] += value
                    widened[power] -= other_point * value
                coeffs = widened
                divisor *= points[column] - other_point
        for line_index in range(4):
            position = points[line_index]
            total = 0.0
            for power, value in enumerate(coeffs):
                total += value * position ** (power + 1) / (power + 1)
            table[line_index, column] = total / divisor
    return table

def center(field):
    return field[1:-1, 1:-1]

def ddx(field):
    return 0.5 * (field[2:, 1:-1] - field[:-2, 1:-1])

def ddy(field):
    return 0.5 * (field[1:-1, 2:] - field[1:-1, :-2])

def ddz(field):
    middle = center(field)
    return 0.5 * (jnp.roll(middle, -1, axis=-1) - jnp.roll(middle, 1, axis=-1))

def laplace(field):
    middle = center(field)
    return field[2:, 1:-1] + field[:-2, 1:-1] + field[1:-1, 2:] + field[1:-1, :-2] + jnp.roll(middle, -1, axis=-1) + jnp.roll(middle, 1, axis=-1) - 6.0 * middle

def gradient_dot(first, second):
    return ddx(first) * ddx(second) + ddy(first) * ddy(second) + ddz(first) * ddz(second)

def tendency(padded, exponent):
    concen = padded[0]
    shear = padded[1]
    stream = padded[2]
    normal = padded[3]
    spanwise = padded[4]
    regular = jnp.power(shear * shear + 0.25, 0.5 * exponent)
    flux_q = concen * regular
    viscous = 0.08 * (1.0 + 2.5 * concen + 6.2 * concen * concen) * regular
    stress = 0.5 * concen * concen * regular
    along = center(stream)
    across = center(normal)
    depth = center(spanwise)

    def carry_term(field):
        return along * ddx(field) + across * ddy(field) + depth * ddz(field)

    def diffuse(field):
        return center(viscous) * laplace(field) + gradient_dot(viscous, field)
    d_concen = -carry_term(concen) + 0.3 * (center(concen) * laplace(flux_q) + gradient_dot(concen, flux_q))
    strain = ddy(stream) ** 2 + ddy(spanwise) ** 2 + ddx(normal) ** 2 + ddz(normal) ** 2
    d_shear = 2.0 * (jnp.sqrt(strain + 0.25) - center(shear))
    d_stream = -carry_term(stream) + diffuse(stream) + 0.5
    d_normal = -carry_term(normal) + diffuse(normal) - ddy(stress)
    d_span = -carry_term(spanwise) + diffuse(spanwise)
    return jnp.stack([d_concen, d_shear, d_stream, d_normal, d_span])

def ghost_row(layer, flag):
    slip = 1.0 - 2.0 * flag.astype(jnp.float32)
    return jnp.stack([layer[0], layer[1], layer[2] * slip, -layer[3], layer[4] * slip])

def pad_state(state, wall_flags):
    padded = jnp.pad(state, ((0, 0), (1, 1), (1, 1), (0, 0)), mode='edge')
    lower = ghost_row(state[:, :, 0, :], wall_flags[0])
    upper = ghost_row(state[:, :, -1, :], wall_flags[1])
    padded = padded.at[:, 1:-1, 0, :].set(lower)
    return padded.at[:, 1:-1, -1, :].set(upper)

def reference(start_state, iterate, wall_flags, reg_index):
    exponent = 0.4 + 0.1 * reg_index[0].astype(jnp.float32)
    table = jnp.asarray(quadrature_table(), jnp.float32)

    def node_rate(state):
        return tendency(pad_state(state, wall_flags), exponent)
    for sweep in range(SWEEPS):
        rates = lax.map(node_rate, iterate)
        summed = jnp.einsum('mj,jabc->mabc', table, rates.reshape(rates.shape[0], 5, rates.shape[2], -1), precision=lax.Precision.HIGHEST).reshape(rates.shape)
        iterate = start_state[None] + step_length * summed
    return iterate
```

```python
import functools

import jax
import jax.numpy as jnp
import numpy as np
from jax import lax
from jax.experimental import pallas as pl
from jax.experimental.pallas import tpu as pltpu
from jax.sharding import PartitionSpec as P

STEP = 0.2
MAIN = 20
EDGE = 12
VMEM = pl.BlockSpec(memory_space=pltpu.VMEM)
SMEM = pl.BlockSpec(memory_space=pltpu.SMEM)


def quadrature_table():
    points = [0.25, 0.5, 0.75, 1.0]
    table = np.zeros((4, 4))
    for column in range(4):
        coeffs = [1.0]
        divisor = 1.0
        for other in range(4):
            if other != column:
                other_point = points[other]
                widened = [0.0] * (len(coeffs) + 1)
                for power, value in enumerate(coeffs):
                    widened[power + 1] += value
                    widened[power] -= other_point * value
                coeffs = widened
                divisor *= points[column] - other_point
        for line_index in range(4):
            position = points[line_index]
            total = 0.0
            for power, value in enumerate(coeffs):
                total += value * position ** (power + 1) / (power + 1)
            table[line_index, column] = total / divisor
    return table


def relative_table():
    table = np.asarray(quadrature_table(), np.float32) * np.float32(STEP)
    out = np.zeros((4, 4, 4), np.float32)
    for me in range(4):
        for a in range(4):
            for b in range(4):
                out[me, a, b] = table[me ^ a, me ^ b]
    return out.reshape(-1)


def iotas():
    sub = lax.broadcasted_iota(jnp.int32, (16, 128), 0)
    lane = lax.broadcasted_iota(jnp.int32, (16, 128), 1)
    return sub, lane


def derived(c, g, power):
    r = jnp.exp(power * jnp.log(g * g + 0.25))
    q = c * r
    eta = (0.08 + 0.2 * c + 0.496 * (c * c)) * r
    return q, eta, 0.5 * c * q


def rate(cen, lm, lp, sm, sp, zm, zp, lead_x):
    def diffs(f):
        dl = lp(f) - lm(f)
        ds = sp(f) - sm(f)
        return (dl, ds) if lead_x else (ds, dl)

    def grads(f):
        lo, hi, a, b, n, m = lm(f), lp(f), sm(f), sp(f), zm(f), zp(f)
        x, y = (hi - lo, b - a) if lead_x else (b - a, hi - lo)
        return x, y, m - n, (lo + hi) + (a + b) + (n + m)

    c, g, u, v, w, eta = cen(0), cen(1), cen(2), cen(3), cen(4), cen(6)
    hu, hv, hw = 0.5 * u, 0.5 * v, 0.5 * w
    qx, qy, qz, qsum = grads(5)
    cx, cy, cz, _ = grads(0)
    dc = 0.3 * c * (qsum - 6.0 * cen(5)) + (0.075 * qx - hu) * cx + (0.075 * qy - hv) * cy + (0.075 * qz - hw) * cz
    ex, ey, ez, _ = grads(6)
    ax, ay, az = 0.25 * ex - hu, 0.25 * ey - hv, 0.25 * ez - hw
    ux, uy, uz, usum = grads(2)
    du = eta * (usum - 6.0 * u) + ax * ux + ay * uy + az * uz + 0.5
    vx, vy, vz, vsum = grads(3)
    dv = eta * (vsum - 6.0 * v) + ax * vx + ay * vy + az * vz - 0.5 * diffs(7)[1]
    wx, wy, wz, wsum = grads(4)
    dw = eta * (wsum - 6.0 * w) + ax * wx + ay * wy + az * wz
    strain = uy * uy + wy * wy + vx * vx + vz * vz
    dg = jnp.sqrt(strain + 1.0) - 2.0 * g
    return dc, dg, du, dv, dw


def swap_blocks(tiles, axis, block, index):
    size = 4 * block
    low = index < 2 * block
    even = (index // block) % 2 == 0
    roll = lambda t, k: pltpu.roll(t, k, axis)
    a0, a1, a2, a3 = tiles
    lo0 = jnp.where(low, a0, roll(a2, 2 * block))
    hi0 = jnp.where(low, roll(a0, 2 * block), a2)
    lo1 = jnp.where(low, a1, roll(a3, 2 * block))
    hi1 = jnp.where(low, roll(a1, 2 * block), a3)
    out = []
    for p, q in ((lo0, lo1), (hi0, hi1)):
        out.append(jnp.where(even, p, roll(q, block)))
        out.append(jnp.where(even, roll(p, size - block), q))
    return out


def edges():
    me = lax.axis_index("node")
    t, s = lax.axis_index("tile"), lax.axis_index("slab")
    return me, t == 0, t == lax.axis_size("tile") - 1, s == 0, s == lax.axis_size("slab") - 1


def pick(tiles, me):
    out = tiles[3]
    for q in range(3):
        out = jnp.where(me == q, tiles[q], out)
    return out


def pack_z_edge(z_ref, f, xq, rows, lane):
    place = 4 * f + xq
    spot = lane % 32 == place
    for g in range(4):
        z_ref[g] = jnp.where(spot, pltpu.roll(rows[g], place + 1, 1), z_ref[g])
        z_ref[4 + g] = jnp.where(spot, pltpu.roll(rows[g], place + 96, 1), z_ref[4 + g])


def first_kernel(reg, s_ref, w_ref, slip_ref, m0, m1, m2, m3, wq_ref, wz_ref, slipq_ref, der, packed, zs):
    me = lax.axis_index("node")
    sub, lane = iotas()
    power = 0.2 + 0.05 * reg[0].astype(jnp.float32)

    def derive(x, _):
        q, eta, s = derived(s_ref[0, x], s_ref[1, x], power)
        der[0, x], der[1, x], der[2, x] = q, eta, s
        return _

    lax.fori_loop(0, 16, derive, 0)
    zs[...] = jnp.zeros_like(zs)

    def column(xq, _):
        rows = []
        for g in range(4):
            x = 4 * g + xq
            lo = jnp.maximum(x - 1, 0)
            hi = jnp.minimum(x + 1, 15)
            at = lambda f, r: s_ref[f, r] if f < 5 else der[f - 5, r]
            rows.append(rate(
                lambda f: at(f, x), lambda f: at(f, lo), lambda f: at(f, hi),
                lambda f: pltpu.roll(at(f, x), 1, 0), lambda f: pltpu.roll(at(f, x), 15, 0),
                lambda f: pltpu.roll(at(f, x), 1, 1), lambda f: pltpu.roll(at(f, x), 127, 1), True))
        for f in range(5):
            out = swap_blocks([rows[g][f] for g in range(4)], 1, 32, lane)
            for q in range(4):
                packed[q, f * 4 + xq] = out[q]
            own = [w_ref[f, 4 * g + xq] for g in range(4)]
            wq_ref[f * 4 + xq] = pick(swap_blocks(own, 1, 32, lane), me)
            pack_z_edge(zs, f, xq, own, lane)
        return _

    lax.fori_loop(0, 4, column, 0)
    for r, m in enumerate((m0, m1, m2, m3)):
        m[...] = packed[me ^ r]
    for side in range(2):
        wz_ref[side] = pick(swap_blocks([zs[4 * side + g] for g in range(4)], 1, 32, lane), me)
    zero = jnp.zeros((16, 128), jnp.float32)
    tiles = swap_blocks([zero, slip_ref[0], slip_ref[1], zero], 0, 4, sub)
    slipq_ref[...] = pick(swap_blocks(tiles, 1, 32, lane), me)


def slab_kernel(s_ref, lo_ref, hi_ref, wq_ref, up_ref, down_ref):
    _, t0, t7, _, _ = edges()
    for f in range(5):
        for ref, ys, y in ((up_ref, (14, 15), 15), (down_ref, (0, 1), 0)):
            for k in range(2):
                ref[f, pl.ds(16 * k, 16), :] = s_ref[f, pl.ds(ys[k], 16, stride=16), :]
            ref[f, pl.ds(32, 1), :] = jnp.where(
                t0, s_ref[f, pl.ds(y, 1), :], lo_ref[pl.ds((f * 3 + 1) * 16 + y, 1), :])
            ref[f, pl.ds(33, 1), :] = jnp.where(
                t7, s_ref[f, pl.ds(240 + y, 1), :], hi_ref[pl.ds(f * 48 + y, 1), :])
            for xq in range(4):
                ref[f, pl.ds(34 + xq, 1), :] = wq_ref[f * 4 + xq, pl.ds(y, 1), :]
            ref[f, pl.ds(38, 2), :] = jnp.zeros((2, 128), jnp.float32)


def edge_kernel(reg, s_ref, lo_ref, hi_ref, below_ref, above_ref, slip_ref, wq_ref, wz_ref,
                e0, e1, e2, e3, wxy_ref, ext, yh, band, packed, zs, edge):
    me, t0, t7, s0, s7 = edges()
    sub, lane = iotas()
    power = 0.2 + 0.05 * reg[0].astype(jnp.float32)

    for f in range(5):
        lo = lambda r: lo_ref[pl.ds((f * 3 + r) * 16, 16), :]
        hi = lambda r: hi_ref[pl.ds((f * 3 + r) * 16, 16), :]
        first, last = s_ref[f, pl.ds(0, 16), :], s_ref[f, pl.ds(240, 16), :]
        ext[f, 0] = lo(0)
        ext[f, 1] = jnp.where(t0, first, lo(1))
        ext[f, 18] = jnp.where(t7, last, hi(0))
        ext[f, 19] = hi(1)
        for x in range(16):
            ext[f, x + 2] = s_ref[f, pl.ds(16 * x, 16), :]

    def derive(x, _):
        q, eta, s = derived(ext[0, x], ext[1, x], power)
        ext[5, x], ext[6, x], ext[7, x] = q, eta, s
        return _

    lax.fori_loop(0, 20, derive, 0)

    for side in range(2):
        ref = (below_ref, above_ref)[side]
        near = 16 if side == 0 else 0
        y = 0 if side == 0 else 15
        wall = (s0, s7)[side]
        slip = slip_ref[side]
        slip_lo = lo_ref[pl.ds(240 + side, 1), :]
        slip_hi = hi_ref[pl.ds(240 + side, 1), :]
        for f in range(5):
            def ghost(value, flag):
                return -value if f == 3 else value * flag if f in (2, 4) else value

            mine = s_ref[f, pl.ds(y, 16, stride=16), :]
            yh[f, side, pl.ds(0, 16), :] = jnp.where(wall, ghost(mine, slip), ref[f, pl.ds(near, 16), :])
            yh[f, side, pl.ds(16, 1), :] = jnp.where(
                wall, ghost(ext[f, 1, pl.ds(y, 1), :], slip_lo), ref[f, pl.ds(32, 1), :])
            yh[f, side, pl.ds(17, 1), :] = jnp.where(
                wall, ghost(ext[f, 18, pl.ds(y, 1), :], slip_hi), ref[f, pl.ds(33, 1), :])
            yh[f, side, pl.ds(18, 6), :] = jnp.zeros((6, 128), jnp.float32)
            far = 0 if side == 0 else 16
            band[f, side, 0] = ref[f, pl.ds(far, 16), :]
            band[f, side, 1] = ref[f, pl.ds(near, 16), :]
            band[f, side, 2] = mine
        q, eta, s = derived(yh[0, side], yh[1, side], power)
        yh[5, side], yh[6, side], yh[7, side] = q, eta, s
        for k in range(3):
            q, eta, s = derived(band[0, side, k], band[1, side, k], power)
            band[5, side, k], band[6, side, k], band[7, side, k] = q, eta, s

    def row(x, place):
        def below(f):
            return jnp.where(sub == 0, yh[f, 0, pl.ds(place, 1), :], pltpu.roll(ext[f, x], 1, 0))

        def above(f):
            return jnp.where(sub == 15, yh[f, 1, pl.ds(place, 1), :], pltpu.roll(ext[f, x], 15, 0))

        return rate(
            lambda f: ext[f, x], lambda f: ext[f, x - 1], lambda f: ext[f, x + 1], below, above,
            lambda f: pltpu.roll(ext[f, x], 1, 1), lambda f: pltpu.roll(ext[f, x], 127, 1), True)

    zs[...] = jnp.zeros_like(zs)

    def column(xq, _):
        rows = [row(4 * g + xq + 2, 4 * g + xq) for g in range(4)]
        for f in range(5):
            own = [rows[g][f] for g in range(4)]
            out = swap_blocks(own, 1, 32, lane)
            for q in range(4):
                packed[q, f * 4 + xq] = out[q]
            pack_z_edge(zs, f, xq, own, lane)
        return _

    lax.fori_loop(0, 4, column, 0)
    for side in range(2):
        out = swap_blocks([zs[4 * side + g] for g in range(4)], 1, 32, lane)
        for q in range(4):
            edge[q, 10 + side] = out[q]

    lower, upper = row(1, 16), row(18, 17)
    for f in range(5):
        for q in range(4):
            x_edge = jnp.where(
                lane < 32, packed[q, f * 4],
                jnp.where(lane < 64, pltpu.roll(lower[f], (32 * (1 - q)) % 128, 1),
                          jnp.where(lane < 96, pltpu.roll(upper[f], (32 * (2 - q)) % 128, 1), packed[q, f * 4 + 3])))
            edge[q, f] = x_edge

    def band_rate(side):
        def lo(f):
            return jnp.where(sub == 0, yh[f, side, pl.ds(16, 1), :], pltpu.roll(band[f, side, 1], 1, 0))

        def hi(f):
            return jnp.where(sub == 15, yh[f, side, pl.ds(17, 1), :], pltpu.roll(band[f, side, 1], 15, 0))

        before, after = (0, 2) if side == 0 else (2, 0)
        return rate(
            lambda f: band[f, side, 1], lambda f: band[f, side, before], lambda f: band[f, side, after], lo, hi,
            lambda f: pltpu.roll(band[f, side, 1], 1, 1), lambda f: pltpu.roll(band[f, side, 1], 127, 1), False)

    lower, upper = band_rate(0), band_rate(1)
    zero = jnp.zeros((16, 128), jnp.float32)
    for f in range(5):
        tiles = swap_blocks([zero, lower[f], upper[f], zero], 0, 4, sub)
        out = swap_blocks(tiles, 1, 32, lane)
        for q in range(4):
            edge[q, 5 + f] = out[q]
            for xq in range(4):
                edge[q, 5 + f, pl.ds(xq, 1), :] = packed[q, f * 4 + xq, pl.ds(0, 1), :]
                edge[q, 5 + f, pl.ds(12 + xq, 1), :] = packed[q, f * 4 + xq, pl.ds(15, 1), :]
    for r, e in enumerate((e0, e1, e2, e3)):
        e[...] = edge[me ^ r]

    for f in range(5):
        a = pltpu.roll(lo_ref[pl.ds((f * 3 + 2) * 16, 16), :], (5 - me) % 4 * 32, 1)
        b = pltpu.roll(hi_ref[pl.ds((f * 3 + 2) * 16, 16), :], (6 - me) % 4 * 32, 1)
        wxy_ref[f] = jnp.where(
            lane < 32, wq_ref[f * 4], jnp.where(lane < 64, a, jnp.where(lane < 96, b, wq_ref[f * 4 + 3])))
        wxy_ref[5 + f, pl.ds(4, 4), :] = below_ref[f, pl.ds(34, 4), :]
        wxy_ref[5 + f, pl.ds(8, 4), :] = above_ref[f, pl.ds(34, 4), :]
        for xq in range(4):
            wxy_ref[5 + f, pl.ds(xq, 1), :] = wq_ref[f * 4 + xq, pl.ds(0, 1), :]
            wxy_ref[5 + f, pl.ds(12 + xq, 1), :] = wq_ref[f * 4 + xq, pl.ds(15, 1), :]
    for side in range(2):
        wxy_ref[10 + side] = wz_ref[side]


def second_kernel(reg, weights, a0, a1, a2, a3, b0, b1, b2, b3, wq_ref, wxy_ref, slipq_ref,
                  o0, o1, o2, o3, main, xh, yh, zh, rates):
    me, t0, t7, s0, s7 = edges()
    sub, lane = iotas()
    power = 0.2 + 0.05 * reg[0].astype(jnp.float32)
    slip = slipq_ref[...]
    at_lower = jnp.logical_and(jnp.logical_and(sub >= 4, sub < 8), s0)
    at_upper = jnp.logical_and(jnp.logical_and(sub >= 8, sub < 12), s7)
    arrived, edge = (a0, a1, a2, a3), (b0, b1, b2, b3)

    def node(m, _):
        weight = [weights[me * 16 + m * 4 + r] for r in range(4)]

        def mix(start, refs, k):
            out = start
            for r in range(4):
                out = out + weight[r] * refs[r][k]
            return out

        for f in range(5):
            xb = mix(wxy_ref[f], edge, f)
            yb = mix(wxy_ref[5 + f], edge, 5 + f)
            yh[f] = yb
            for xq in range(4):
                tile = mix(wq_ref[f * 4 + xq], arrived, f * 4 + xq)
                if xq == 0:
                    tile = jnp.where(lane < 32, xb, tile)
                if xq == 3:
                    tile = jnp.where(lane >= 96, xb, tile)
                tile = jnp.where(sub == 0, yh[f, pl.ds(xq, 1), :], tile)
                tile = jnp.where(sub == 15, yh[f, pl.ds(12 + xq, 1), :], tile)
                main[f, xq] = tile
            xh[f] = jnp.where(
                lane < 64, jnp.where(t0, xb, pltpu.roll(xb, 96, 1)), jnp.where(t7, xb, pltpu.roll(xb, 32, 1)))
            lower, upper = pltpu.roll(yb, 4, 0), pltpu.roll(yb, 12, 0)
            if f == 3:
                lower, upper = -lower, -upper
            if f in (2, 4):
                lower, upper = lower * slip, upper * slip
            yh[f] = jnp.where(at_lower, lower, jnp.where(at_upper, upper, yb))
        for xq in range(4):
            main[5, xq], main[6, xq], main[7, xq] = derived(main[0, xq], main[1, xq], power)
        xh[5], xh[6], xh[7] = derived(xh[0], xh[1], power)
        yh[5], yh[6], yh[7] = derived(yh[0], yh[1], power)
        for side in range(2):
            z = mix(wxy_ref[10 + side], edge, 10 + side)
            zh[0, side] = z
            q, eta, _s = derived(z, pltpu.roll(z, 124, 1), power)
            zh[1, side], zh[2, side] = q, eta
        for xq in range(4):
            def left(f):
                if xq > 0:
                    return main[f, xq - 1]
                return jnp.where(lane < 32, xh[f], pltpu.roll(main[f, 3], 32, 1))

            def right(f):
                if xq < 3:
                    return main[f, xq + 1]
                return jnp.where(lane >= 96, xh[f], pltpu.roll(main[f, 0], 96, 1))

            def below(f):
                return jnp.where(sub == 0, yh[f, pl.ds(4 + xq, 1), :], pltpu.roll(main[f, xq], 1, 0))

            def above(f):
                return jnp.where(sub == 15, yh[f, pl.ds(8 + xq, 1), :], pltpu.roll(main[f, xq], 15, 0))

            def spot(f):
                return (0, 4 * f + xq) if f < 5 else (f - 4, xq)

            def before(f):
                k, i = spot(f)
                return jnp.where(lane % 32 == 0, pltpu.roll(zh[k, 0], (128 - i) % 128, 1), pltpu.roll(main[f, xq], 1, 1))

            def after(f):
                k, i = spot(f)
                return jnp.where(lane % 32 == 31, pltpu.roll(zh[k, 1], 31 - i, 1), pltpu.roll(main[f, xq], 127, 1))

            out = rate(lambda f: main[f, xq], left, right, below, above, before, after, True)
            for f in range(5):
                rates[m, f * 4 + xq] = out[f]
        return _

    lax.fori_loop(0, 4, node, 0)
    weight = [[weights[me * 16 + m * 4 + r] for r in range(4)] for m in range(4)]

    def combine(k, _):
        have = [rates[r, k] for r in range(4)]
        for m, o in enumerate((o0, o1, o2, o3)):
            out = wq_ref[k]
            for r in range(4):
                out = out + weight[m][r] * have[r]
            o[k] = out
        return _

    lax.fori_loop(0, MAIN, combine, 0)


def last_kernel(r0, r1, r2, r3, out_ref, quarter):
    me = lax.axis_index("node")
    _, lane = iotas()
    for r, ref in enumerate((r0, r1, r2, r3)):
        quarter[me ^ r] = ref[...]

    def column(k, _):
        tiles = swap_blocks([quarter[q, k] for q in range(4)], 1, 32, lane)
        for g in range(4):
            out_ref[k // 4, 4 * g + k % 4] = tiles[g]
        return _

    lax.fori_loop(0, MAIN, column, 0)


def tiles_of(n):
    return jax.ShapeDtypeStruct((n, 16, 128), jnp.float32)


def shards(start_state, iterate, wall_flags, reg_index):
    state = iterate[0]
    flat = state.reshape(5, 256, 128)
    slip = 1.0 - 2.0 * wall_flags.astype(jnp.float32)
    size = lax.axis_size("tile")
    ring_up = [(i, (i + 1) % size) for i in range(size)]
    ring_down = [(j, i) for i, j in ring_up]
    params = pltpu.CompilerParams(vmem_limit_bytes=48 * 1024 * 1024)
    scratch = lambda *shape: pltpu.VMEM(shape + (16, 128), jnp.float32)

    def tile_message(a, b, w):
        rows = jnp.concatenate([state[:, a:b], start_state[:, w:w + 1]], axis=1).reshape(240, 128)
        return jnp.concatenate([rows, slip[:, w], jnp.zeros((6, 128), jnp.float32)], axis=0)

    from_lower = lax.ppermute(tile_message(14, 16, 15), "tile", ring_up)
    from_upper = lax.ppermute(tile_message(0, 2, 0), "tile", ring_down)

    m0, m1, m2, m3, wq, wz, slipq = pl.pallas_call(
        first_kernel,
        out_shape=[tiles_of(MAIN)] * 5 + [tiles_of(2), jax.ShapeDtypeStruct((16, 128), jnp.float32)],
        in_specs=[SMEM] + [VMEM] * 3,
        out_specs=[VMEM] * 7,
        scratch_shapes=[scratch(3, 16), scratch(4, MAIN), scratch(8)],
        compiler_params=params,
    )(reg_index, state, start_state, slip)

    slab_shape = jax.ShapeDtypeStruct((5, 40, 128), jnp.float32)
    up, down = pl.pallas_call(
        slab_kernel,
        out_shape=[slab_shape] * 2,
        in_specs=[VMEM] * 4,
        out_specs=[VMEM] * 2,
        compiler_params=params,
    )(flat, from_lower, from_upper, wq)
    from_below = lax.ppermute(up, "slab", ring_up)
    from_above = lax.ppermute(down, "slab", ring_down)

    xor = lambda r: [(i, i ^ r) for i in range(4)]
    arrived = [m0] + [lax.ppermute(m, "node", xor(r)) for r, m in ((1, m1), (2, m2), (3, m3))]

    e0, e1, e2, e3, wxy = pl.pallas_call(
        edge_kernel,
        out_shape=[tiles_of(EDGE)] * 5,
        in_specs=[SMEM] + [VMEM] * 8,
        out_specs=[VMEM] * 5,
        scratch_shapes=[
            scratch(8, 20), pltpu.VMEM((8, 2, 24, 128), jnp.float32), scratch(8, 2, 3),
            scratch(4, MAIN), scratch(8), scratch(4, EDGE)],
        compiler_params=params,
    )(reg_index, flat, from_lower, from_upper, from_below, from_above, slip, wq, wz)
    edge = [e0] + [lax.ppermute(e, "node", xor(r)) for r, e in ((1, e1), (2, e2), (3, e3))]

    weights = jnp.asarray(relative_table())
    outs = pl.pallas_call(
        second_kernel,
        out_shape=[tiles_of(MAIN)] * 4,
        in_specs=[SMEM] * 2 + [VMEM] * 11,
        out_specs=[VMEM] * 4,
        scratch_shapes=[scratch(8, 4), scratch(8), scratch(8), scratch(3, 2), scratch(4, MAIN)],
        compiler_params=params,
    )(reg_index, weights, *arrived, *edge, wq, wxy, slipq)
    back = [outs[0]] + [lax.ppermute(outs[r], "node", xor(r)) for r in (1, 2, 3)]

    result = pl.pallas_call(
        last_kernel,
        out_shape=jax.ShapeDtypeStruct((5, 16, 16, 128), jnp.float32),
        in_specs=[VMEM] * 4,
        out_specs=VMEM,
        scratch_shapes=[scratch(4, MAIN)],
        compiler_params=params,
    )(*back)
    return result[None]


def solution(mesh):
    return jax.shard_map(
        shards,
        mesh=mesh,
        in_specs=(
            P(None, "tile", "slab", None),
            P("node", None, "tile", "slab", None),
            P(None, "tile", None),
            P(),
        ),
        out_specs=P("node", None, "tile", "slab", None),
        check_vma=False,
    )
```

```python
import jax
import jax.numpy as jnp
import numpy as np
from jax import lax
from jax.experimental import pallas as pl
from jax.experimental.pallas import tpu as pltpu
from jax.sharding import PartitionSpec as P

STEP = 0.2
MAIN = 20
EDGE = 12
VMEM = pl.BlockSpec(memory_space=pltpu.VMEM)
SMEM = pl.BlockSpec(memory_space=pltpu.SMEM)
ANY = pl.BlockSpec(memory_space=pl.ANY)
HBM = pl.BlockSpec(memory_space=pltpu.HBM)


def quadrature_table():
    points = [0.25, 0.5, 0.75, 1.0]
    table = np.zeros((4, 4))
    for column in range(4):
        coeffs = [1.0]
        divisor = 1.0
        for other in range(4):
            if other != column:
                other_point = points[other]
                widened = [0.0] * (len(coeffs) + 1)
                for power, value in enumerate(coeffs):
                    widened[power + 1] += value
                    widened[power] -= other_point * value
                coeffs = widened
                divisor *= points[column] - other_point
        for line_index in range(4):
            position = points[line_index]
            total = 0.0
            for power, value in enumerate(coeffs):
                total += value * position ** (power + 1) / (power + 1)
            table[line_index, column] = total / divisor
    return table


def relative_weights(me):
    table = np.asarray(quadrature_table(), np.float32) * np.float32(STEP)

    def entry(a, b):
        value = jnp.float32(table[3 ^ a, 3 ^ b])
        for node in range(3):
            value = jnp.where(me == node, jnp.float32(table[node ^ a, node ^ b]), value)
        return value

    return [[entry(a, b) for b in range(4)] for a in range(4)]


def iotas():
    sub = lax.broadcasted_iota(jnp.int32, (16, 128), 0)
    lane = lax.broadcasted_iota(jnp.int32, (16, 128), 1)
    return sub, lane


def derived(c, g, power):
    r = jnp.exp(power * jnp.log(g * g + 0.25))
    q = c * r
    eta = (0.08 + 0.2 * c + 0.496 * (c * c)) * r
    return q, eta, 0.5 * c * q


def rate(cen, lm, lp, sm, sp, zm, zp, lead_x):
    def diffs(f):
        dl = lp(f) - lm(f)
        ds = sp(f) - sm(f)
        return (dl, ds) if lead_x else (ds, dl)

    def grads(f):
        lo, hi, a, b, n, m = lm(f), lp(f), sm(f), sp(f), zm(f), zp(f)
        x, y = (hi - lo, b - a) if lead_x else (b - a, hi - lo)
        return x, y, m - n, (lo + hi) + (a + b) + (n + m)

    c, g, u, v, w, eta = cen(0), cen(1), cen(2), cen(3), cen(4), cen(6)
    hu, hv, hw = 0.5 * u, 0.5 * v, 0.5 * w
    qx, qy, qz, qsum = grads(5)
    cx, cy, cz, _ = grads(0)
    dc = 0.3 * c * (qsum - 6.0 * cen(5)) + (0.075 * qx - hu) * cx + (0.075 * qy - hv) * cy + (0.075 * qz - hw) * cz
    ex, ey, ez, _ = grads(6)
    ax, ay, az = 0.25 * ex - hu, 0.25 * ey - hv, 0.25 * ez - hw
    ux, uy, uz, usum = grads(2)
    du = eta * (usum - 6.0 * u) + ax * ux + ay * uy + az * uz + 0.5
    vx, vy, vz, vsum = grads(3)
    dv = eta * (vsum - 6.0 * v) + ax * vx + ay * vy + az * vz - 0.5 * diffs(7)[1]
    wx, wy, wz, wsum = grads(4)
    dw = eta * (wsum - 6.0 * w) + ax * wx + ay * wy + az * wz
    strain = uy * uy + wy * wy + vx * vx + vz * vz
    dg = jnp.sqrt(strain + 1.0) - 2.0 * g
    return dc, dg, du, dv, dw


def swap_blocks(tiles, axis, block, index):
    size = 4 * block
    low = index < 2 * block
    even = (index // block) % 2 == 0
    roll = lambda t, k: pltpu.roll(t, k, axis)
    a0, a1, a2, a3 = tiles
    lo0 = jnp.where(low, a0, roll(a2, 2 * block))
    hi0 = jnp.where(low, roll(a0, 2 * block), a2)
    lo1 = jnp.where(low, a1, roll(a3, 2 * block))
    hi1 = jnp.where(low, roll(a1, 2 * block), a3)
    out = []
    for p, q in ((lo0, lo1), (hi0, hi1)):
        out.append(jnp.where(even, p, roll(q, block)))
        out.append(jnp.where(even, roll(p, size - block), q))
    return out


def edges():
    me = lax.axis_index("node")
    t, s = lax.axis_index("tile"), lax.axis_index("slab")
    return me, t == 0, t == lax.axis_size("tile") - 1, s == 0, s == lax.axis_size("slab") - 1


def pick(tiles, me):
    out = tiles[3]
    for q in range(3):
        out = jnp.where(me == q, tiles[q], out)
    return out


def pack_z_edge(z_ref, f, xq, rows, lane):
    place = 4 * f + xq
    spot = lane % 32 == place
    for g in range(4):
        z_ref[g] = jnp.where(spot, pltpu.roll(rows[g], place + 1, 1), z_ref[g])
        z_ref[4 + g] = jnp.where(spot, pltpu.roll(rows[g], place + 96, 1), z_ref[4 + g])


def slip_of(flags):
    return 1.0 - 2.0 * flags.astype(jnp.float32)


def tile_kernel(s_ref, w_ref, flag_ref, _after, up_ref, down_ref):
    for ref, rows, edge in ((up_ref, (14, 15), 15), (down_ref, (0, 1), 0)):
        for f in range(5):
            ref[f] = s_ref[f, rows[0]]
            ref[5 + f] = s_ref[f, rows[1]]
            ref[10 + f] = w_ref[f, edge]
        ref[15] = jnp.zeros((16, 128), jnp.float32)
        for side in range(2):
            ref[15, pl.ds(side, 1), :] = slip_of(flag_ref[side, pl.ds(edge, 1), :])


def first_kernel(reg, s_ref, _after, m0, m1, m2, m3, der, packed):
    me = lax.axis_index("node")
    sub, lane = iotas()
    power = 0.2 + 0.05 * reg[0].astype(jnp.float32)

    def derive(k, _):
        x = pl.ds(4 * k, 4)
        der[0, x], der[1, x], der[2, x] = derived(s_ref[0, x], s_ref[1, x], power)
        return _

    lax.fori_loop(0, 4, derive, 0)

    def column(xq, _):
        rows = []
        for g in range(4):
            x = 4 * g + xq
            lo = jnp.maximum(x - 1, 0)
            hi = jnp.minimum(x + 1, 15)
            at = lambda f, r: s_ref[f, r] if f < 5 else der[f - 5, r]
            rows.append(rate(
                lambda f: at(f, x), lambda f: at(f, lo), lambda f: at(f, hi),
                lambda f: pltpu.roll(at(f, x), 1, 0), lambda f: pltpu.roll(at(f, x), 15, 0),
                lambda f: pltpu.roll(at(f, x), 1, 1), lambda f: pltpu.roll(at(f, x), 127, 1), True))
        for f in range(5):
            out = swap_blocks([rows[g][f] for g in range(4)], 1, 32, lane)
            for q in range(4):
                packed[q, f * 4 + xq] = out[q]
        return _

    lax.fori_loop(0, 4, column, 0)
    for r, m in enumerate((m0, m1, m2, m3)):
        m[...] = packed[me ^ r]


def start_kernel(w_ref, flag_ref, _after, wq_ref, wz_ref, slipq_ref, zs):
    me = lax.axis_index("node")
    sub, lane = iotas()
    zs[...] = jnp.zeros_like(zs)
    for xq in range(4):
        for f in range(5):
            own = [w_ref[f, 4 * g + xq] for g in range(4)]
            wq_ref[f * 4 + xq] = pick(swap_blocks(own, 1, 32, lane), me)
            pack_z_edge(zs, f, xq, own, lane)
    for side in range(2):
        wz_ref[side] = pick(swap_blocks([zs[4 * side + g] for g in range(4)], 1, 32, lane), me)
    slipq_ref[...] = pack_y_edge(slip_of(flag_ref[0]), slip_of(flag_ref[1]), me, sub, lane)


def pack_y_edge(lower, upper, me, sub, lane):
    zero = jnp.zeros((16, 128), jnp.float32)
    tiles = swap_blocks([zero, lower, upper, zero], 0, 4, sub)
    return pick(swap_blocks(tiles, 1, 32, lane), me)


def slab_kernel(s_hbm, w_hbm, up_ref, down_ref, rows, sems):
    me = lax.axis_index("node")
    sub, lane = iotas()
    copies = []
    for k, (ref, ys) in enumerate(((up_ref, (14, 15)), (down_ref, (0, 1)))):
        for r in range(2):
            copies.append(pltpu.make_async_copy(
                s_hbm.at[:, :, ys[r], :], ref.at[:, pl.ds(16 * r, 16), :], sems.at[2 * k + r]))
        copies.append(pltpu.make_async_copy(w_hbm.at[:, :, (15, 0)[k], :], rows.at[k], sems.at[4 + k]))
    for copy in copies:
        copy.start()
    copies[2].wait()
    copies[5].wait()
    for f in range(5):
        start = pack_y_edge(rows[1, f], rows[0, f], me, sub, lane)
        for ref, place in ((up_ref, 8), (down_ref, 4)):
            ref[f, pl.ds(32, 4), :] = start[place:place + 4]
            ref[f, pl.ds(36, 4), :] = jnp.zeros((4, 128), jnp.float32)
    for k in (0, 1, 3, 4):
        copies[k].wait()


def corner_kernel(below_ref, above_ref, up_ref, down_ref):
    for ref, x in ((up_ref, 15), (down_ref, 0)):
        ref[pl.ds(10, 6), :] = jnp.zeros((6, 128), jnp.float32)
        for f in range(5):
            ref[pl.ds(f, 1), :] = below_ref[f, pl.ds(16 + x, 1), :]
            ref[pl.ds(5 + f, 1), :] = above_ref[f, pl.ds(x, 1), :]


def fill_ext(ext, s_ref, lo_ref, hi_ref, rows, t0, t7):
    for f in range(5):
        ext[f, 0] = lo_ref[f]
        ext[f, 1] = jnp.where(t0, s_ref[f, pl.ds(0, 16), :], lo_ref[5 + f])
        ext[f, 18] = jnp.where(t7, s_ref[f, pl.ds(240, 16), :], hi_ref[f])
        ext[f, 19] = hi_ref[5 + f]
        for x in rows:
            ext[f, x + 2] = s_ref[f, pl.ds(16 * x, 16), :]


def inner_kernel(reg, s_ref, lo_ref, hi_ref, out_ref, ext, zs):
    _, t0, t7, _, _ = edges()
    sub, lane = iotas()
    power = 0.2 + 0.05 * reg[0].astype(jnp.float32)
    fill_ext(ext, s_ref, lo_ref, hi_ref, range(16), t0, t7)

    def derive(k, _):
        x = pl.ds(4 * k, 4)
        ext[5, x], ext[6, x], ext[7, x] = derived(ext[0, x], ext[1, x], power)
        return _

    lax.fori_loop(0, 5, derive, 0)
    zs[...] = jnp.zeros_like(zs)

    def column(xq, _):
        rows = []
        for g in range(4):
            x = 4 * g + xq + 2
            rows.append(rate(
                lambda f: ext[f, x], lambda f: ext[f, x - 1], lambda f: ext[f, x + 1],
                lambda f: pltpu.roll(ext[f, x], 1, 0), lambda f: pltpu.roll(ext[f, x], 15, 0),
                lambda f: pltpu.roll(ext[f, x], 1, 1), lambda f: pltpu.roll(ext[f, x], 127, 1), True))
        for f in range(5):
            own = [rows[g][f] for g in range(4)]
            pack_z_edge(zs, f, xq, own, lane)
            first, last = own[0], own[3]

            @pl.when(xq == 0)
            def _first():
                for q in range(4):
                    out_ref[q, f] = pltpu.roll(first, 32 * (4 - q) % 128, 1)

            @pl.when(xq == 3)
            def _last():
                for q in range(4):
                    out_ref[q, f] = jnp.where(lane < 32, out_ref[q, f], pltpu.roll(last, 32 * (3 - q), 1))
        return _

    lax.fori_loop(0, 4, column, 0)
    for side in range(2):
        out = swap_blocks([zs[4 * side + g] for g in range(4)], 1, 32, lane)
        for q in range(4):
            out_ref[q, 5 + side] = out[q]


def edge_kernel(reg, s_ref, lo_ref, hi_ref, below_ref, above_ref, clo_ref, chi_ref, flag_ref, inner_ref,
                e0, e1, e2, e3, ext, yh, band, edge):
    me, t0, t7, s0, s7 = edges()
    sub, lane = iotas()
    power = 0.2 + 0.05 * reg[0].astype(jnp.float32)
    fill_ext(ext, s_ref, lo_ref, hi_ref, (0, 15), t0, t7)
    for x in (pl.ds(0, 3), pl.ds(17, 3)):
        ext[5, x], ext[6, x], ext[7, x] = derived(ext[0, x], ext[1, x], power)

    for side in range(2):
        ref = (below_ref, above_ref)[side]
        near, far = ((16, 0), (0, 16))[side]
        y, inward = ((0, 1), (15, 14))[side]
        wall = (s0, s7)[side]
        slip = slip_of(flag_ref[side])
        slip_lo = lo_ref[15, pl.ds(side, 1), :]
        slip_hi = hi_ref[15, pl.ds(side, 1), :]
        for f in range(5):
            def ghost(value, flag):
                return -value if f == 3 else value * flag if f in (2, 4) else value

            mine = s_ref[f, pl.ds(y, 16, stride=16), :]
            yh[f, side, pl.ds(0, 16), :] = jnp.where(wall, ghost(mine, slip), ref[f, pl.ds(near, 16), :])
            yh[f, side, pl.ds(16, 1), :] = jnp.where(
                wall, ghost(ext[f, 1, pl.ds(y, 1), :], slip_lo),
                jnp.where(t0, ref[f, pl.ds(near, 1), :], clo_ref[pl.ds(5 * side + f, 1), :]))
            yh[f, side, pl.ds(17, 1), :] = jnp.where(
                wall, ghost(ext[f, 18, pl.ds(y, 1), :], slip_hi),
                jnp.where(t7, ref[f, pl.ds(near + 15, 1), :], chi_ref[pl.ds(5 * side + f, 1), :]))
            yh[f, side, pl.ds(18, 6), :] = jnp.zeros((6, 128), jnp.float32)
            band[f, side, 0] = ref[f, pl.ds(far, 16), :]
            band[f, side, 1] = ref[f, pl.ds(near, 16), :]
            band[f, side, 2] = mine
            band[f, side, 3] = s_ref[f, pl.ds(inward, 16, stride=16), :]
        yh[5, side], yh[6, side], yh[7, side] = derived(yh[0, side], yh[1, side], power)
        band[5, side], band[6, side], band[7, side] = derived(band[0, side], band[1, side], power)

    def row(x, place):
        def below(f):
            return jnp.where(sub == 0, yh[f, 0, pl.ds(place, 1), :], pltpu.roll(ext[f, x], 1, 0))

        def above(f):
            return jnp.where(sub == 15, yh[f, 1, pl.ds(place, 1), :], pltpu.roll(ext[f, x], 15, 0))

        return rate(
            lambda f: ext[f, x], lambda f: ext[f, x - 1], lambda f: ext[f, x + 1], below, above,
            lambda f: pltpu.roll(ext[f, x], 1, 1), lambda f: pltpu.roll(ext[f, x], 127, 1), True)

    lower, upper = row(1, 16), row(18, 17)
    for f in range(5):
        for q in range(4):
            edge[q, f] = jnp.where(
                jnp.logical_or(lane < 32, lane >= 96), inner_ref[q, f],
                jnp.where(lane < 64, pltpu.roll(lower[f], (32 * (1 - q)) % 128, 1),
                          pltpu.roll(upper[f], (32 * (2 - q)) % 128, 1)))

    def band_rate(side, k):
        y = 0 if side == 0 else 15
        left = (lambda f: yh[f, side, pl.ds(16, 1), :]) if k == 1 else (lambda f: ext[f, 1, pl.ds(y, 1), :])
        right = (lambda f: yh[f, side, pl.ds(17, 1), :]) if k == 1 else (lambda f: ext[f, 18, pl.ds(y, 1), :])

        def lo(f):
            return jnp.where(sub == 0, left(f), pltpu.roll(band[f, side, k], 1, 0))

        def hi(f):
            return jnp.where(sub == 15, right(f), pltpu.roll(band[f, side, k], 15, 0))

        outer = (lambda f: band[f, side, 0]) if k == 1 else (lambda f: yh[f, side, pl.ds(0, 16), :])
        inner = lambda f: band[f, side, k + 1]
        before, after = (outer, inner) if side == 0 else (inner, outer)
        return rate(
            lambda f: band[f, side, k], before, after, lo, hi,
            lambda f: pltpu.roll(band[f, side, k], 1, 1), lambda f: pltpu.roll(band[f, side, k], 127, 1), False)

    rows = [band_rate(0, 2), band_rate(0, 1), band_rate(1, 1), band_rate(1, 2)]
    zero = jnp.zeros((16, 128), jnp.float32)
    beside = [[zero, zero] for q in range(4)]
    for f in range(5):
        out = swap_blocks(swap_blocks([r[f] for r in rows], 0, 4, sub), 1, 32, lane)
        for q in range(4):
            edge[q, 5 + f] = out[q]
            for xq in range(4):
                place = 4 * f + xq
                spot = jnp.logical_and(lane % 32 == place, sub % 4 == xq)
                for side, to, shift in ((0, (q + 1) % 4, (place + 97) % 128), (1, (q + 3) % 4, place)):
                    beside[to][side] = jnp.where(spot, pltpu.roll(out[q], shift, 1), beside[to][side])
    for q in range(4):
        for side in range(2):
            b = beside[q][side]
            low = b + pltpu.roll(b, 15, 0)
            low = low + pltpu.roll(low, 14, 0)
            high = b + pltpu.roll(b, 1, 0)
            high = high + pltpu.roll(high, 2, 0)
            edge[q, 10 + side] = jnp.where(sub == 0, low, jnp.where(sub == 15, high, inner_ref[q, 5 + side]))
    for r, e in enumerate((e0, e1, e2, e3)):
        e[...] = edge[me ^ r]


def start_tiles_kernel(lo_ref, hi_ref, below_ref, above_ref, wq_ref, wz_ref, _after, wxy_ref):
    me = lax.axis_index("node")
    sub, lane = iotas()
    for f in range(5):
        a = pltpu.roll(lo_ref[10 + f], (5 - me) % 4 * 32, 1)
        b = pltpu.roll(hi_ref[10 + f], (6 - me) % 4 * 32, 1)
        wxy_ref[f] = jnp.where(
            lane < 32, wq_ref[f * 4], jnp.where(lane < 64, a, jnp.where(lane < 96, b, wq_ref[f * 4 + 3])))
        wxy_ref[5 + f, pl.ds(4, 4), :] = below_ref[f, pl.ds(32, 4), :]
        wxy_ref[5 + f, pl.ds(8, 4), :] = above_ref[f, pl.ds(32, 4), :]
        for xq in range(4):
            wxy_ref[5 + f, pl.ds(xq, 1), :] = wq_ref[f * 4 + xq, pl.ds(0, 1), :]
            wxy_ref[5 + f, pl.ds(12 + xq, 1), :] = wq_ref[f * 4 + xq, pl.ds(15, 1), :]
    for side in range(2):
        wxy_ref[10 + side] = wz_ref[side]


def second_kernel(reg, a0, a1, a2, a3, b0, b1, b2, b3, wq_ref, wxy_ref, slipq_ref,
                  o0, o1, o2, o3, main, xh, yh, zh, rates, table):
    me, t0, t7, s0, s7 = edges()
    sub, lane = iotas()
    power = 0.2 + 0.05 * reg[0].astype(jnp.float32)
    slip = slipq_ref[...]
    at_lower = jnp.logical_and(jnp.logical_and(sub >= 4, sub < 8), s0)
    at_upper = jnp.logical_and(jnp.logical_and(sub >= 8, sub < 12), s7)
    arrived, edge = (a0, a1, a2, a3), (b0, b1, b2, b3)
    weights = relative_weights(me)
    for m in range(4):
        for r in range(4):
            table[m * 4 + r] = weights[m][r]

    def node(m, _):
        weight = [table[m * 4 + r] for r in range(4)]

        def mix(start, refs, k):
            out = start
            for r in range(4):
                out = out + weight[r] * refs[r][k]
            return out

        for f in range(5):
            xb = mix(wxy_ref[f], edge, f)
            yb = mix(wxy_ref[5 + f], edge, 5 + f)
            yh[f] = yb
            for xq in range(4):
                tile = mix(wq_ref[f * 4 + xq], arrived, f * 4 + xq)
                if xq == 0:
                    tile = jnp.where(lane < 32, xb, tile)
                if xq == 3:
                    tile = jnp.where(lane >= 96, xb, tile)
                tile = jnp.where(sub == 0, yh[f, pl.ds(xq, 1), :], tile)
                tile = jnp.where(sub == 15, yh[f, pl.ds(12 + xq, 1), :], tile)
                main[f, xq] = tile
            xh[f] = jnp.where(
                lane < 64, jnp.where(t0, main[f, 0], pltpu.roll(xb, 96, 1)),
                jnp.where(t7, main[f, 3], pltpu.roll(xb, 32, 1)))
            lower, upper = pltpu.roll(yb, 4, 0), pltpu.roll(yb, 12, 0)
            if f == 3:
                lower, upper = -lower, -upper
            if f in (2, 4):
                lower, upper = lower * slip, upper * slip
            yh[f] = jnp.where(at_lower, lower, jnp.where(at_upper, upper, yb))
        for xq in range(4):
            main[5, xq], main[6, xq], main[7, xq] = derived(main[0, xq], main[1, xq], power)
        xh[5], xh[6], xh[7] = derived(xh[0], xh[1], power)
        yh[5], yh[6], yh[7] = derived(yh[0], yh[1], power)
        for side in range(2):
            z = mix(wxy_ref[10 + side], edge, 10 + side)
            zh[0, side] = z
            q, eta, _s = derived(z, pltpu.roll(z, 124, 1), power)
            zh[1, side], zh[2, side] = q, eta
        for xq in range(4):
            def left(f):
                if xq > 0:
                    return main[f, xq - 1]
                return jnp.where(lane < 32, xh[f], pltpu.roll(main[f, 3], 32, 1))

            def right(f):
                if xq < 3:
                    return main[f, xq + 1]
                return jnp.where(lane >= 96, xh[f], pltpu.roll(main[f, 0], 96, 1))

            def below(f):
                return jnp.where(sub == 0, yh[f, pl.ds(4 + xq, 1), :], pltpu.roll(main[f, xq], 1, 0))

            def above(f):
                return jnp.where(sub == 15, yh[f, pl.ds(8 + xq, 1), :], pltpu.roll(main[f, xq], 15, 0))

            def spot(f):
                return (0, 4 * f + xq) if f < 5 else (f - 4, xq)

            def before(f):
                k, i = spot(f)
                return jnp.where(lane % 32 == 0, pltpu.roll(zh[k, 0], (128 - i) % 128, 1), pltpu.roll(main[f, xq], 1, 1))

            def after(f):
                k, i = spot(f)
                return jnp.where(lane % 32 == 31, pltpu.roll(zh[k, 1], 31 - i, 1), pltpu.roll(main[f, xq], 127, 1))

            out = rate(lambda f: main[f, xq], left, right, below, above, before, after, True)
            for f in range(5):
                rates[m, f * 4 + xq] = out[f]
        return _

    lax.fori_loop(0, 4, node, 0)

    def combine(k, _):
        have = [rates[r, k] for r in range(4)]
        for m, o in enumerate((o0, o1, o2, o3)):
            out = wq_ref[k]
            for r in range(4):
                out = out + weights[m][r] * have[r]
            o[k] = out
        return _

    lax.fori_loop(0, MAIN, combine, 0)


def last_kernel(r0, r1, r2, r3, out_hbm, quarter, out, sems):
    me = lax.axis_index("node")
    _, lane = iotas()
    copies = []
    for f in range(5):
        for r, ref in enumerate((r0, r1, r2, r3)):
            quarter[me ^ r, pl.ds(4 * f, 4)] = ref[pl.ds(4 * f, 4)]
        for xq in range(4):
            tiles = swap_blocks([quarter[q, 4 * f + xq] for q in range(4)], 1, 32, lane)
            for g in range(4):
                out[f, 4 * g + xq] = tiles[g]
        copies.append(pltpu.make_async_copy(out.at[f], out_hbm.at[f], sems.at[f]))
        copies[f].start()
    for copy in copies:
        copy.wait()


def tiles_of(n):
    return jax.ShapeDtypeStruct((n, 16, 128), jnp.float32)


def shards(start_state, iterate, wall_flags, reg_index):
    state = iterate[0]
    flat = state.reshape(5, 256, 128)
    size = lax.axis_size("tile")
    ring_up = [(i, (i + 1) % size) for i in range(size)]
    ring_down = [(j, i) for i, j in ring_up]
    params = pltpu.CompilerParams(vmem_limit_bytes=32 * 1024 * 1024)
    scratch = lambda *shape: pltpu.VMEM(shape + (16, 128), jnp.float32)

    def call(kernel, ins, outs, scratch_shapes=(), place=VMEM):
        return pl.pallas_call(
            kernel, out_shape=outs, in_specs=ins, out_specs=[place] * len(outs),
            scratch_shapes=scratch_shapes, compiler_params=params)

    def exchange(tiles):
        out = [tiles[0]] + [None] * 3
        for r in (2, 3, 1):
            out[r] = lax.ppermute(tiles[r], "node", [(i, i ^ r) for i in range(4)])
        return out

    far = pltpu.with_memory_space_constraint
    slab_shape = jax.ShapeDtypeStruct((5, 40, 128), jnp.float32)
    slab_up, slab_down = call(
        slab_kernel, [HBM] * 2, [slab_shape] * 2, [scratch(2, 5), pltpu.SemaphoreType.DMA((6,))])(
        far(state, pltpu.HBM), far(start_state, pltpu.HBM))
    from_above = lax.ppermute(slab_down, "slab", ring_down)
    from_below = lax.ppermute(slab_up, "slab", ring_up)

    tile_up, tile_down = call(tile_kernel, [VMEM] * 3 + [ANY], [tiles_of(16)] * 2)(
        state, start_state, wall_flags, slab_up)
    from_lower = lax.ppermute(tile_up, "tile", ring_up)
    from_upper = lax.ppermute(tile_down, "tile", ring_down)

    rates = call(first_kernel, [SMEM, VMEM, ANY], [tiles_of(MAIN)] * 4, [scratch(3, 16), scratch(4, MAIN)])(
        reg_index, state, tile_up)
    arrived = exchange(rates)

    wq, wz, slipq = call(
        start_kernel, [VMEM, VMEM, ANY], [tiles_of(MAIN), tiles_of(2), jax.ShapeDtypeStruct((16, 128), jnp.float32)],
        [scratch(8)])(start_state, wall_flags, rates[1])

    inner, = call(
        inner_kernel, [SMEM] + [VMEM] * 3, [jax.ShapeDtypeStruct((4, 7, 16, 128), jnp.float32)],
        [scratch(8, 20), scratch(8)])(reg_index, flat, from_lower, from_upper)

    corner_shape = jax.ShapeDtypeStruct((16, 128), jnp.float32)
    corner_up, corner_down = call(corner_kernel, [VMEM] * 2, [corner_shape] * 2)(from_below, from_above)
    corner_lower = lax.ppermute(corner_up, "tile", ring_up)
    corner_upper = lax.ppermute(corner_down, "tile", ring_down)

    edge = call(
        edge_kernel, [SMEM] + [VMEM] * 9, [tiles_of(EDGE)] * 4,
        [scratch(8, 20), pltpu.VMEM((8, 2, 24, 128), jnp.float32), scratch(8, 2, 4), scratch(4, EDGE)])(
        reg_index, flat, from_lower, from_upper, from_below, from_above, corner_lower, corner_upper, wall_flags, inner)
    wxy, = call(start_tiles_kernel, [VMEM] * 6 + [ANY], [tiles_of(EDGE)])(
        from_lower, from_upper, from_below, from_above, wq, wz, edge[1])
    edge = exchange(edge)

    outs = call(
        second_kernel, [SMEM] + [VMEM] * 11, [tiles_of(MAIN)] * 4,
        [scratch(8, 4), scratch(8), scratch(8), scratch(3, 2), scratch(4, MAIN), pltpu.SMEM((16,), jnp.float32)])(
        reg_index, *arrived, *edge, wq, wxy, slipq)
    back = exchange(outs)

    result, = call(
        last_kernel, [VMEM] * 4, [jax.ShapeDtypeStruct((5, 16, 16, 128), jnp.float32)],
        [scratch(4, MAIN), scratch(5, 16), pltpu.SemaphoreType.DMA((5,))], HBM)(*back)
    return result[None]


def solution(mesh):
    return jax.shard_map(
        shards,
        mesh=mesh,
        in_specs=(
            P(None, "tile", "slab", None),
            P("node", None, "tile", "slab", None),
            P(None, "tile", None),
            P(),
        ),
        out_specs=P("node", None, "tile", "slab", None),
        check_vma=False,
    )
```

```python
import jax
import jax.numpy as jnp
import numpy as np
from jax import lax
from jax.experimental import pallas as pl
from jax.experimental.pallas import tpu as pltpu
from jax.sharding import PartitionSpec as P

STEP = 0.2
MAIN = 18
EDGE = 12
VMEM = pl.BlockSpec(memory_space=pltpu.VMEM)
SMEM = pl.BlockSpec(memory_space=pltpu.SMEM)
ANY = pl.BlockSpec(memory_space=pl.ANY)
HBM = pl.BlockSpec(memory_space=pltpu.HBM)


def quadrature_table():
    points = [0.25, 0.5, 0.75, 1.0]
    table = np.zeros((4, 4))
    for column in range(4):
        coeffs = [1.0]
        divisor = 1.0
        for other in range(4):
            if other != column:
                other_point = points[other]
                widened = [0.0] * (len(coeffs) + 1)
                for power, value in enumerate(coeffs):
                    widened[power + 1] += value
                    widened[power] -= other_point * value
                coeffs = widened
                divisor *= points[column] - other_point
        for line_index in range(4):
            position = points[line_index]
            total = 0.0
            for power, value in enumerate(coeffs):
                total += value * position ** (power + 1) / (power + 1)
            table[line_index, column] = total / divisor
    return table


def relative_weights(me):
    table = np.asarray(quadrature_table(), np.float32) * np.float32(STEP)

    def entry(a, b):
        value = jnp.float32(table[3 ^ a, 3 ^ b])
        for node in range(3):
            value = jnp.where(me == node, jnp.float32(table[node ^ a, node ^ b]), value)
        return value

    return [[entry(a, b) for b in range(4)] for a in range(4)]


def iotas():
    sub = lax.broadcasted_iota(jnp.int32, (16, 128), 0)
    lane = lax.broadcasted_iota(jnp.int32, (16, 128), 1)
    return sub, lane


def derived(c, g, power):
    r = jnp.exp(power * jnp.log(g * g + 0.25))
    q = c * r
    eta = (0.08 + 0.2 * c + 0.496 * (c * c)) * r
    return q, eta, 0.5 * c * q


def rate(cen, lm, lp, sm, sp, zm, zp, lead_x):
    def diffs(f):
        dl = lp(f) - lm(f)
        ds = sp(f) - sm(f)
        return (dl, ds) if lead_x else (ds, dl)

    def grads(f):
        lo, hi, a, b, n, m = lm(f), lp(f), sm(f), sp(f), zm(f), zp(f)
        x, y = (hi - lo, b - a) if lead_x else (b - a, hi - lo)
        return x, y, m - n, (lo + hi) + (a + b) + (n + m)

    c, g, u, v, w, eta = cen(0), cen(1), cen(2), cen(3), cen(4), cen(6)
    hu, hv, hw = 0.5 * u, 0.5 * v, 0.5 * w
    qx, qy, qz, qsum = grads(5)
    cx, cy, cz, _ = grads(0)
    dc = 0.3 * c * (qsum - 6.0 * cen(5)) + (0.075 * qx - hu) * cx + (0.075 * qy - hv) * cy + (0.075 * qz - hw) * cz
    ex, ey, ez, _ = grads(6)
    ax, ay, az = 0.25 * ex - hu, 0.25 * ey - hv, 0.25 * ez - hw
    ux, uy, uz, usum = grads(2)
    du = eta * (usum - 6.0 * u) + ax * ux + ay * uy + az * uz + 0.5
    vx, vy, vz, vsum = grads(3)
    dv = eta * (vsum - 6.0 * v) + ax * vx + ay * vy + az * vz - 0.5 * diffs(7)[1]
    wx, wy, wz, wsum = grads(4)
    dw = eta * (wsum - 6.0 * w) + ax * wx + ay * wy + az * wz
    strain = uy * uy + wy * wy + vx * vx + vz * vz
    dg = jnp.sqrt(strain + 1.0) - 2.0 * g
    return dc, dg, du, dv, dw


def swap_blocks(tiles, axis, block, index):
    size = 4 * block
    low = index < 2 * block
    even = (index // block) % 2 == 0
    roll = lambda t, k: pltpu.roll(t, k, axis)
    a0, a1, a2, a3 = tiles
    lo0 = jnp.where(low, a0, roll(a2, 2 * block))
    hi0 = jnp.where(low, roll(a0, 2 * block), a2)
    lo1 = jnp.where(low, a1, roll(a3, 2 * block))
    hi1 = jnp.where(low, roll(a1, 2 * block), a3)
    out = []
    for p, q in ((lo0, lo1), (hi0, hi1)):
        out.append(jnp.where(even, p, roll(q, block)))
        out.append(jnp.where(even, roll(p, size - block), q))
    return out


def edges():
    me = lax.axis_index("node")
    t, s = lax.axis_index("tile"), lax.axis_index("slab")
    return me, t == 0, t == lax.axis_size("tile") - 1, s == 0, s == lax.axis_size("slab") - 1


def pick(tiles, me):
    out = tiles[3]
    for q in range(3):
        out = jnp.where(me == q, tiles[q], out)
    return out


def reads(*refs):
    return [lambda *at, ref=ref: ref[at] for ref in refs]


def pack_z_edge(row, sides, lane):
    left = right = jnp.zeros((16, 128), jnp.float32)
    for xq in range(4):
        for f in range(5):
            place = 4 * f + xq
            spot = lane % 32 == place
            tile = row(f, xq)
            left = jnp.where(spot, pltpu.roll(tile, place + 1, 1), left)
            right = jnp.where(spot, pltpu.roll(tile, (place + 96) % 128, 1), right)
    return left, right


def slip_of(flags):
    return 1.0 - 2.0 * flags.astype(jnp.float32)


def tile_kernel(s_ref, w_ref, slip_ref, _after, up_ref, down_ref):
    for ref, up in ((up_ref, True), (down_ref, False)):
        for f in range(5):
            ref[f] = ((s_ref[f, 14]) if up else s_ref[f, 0])
            ref[5 + f] = ((s_ref[f, 15]) if up else s_ref[f, 1])
            ref[10 + f] = ((w_ref[f, 15]) if up else w_ref[f, 0])
        ref[15] = jnp.zeros((16, 128), jnp.float32)
        for side in range(2):
            ref[15, pl.ds(side, 1), :] = ((slip_ref[side, pl.ds(15, 1), :]) if up else slip_ref[side, pl.ds(0, 1), :])


def first_kernel(power_ref, s_ref, m0, m1, m2, m3, rates, der, packed):
    me = lax.axis_index("node")
    sub, lane = iotas()
    power = power_ref[0:1, :]

    def derive(k, _):
        x = pl.ds(4 * k, 4)
        der[0, x], der[1, x], der[2, x] = derived(s_ref[0, x], s_ref[1, x], power)
        return _

    lax.fori_loop(0, 4, derive, 0)

    def column(xq, _):
        rows = []
        for g in range(4):
            x = 4 * g + xq
            lo = jnp.maximum(x - 1, 0)
            hi = jnp.minimum(x + 1, 15)
            at = lambda f, r: s_ref[f, r] if f < 5 else der[f - 5, r]
            rows.append(rate(
                lambda f: at(f, x), lambda f: at(f, lo), lambda f: at(f, hi),
                lambda f: pltpu.roll(at(f, x), 1, 0), lambda f: pltpu.roll(at(f, x), 15, 0),
                lambda f: pltpu.roll(at(f, x), 1, 1), lambda f: pltpu.roll(at(f, x), 127, 1), True))
        for f in range(5):
            for g in range(4):
                rates[f, 4 * g + xq] = rows[g][f]
            out = swap_blocks([rows[g][f] for g in range(4)], 1, 32, lane)
            for q in range(4):
                packed[q, f * 4 + xq] = out[q]
        return _

    lax.fori_loop(0, 4, column, 0)
    for r, m in enumerate((m0, m1, m2, m3)):
        q = me ^ r
        for f in range(5):
            for xq in (1, 2):
                m[2 * f + xq - 1] = packed[q, f * 4 + xq]
        for p in range(2):
            a0, a3 = packed[q, 8 * p], packed[q, 8 * p + 3]
            b0, b3 = packed[q, 8 * p + 4], packed[q, 8 * p + 7]
            m[10 + 3 * p] = jnp.where(lane < 32, b3, a0)
            m[11 + 3 * p] = jnp.where(lane >= 96, b0, a3)
            m[12 + 3 * p] = jnp.where(
                lane < 32, pltpu.roll(b3, 96, 1), jnp.where(lane < 96, b0, pltpu.roll(b3, 32, 1)))
        m[16] = packed[q, 16]
        m[17] = packed[q, 19]


def start_kernel(w_ref, slip_ref, _after, wq_ref, wz_ref, slipq_ref):
    me = lax.axis_index("node")
    sub, lane = iotas()
    for xq in range(4):
        for f in range(5):
            own = [w_ref[f, 4 * g + xq] for g in range(4)]
            wq_ref[f * 4 + xq] = pick(swap_blocks(own, 1, 32, lane), me)
    packs = [pack_z_edge(lambda f, xq: w_ref[f, 4 * g + xq], 2, lane) for g in range(4)]
    for side in range(2):
        wz_ref[side] = pick(swap_blocks([packs[g][side] for g in range(4)], 1, 32, lane), me)
    slipq_ref[...] = pack_y_edge(slip_ref[0], slip_ref[1], me, sub, lane)


def pack_y_edge(lower, upper, me, sub, lane):
    zero = jnp.zeros((16, 128), jnp.float32)
    tiles = swap_blocks([zero, lower, upper, zero], 0, 4, sub)
    return pick(swap_blocks(tiles, 1, 32, lane), me)


def slab_kernel(reg_hbm, flag_hbm, s_hbm, w_hbm, up_ref, down_ref, slip_ref, power_ref, rows, flags, reg, sems):
    me = lax.axis_index("node")
    sub, lane = iotas()

    def run(up_ref, down_ref):
        copies = []
        for k, (ref, ys) in enumerate(((up_ref, (14, 15)), (down_ref, (0, 1)))):
            for r in range(2):
                copies.append(pltpu.make_async_copy(
                    s_hbm.at[:, :, ys[r], :], ref.at[:, pl.ds(16 * r, 16), :], sems.at[2 * k + r]))
            copies.append(pltpu.make_async_copy(w_hbm.at[:, :, (15, 0)[k], :], rows.at[k], sems.at[4 + k]))
        copies.append(pltpu.make_async_copy(flag_hbm, flags, sems.at[6]))
        copies.append(pltpu.make_async_copy(reg_hbm, reg, sems.at[7]))
        for copy in copies:
            copy.start()
        copies[2].wait()
        copies[5].wait()
        for f in range(5):
            start = pack_y_edge(rows[1, f], rows[0, f], me, sub, lane)
            for ref, place in ((up_ref, 8), (down_ref, 4)):
                ref[f, pl.ds(32, 4), :] = start[place:place + 4]
                ref[f, pl.ds(36, 4), :] = jnp.zeros((4, 128), jnp.float32)
        for k in (0, 1, 3, 4, 6, 7):
            copies[k].wait()

    run(up_ref, down_ref)

    slip_ref[...] = slip_of(flags[...])
    power_ref[...] = jnp.full((8, 128), 0.2 + 0.05 * reg[0].astype(jnp.float32))


def corner_kernel(slow_ref, shigh_ref, up_ref, down_ref):
    below, above = reads(slow_ref, shigh_ref)
    for ref, up in ((up_ref, True), (down_ref, False)):
        ref[pl.ds(10, 6), :] = jnp.zeros((6, 128), jnp.float32)
        for f in range(5):
            ref[pl.ds(f, 1), :] = ((below(f, pl.ds(31, 1))) if up else below(f, pl.ds(16, 1)))
            ref[pl.ds(5 + f, 1), :] = ((above(f, pl.ds(15, 1))) if up else above(f, pl.ds(0, 1)))


def fill_ext(ext, s_ref, tlow_ref, thigh_ref, t0, t7):
    lo, hi = reads(tlow_ref, thigh_ref)
    for f in range(5):
        first, last = s_ref[f, pl.ds(0, 16), :], s_ref[f, pl.ds(240, 16), :]
        ext[f, 0] = lo(f)
        ext[f, 1] = jnp.where(t0, first, lo(5 + f))
        ext[f, 2] = first
        ext[f, 3] = s_ref[f, pl.ds(16, 16), :]
        ext[f, 4] = s_ref[f, pl.ds(224, 16), :]
        ext[f, 5] = last
        ext[f, 6] = jnp.where(t7, last, hi(f))
        ext[f, 7] = hi(5 + f)


def inner_kernel(power_ref, s_ref, tlow_ref, thigh_ref, rates, out_ref, ext):
    _, t0, t7, _, _ = edges()
    sub, lane = iotas()
    fill_ext(ext, s_ref, tlow_ref, thigh_ref, t0, t7)
    ext[5], ext[6], ext[7] = derived(ext[0], ext[1], power_ref[0:1, :])

    def row(x):
        return rate(
            lambda f: ext[f, x], lambda f: ext[f, x - 1], lambda f: ext[f, x + 1],
            lambda f: pltpu.roll(ext[f, x], 1, 0), lambda f: pltpu.roll(ext[f, x], 15, 0),
            lambda f: pltpu.roll(ext[f, x], 1, 1), lambda f: pltpu.roll(ext[f, x], 127, 1), True)

    first, last = row(2), row(5)
    for f in range(5):
        for q in range(4):
            out_ref[q, f] = jnp.where(
                lane < 32, pltpu.roll(first[f], 32 * (4 - q) % 128, 1), pltpu.roll(last[f], 32 * (3 - q), 1))

    def at(g):
        def tile(f, xq):
            return first[f] if g + xq == 0 else last[f] if g + xq == 6 else rates[f, 4 * g + xq]

        return tile

    packs = [pack_z_edge(at(g), 2, lane) for g in range(4)]
    for side in range(2):
        out = swap_blocks([packs[g][side] for g in range(4)], 1, 32, lane)
        for q in range(4):
            out_ref[q, 5 + side] = out[q]


def edge_kernel(power_ref, s_ref, tlow_ref, thigh_ref, slow_ref, shigh_ref, clow_ref, chigh_ref, slip_ref,
                inner_ref, e0, e1, e2, e3, ext, yh, band, edge):
    me, t0, t7, s0, s7 = edges()
    sub, lane = iotas()
    power = power_ref[0:1, :]
    lo, hi = reads(tlow_ref, thigh_ref)
    corner_lo, corner_hi = reads(clow_ref, chigh_ref)
    below_row, above_row = reads(slow_ref, shigh_ref)
    fill_ext(ext, s_ref, tlow_ref, thigh_ref, t0, t7)
    ext[5], ext[6], ext[7] = derived(ext[0], ext[1], power)

    for side in range(2):
        ref = (below_row, above_row)[side]
        near, far = ((16, 0), (0, 16))[side]
        y, inward = ((0, 1), (15, 14))[side]
        wall = (s0, s7)[side]
        slip = slip_ref[side]
        slip_lo = lo(15, pl.ds(side, 1))
        slip_hi = hi(15, pl.ds(side, 1))
        for f in range(5):
            def ghost(value, flag):
                return -value if f == 3 else value * flag if f in (2, 4) else value

            mine = s_ref[f, pl.ds(y, 16, stride=16), :]
            yh[f, side, pl.ds(0, 16), :] = jnp.where(wall, ghost(mine, slip), ref(f, pl.ds(near, 16)))
            yh[f, side, pl.ds(16, 1), :] = jnp.where(
                wall, ghost(ext[f, 1, pl.ds(y, 1), :], slip_lo),
                jnp.where(t0, ref(f, pl.ds(near, 1)), corner_lo(pl.ds(5 * side + f, 1))))
            yh[f, side, pl.ds(17, 1), :] = jnp.where(
                wall, ghost(ext[f, 6, pl.ds(y, 1), :], slip_hi),
                jnp.where(t7, ref(f, pl.ds(near + 15, 1)), corner_hi(pl.ds(5 * side + f, 1))))
            yh[f, side, pl.ds(18, 6), :] = jnp.zeros((6, 128), jnp.float32)
            band[f, side, 0] = ref(f, pl.ds(far, 16))
            band[f, side, 1] = ref(f, pl.ds(near, 16))
            band[f, side, 2] = mine
            band[f, side, 3] = s_ref[f, pl.ds(inward, 16, stride=16), :]
        yh[5, side], yh[6, side], yh[7, side] = derived(yh[0, side], yh[1, side], power)
        band[5, side], band[6, side], band[7, side] = derived(band[0, side], band[1, side], power)

    def row(x, place):
        def below(f):
            return jnp.where(sub == 0, yh[f, 0, pl.ds(place, 1), :], pltpu.roll(ext[f, x], 1, 0))

        def above(f):
            return jnp.where(sub == 15, yh[f, 1, pl.ds(place, 1), :], pltpu.roll(ext[f, x], 15, 0))

        return rate(
            lambda f: ext[f, x], lambda f: ext[f, x - 1], lambda f: ext[f, x + 1], below, above,
            lambda f: pltpu.roll(ext[f, x], 1, 1), lambda f: pltpu.roll(ext[f, x], 127, 1), True)

    lower, upper = row(1, 16), row(6, 17)
    for f in range(5):
        for q in range(4):
            edge[q, f] = jnp.where(
                jnp.logical_or(lane < 32, lane >= 96), inner_ref[q, f],
                jnp.where(lane < 64, pltpu.roll(lower[f], (32 * (1 - q)) % 128, 1),
                          pltpu.roll(upper[f], (32 * (2 - q)) % 128, 1)))

    def band_rate(side, k):
        y = 0 if side == 0 else 15
        left = (lambda f: yh[f, side, pl.ds(16, 1), :]) if k == 1 else (lambda f: ext[f, 1, pl.ds(y, 1), :])
        right = (lambda f: yh[f, side, pl.ds(17, 1), :]) if k == 1 else (lambda f: ext[f, 6, pl.ds(y, 1), :])

        def before_x(f):
            return jnp.where(sub == 0, left(f), pltpu.roll(band[f, side, k], 1, 0))

        def after_x(f):
            return jnp.where(sub == 15, right(f), pltpu.roll(band[f, side, k], 15, 0))

        outer = (lambda f: band[f, side, 0]) if k == 1 else (lambda f: yh[f, side, pl.ds(0, 16), :])
        inner = lambda f: band[f, side, k + 1]
        before, after = (outer, inner) if side == 0 else (inner, outer)
        return rate(
            lambda f: band[f, side, k], before, after, before_x, after_x,
            lambda f: pltpu.roll(band[f, side, k], 1, 1), lambda f: pltpu.roll(band[f, side, k], 127, 1), False)

    rows = [band_rate(0, 2), band_rate(0, 1), band_rate(1, 1), band_rate(1, 2)]
    zero = jnp.zeros((16, 128), jnp.float32)
    beside = [[zero, zero] for q in range(4)]
    for f in range(5):
        out = swap_blocks(swap_blocks([r[f] for r in rows], 0, 4, sub), 1, 32, lane)
        for q in range(4):
            edge[q, 5 + f] = out[q]
            for xq in range(4):
                place = 4 * f + xq
                spot = jnp.logical_and(lane % 32 == place, sub % 4 == xq)
                for side, to, shift in ((0, (q + 1) % 4, (place + 97) % 128), (1, (q + 3) % 4, place)):
                    beside[to][side] = jnp.where(spot, pltpu.roll(out[q], shift, 1), beside[to][side])
    for q in range(4):
        for side in range(2):
            b = beside[q][side]
            low = b + pltpu.roll(b, 15, 0)
            low = low + pltpu.roll(low, 14, 0)
            high = b + pltpu.roll(b, 1, 0)
            high = high + pltpu.roll(high, 2, 0)
            edge[q, 10 + side] = jnp.where(sub == 0, low, jnp.where(sub == 15, high, inner_ref[q, 5 + side]))
    for r, e in enumerate((e0, e1, e2, e3)):
        e[...] = edge[me ^ r]


def start_tiles_kernel(tlow_ref, thigh_ref, slow_ref, shigh_ref, wq_ref, wz_ref, _after, wxy_ref):
    me = lax.axis_index("node")
    sub, lane = iotas()
    lo, hi = reads(tlow_ref, thigh_ref)
    below, above = reads(slow_ref, shigh_ref)
    for f in range(5):
        a = pltpu.roll(lo(10 + f), (5 - me) % 4 * 32, 1)
        b = pltpu.roll(hi(10 + f), (6 - me) % 4 * 32, 1)
        wxy_ref[f] = jnp.where(
            lane < 32, wq_ref[f * 4], jnp.where(lane < 64, a, jnp.where(lane < 96, b, wq_ref[f * 4 + 3])))
        wxy_ref[5 + f, pl.ds(4, 4), :] = below(f, pl.ds(32, 4))
        wxy_ref[5 + f, pl.ds(8, 4), :] = above(f, pl.ds(32, 4))
        for xq in range(4):
            wxy_ref[5 + f, pl.ds(xq, 1), :] = wq_ref[f * 4 + xq, pl.ds(0, 1), :]
            wxy_ref[5 + f, pl.ds(12 + xq, 1), :] = wq_ref[f * 4 + xq, pl.ds(15, 1), :]
    for side in range(2):
        wxy_ref[10 + side] = wz_ref[side]


def second_kernel(a2, a3, power_ref, a0, a1, b0, b1, b2, b3, wq_ref, wxy_ref, slipq_ref,
                  o0, o1, o2, o3, main, xh, yh, zh, rates, table):
    me, t0, t7, s0, s7 = edges()
    sub, lane = iotas()
    power = power_ref[0:1, :]
    slip = slipq_ref[...]
    at_lower = jnp.logical_and(jnp.logical_and(sub >= 4, sub < 8), s0)
    at_upper = jnp.logical_and(jnp.logical_and(sub >= 8, sub < 12), s7)
    arrived = ((a0, 0), (a1, 0), (a2, 0), (a3, 0))
    edge = ((b0, 0), (b1, 0), (b2, 0), (b3, 0))
    weights = relative_weights(me)
    for m in range(4):
        for r in range(4):
            table[m * 4 + r] = weights[m][r]

    def node(m, _):
        weight = [table[m * 4 + r] for r in range(4)]

        def mix(refs, k):
            out = None
            for r, (ref, base) in enumerate(refs):
                term = weight[r] * ref[base + k]
                out = term if out is None else out + term
            return out

        outer = {}
        for p in range(2):
            a0, a3, b = (mix(arrived, 10 + 3 * p + k) for k in range(3))
            outer[2 * p] = a0, a3
            outer[2 * p + 1] = jnp.where(lane < 96, b, a3), jnp.where(
                lane < 32, a0, jnp.where(lane < 64, pltpu.roll(b, 32, 1), pltpu.roll(b, 96, 1)))
        outer[4] = mix(arrived, 16), mix(arrived, 17)

        for f in range(5):
            xb = wxy_ref[f] + mix(edge, f)
            yb = wxy_ref[5 + f] + mix(edge, 5 + f)
            yh[f] = yb
            for xq in range(4):
                tile = wq_ref[f * 4 + xq] + (mix(arrived, 2 * f + xq - 1) if xq in (1, 2) else outer[f][xq // 3])
                if xq == 0:
                    tile = jnp.where(lane < 32, xb, tile)
                if xq == 3:
                    tile = jnp.where(lane >= 96, xb, tile)
                tile = jnp.where(sub == 0, yh[f, pl.ds(xq, 1), :], tile)
                tile = jnp.where(sub == 15, yh[f, pl.ds(12 + xq, 1), :], tile)
                main[f, xq] = tile
            xh[f] = jnp.where(
                lane < 64, jnp.where(t0, main[f, 0], pltpu.roll(xb, 96, 1)),
                jnp.where(t7, main[f, 3], pltpu.roll(xb, 32, 1)))
            lower, upper = pltpu.roll(yb, 4, 0), pltpu.roll(yb, 12, 0)
            if f == 3:
                lower, upper = -lower, -upper
            if f in (2, 4):
                lower, upper = lower * slip, upper * slip
            yh[f] = jnp.where(at_lower, lower, jnp.where(at_upper, upper, yb))
        for xq in range(4):
            main[5, xq], main[6, xq], main[7, xq] = derived(main[0, xq], main[1, xq], power)
        xh[5], xh[6], xh[7] = derived(xh[0], xh[1], power)
        yh[5], yh[6], yh[7] = derived(yh[0], yh[1], power)
        for side in range(2):
            z = wxy_ref[10 + side] + mix(edge, 10 + side)
            zh[0, side] = z
            q, eta, _s = derived(z, pltpu.roll(z, 124, 1), power)
            zh[1, side], zh[2, side] = q, eta
        for xq in range(4):
            def left(f):
                if xq > 0:
                    return main[f, xq - 1]
                return jnp.where(lane < 32, xh[f], pltpu.roll(main[f, 3], 32, 1))

            def right(f):
                if xq < 3:
                    return main[f, xq + 1]
                return jnp.where(lane >= 96, xh[f], pltpu.roll(main[f, 0], 96, 1))

            def below(f):
                return jnp.where(sub == 0, yh[f, pl.ds(4 + xq, 1), :], pltpu.roll(main[f, xq], 1, 0))

            def above(f):
                return jnp.where(sub == 15, yh[f, pl.ds(8 + xq, 1), :], pltpu.roll(main[f, xq], 15, 0))

            def spot(f):
                return (0, 4 * f + xq) if f < 5 else (f - 4, xq)

            def before(f):
                k, i = spot(f)
                return jnp.where(lane % 32 == 0, pltpu.roll(zh[k, 0], (128 - i) % 128, 1), pltpu.roll(main[f, xq], 1, 1))

            def after(f):
                k, i = spot(f)
                return jnp.where(lane % 32 == 31, pltpu.roll(zh[k, 1], 31 - i, 1), pltpu.roll(main[f, xq], 127, 1))

            out = rate(lambda f: main[f, xq], left, right, below, above, before, after, True)
            for f in range(5):
                rates[m, f * 4 + xq] = out[f]
        return _

    lax.fori_loop(0, 4, node, 0)

    def combine(k, _):
        have = [rates[r, k] for r in range(4)]
        for m, o in enumerate((o0, o1, o2, o3)):
            out = wq_ref[k]
            for r in range(4):
                out = out + weights[m][r] * have[r]
            o[k] = out
        return _

    lax.fori_loop(0, 20, combine, 0)


def last_kernel(r0, r1, r2, r3, out_hbm, quarter, out, sems):
    me = lax.axis_index("node")
    _, lane = iotas()
    copies = []
    for f in range(5):
        for r, ref in enumerate((r0, r1, r2, r3)):
            quarter[me ^ r, pl.ds(4 * f, 4)] = ref[pl.ds(4 * f, 4)]
        for xq in range(4):
            tiles = swap_blocks([quarter[q, 4 * f + xq] for q in range(4)], 1, 32, lane)
            for g in range(4):
                out[f, 4 * g + xq] = tiles[g]
        copies.append(pltpu.make_async_copy(out.at[f], out_hbm.at[f], sems.at[f]))
        copies[f].start()
    for copy in copies:
        copy.wait()


def tiles_of(n):
    return jax.ShapeDtypeStruct((n, 16, 128), jnp.float32)


def shards(start_state, iterate, wall_flags, reg_index):
    state = iterate[0]
    flat = state.reshape(5, 256, 128)
    params = pltpu.CompilerParams(vmem_limit_bytes=32 * 1024 * 1024)
    scratch = lambda *shape: pltpu.VMEM(shape + (16, 128), jnp.float32)
    shape = lambda *dims: jax.ShapeDtypeStruct(dims, jnp.float32)
    dma = lambda n: pltpu.SemaphoreType.DMA((n,))

    def call(kernel, ins, outs, scratch_shapes=(), place=VMEM):
        return pl.pallas_call(
            kernel, out_shape=outs, in_specs=ins, out_specs=[place] * len(outs),
            scratch_shapes=scratch_shapes, compiler_params=params,
            cost_estimate=pl.CostEstimate(flops=1, bytes_accessed=1, transcendentals=0))

    def neighbours(up, down, axis):
        size = lax.axis_size(axis)
        from_lower = lax.ppermute(up, axis, [(i, (i + 1) % size) for i in range(size)])
        from_upper = lax.ppermute(down, axis, [((i + 1) % size, i) for i in range(size)])
        return from_lower, from_upper

    def send(tiles, r):
        return lax.ppermute(tiles, "node", [(i, i ^ r) for i in range(4)])

    far = lambda x: pltpu.with_memory_space_constraint(x, pltpu.HBM)
    slab_near, slab_next, slip, power = call(
        slab_kernel, [ANY] + [HBM] * 3, [shape(5, 40, 128)] * 2 + [shape(2, 16, 128), shape(8, 128)],
        [scratch(2, 5), pltpu.VMEM((2, 16, 128), jnp.int32), pltpu.SMEM((1,), jnp.int32), dma(8)])(
        reg_index, far(wall_flags), far(state), far(start_state))
    slab = neighbours(slab_near, slab_next, "slab")

    m0, m1, m2, m3, rates = call(
        first_kernel, [VMEM, VMEM], [tiles_of(MAIN)] * 4 + [shape(5, 16, 16, 128)],
        [scratch(3, 16), scratch(4, 20)])(power, state)
    a2, a3, a1 = send(m2, 2), send(m3, 3), send(m1, 1)

    tile = neighbours(*call(tile_kernel, [VMEM] * 3 + [ANY], [tiles_of(16)] * 2)(
        state, start_state, slip, m2), "tile")

    inner, = call(
        inner_kernel, [VMEM] * 5, [shape(4, 7, 16, 128)], [scratch(8, 8)])(power, flat, *tile, rates)

    corner = neighbours(*call(corner_kernel, [VMEM] * 2, [shape(16, 128)] * 2)(*slab), "tile")

    e0, e1, e2, e3 = call(
        edge_kernel, [VMEM] * 10, [tiles_of(EDGE)] * 4,
        [scratch(8, 8), pltpu.VMEM((8, 2, 24, 128), jnp.float32), scratch(8, 2, 4), scratch(4, EDGE)])(
        power, flat, *tile, *slab, *corner, slip, inner)
    b2, b3, b1 = send(e2, 2), send(e3, 3), send(e1, 1)

    wq, wz, slipq = call(
        start_kernel, [VMEM, VMEM, ANY], [tiles_of(20), tiles_of(2), shape(16, 128)])(start_state, slip, e2)
    wxy, = call(start_tiles_kernel, [VMEM] * 6 + [ANY], [tiles_of(EDGE)])(*tile, *slab, wq, wz, e2)

    outs = call(
        second_kernel, [VMEM] * 12, [tiles_of(20)] * 4,
        [scratch(8, 4), scratch(8), scratch(8), scratch(3, 2), scratch(4, 20), pltpu.SMEM((16,), jnp.float32)])(
        a2, a3, power, m0, a1, e0, b1, b2, b3, wq, wxy, slipq)
    back = {r: send(outs[r], r) for r in (2, 3, 1)}

    result, = call(
        last_kernel, [VMEM] * 4, [shape(5, 16, 16, 128)], [scratch(4, 20), scratch(5, 16), dma(5)], HBM)(
        outs[0], back[1], back[2], back[3])
    return result[None]


def solution(mesh):
    return jax.shard_map(
        shards,
        mesh=mesh,
        in_specs=(
            P(None, "tile", "slab", None),
            P("node", None, "tile", "slab", None),
            P(None, "tile", None),
            P(),
        ),
        out_specs=P("node", None, "tile", "slab", None),
        check_vma=False,
    )
```

```python
import jax
import jax.numpy as jnp
import numpy as np
from jax import lax
from jax.experimental import pallas as pl
from jax.experimental.pallas import tpu as pltpu
from jax.sharding import PartitionSpec as P

STEP = 0.2
MAIN = 18
EDGE = 12
VMEM = pl.BlockSpec(memory_space=pltpu.VMEM)
SMEM = pl.BlockSpec(memory_space=pltpu.SMEM)
ANY = pl.BlockSpec(memory_space=pl.ANY)
HBM = pl.BlockSpec(memory_space=pltpu.HBM)


def quadrature_table():
    points = [0.25, 0.5, 0.75, 1.0]
    table = np.zeros((4, 4))
    for column in range(4):
        coeffs = [1.0]
        divisor = 1.0
        for other in range(4):
            if other != column:
                other_point = points[other]
                widened = [0.0] * (len(coeffs) + 1)
                for power, value in enumerate(coeffs):
                    widened[power + 1] += value
                    widened[power] -= other_point * value
                coeffs = widened
                divisor *= points[column] - other_point
        for line_index in range(4):
            position = points[line_index]
            total = 0.0
            for power, value in enumerate(coeffs):
                total += value * position ** (power + 1) / (power + 1)
            table[line_index, column] = total / divisor
    return table


def relative_weights(me):
    table = np.asarray(quadrature_table(), np.float32) * np.float32(STEP)

    def entry(a, b):
        value = jnp.float32(table[3 ^ a, 3 ^ b])
        for node in range(3):
            value = jnp.where(me == node, jnp.float32(table[node ^ a, node ^ b]), value)
        return value

    return [[entry(a, b) for b in range(4)] for a in range(4)]


def iotas():
    sub = lax.broadcasted_iota(jnp.int32, (16, 128), 0)
    lane = lax.broadcasted_iota(jnp.int32, (16, 128), 1)
    return sub, lane


def derived(c, g, power):
    r = jnp.exp(power * jnp.log(g * g + 0.25))
    q = c * r
    eta = (0.08 + 0.2 * c + 0.496 * (c * c)) * r
    return q, eta, 0.5 * c * q


def rate(cen, lm, lp, sm, sp, zm, zp, lead_x):
    def diffs(f):
        dl = lp(f) - lm(f)
        ds = sp(f) - sm(f)
        return (dl, ds) if lead_x else (ds, dl)

    def grads(f):
        lo, hi, a, b, n, m = lm(f), lp(f), sm(f), sp(f), zm(f), zp(f)
        x, y = (hi - lo, b - a) if lead_x else (b - a, hi - lo)
        return x, y, m - n, (lo + hi) + (a + b) + (n + m)

    c, g, u, v, w, eta = cen(0), cen(1), cen(2), cen(3), cen(4), cen(6)
    hu, hv, hw = 0.5 * u, 0.5 * v, 0.5 * w
    qx, qy, qz, qsum = grads(5)
    cx, cy, cz, _ = grads(0)
    dc = 0.3 * c * (qsum - 6.0 * cen(5)) + (0.075 * qx - hu) * cx + (0.075 * qy - hv) * cy + (0.075 * qz - hw) * cz
    ex, ey, ez, _ = grads(6)
    ax, ay, az = 0.25 * ex - hu, 0.25 * ey - hv, 0.25 * ez - hw
    ux, uy, uz, usum = grads(2)
    du = eta * (usum - 6.0 * u) + ax * ux + ay * uy + az * uz + 0.5
    vx, vy, vz, vsum = grads(3)
    dv = eta * (vsum - 6.0 * v) + ax * vx + ay * vy + az * vz - 0.5 * diffs(7)[1]
    wx, wy, wz, wsum = grads(4)
    dw = eta * (wsum - 6.0 * w) + ax * wx + ay * wy + az * wz
    strain = uy * uy + wy * wy + vx * vx + vz * vz
    dg = jnp.sqrt(strain + 1.0) - 2.0 * g
    return dc, dg, du, dv, dw


def swap_blocks(tiles, axis, block, index):
    size = 4 * block
    low = index < 2 * block
    even = (index // block) % 2 == 0
    roll = lambda t, k: pltpu.roll(t, k, axis)
    a0, a1, a2, a3 = tiles
    lo0 = jnp.where(low, a0, roll(a2, 2 * block))
    hi0 = jnp.where(low, roll(a0, 2 * block), a2)
    lo1 = jnp.where(low, a1, roll(a3, 2 * block))
    hi1 = jnp.where(low, roll(a1, 2 * block), a3)
    out = []
    for p, q in ((lo0, lo1), (hi0, hi1)):
        out.append(jnp.where(even, p, roll(q, block)))
        out.append(jnp.where(even, roll(p, size - block), q))
    return out


def edges():
    me = lax.axis_index("node")
    t, s = lax.axis_index("tile"), lax.axis_index("slab")
    return me, t == 0, t == lax.axis_size("tile") - 1, s == 0, s == lax.axis_size("slab") - 1


def pick(tiles, me):
    out = tiles[3]
    for q in range(3):
        out = jnp.where(me == q, tiles[q], out)
    return out


def reads(*refs):
    return [lambda *at, ref=ref: ref[at] for ref in refs]


def pack_z_edge(row, sides, lane):
    left = right = jnp.zeros((16, 128), jnp.float32)
    for xq in range(4):
        for f in range(5):
            place = 4 * f + xq
            spot = lane % 32 == place
            tile = row(f, xq)
            left = jnp.where(spot, pltpu.roll(tile, place + 1, 1), left)
            right = jnp.where(spot, pltpu.roll(tile, (place + 96) % 128, 1), right)
    return left, right


def slip_of(flags):
    return 1.0 - 2.0 * flags.astype(jnp.float32)


def tile_kernel(s_ref, w_ref, slip_ref, _after, up_ref, down_ref):
    for ref, up in ((up_ref, True), (down_ref, False)):
        for f in range(5):
            ref[f] = ((s_ref[f, 14]) if up else s_ref[f, 0])
            ref[5 + f] = ((s_ref[f, 15]) if up else s_ref[f, 1])
            ref[10 + f] = ((w_ref[f, 15]) if up else w_ref[f, 0])
        ref[15] = jnp.zeros((16, 128), jnp.float32)
        for side in range(2):
            ref[15, pl.ds(side, 1), :] = ((slip_ref[side, pl.ds(15, 1), :]) if up else slip_ref[side, pl.ds(0, 1), :])


def first_kernel(power_ref, s_ref, _after, m0, m1, m2, m3, rates, der, packed):
    me = lax.axis_index("node")
    sub, lane = iotas()
    power = power_ref[0:1, :]

    def derive(k, _):
        x = pl.ds(4 * k, 4)
        der[0, x], der[1, x], der[2, x] = derived(s_ref[0, x], s_ref[1, x], power)
        return _

    lax.fori_loop(0, 4, derive, 0)

    def column(xq, _):
        rows = []
        for g in range(4):
            x = 4 * g + xq
            lo = jnp.maximum(x - 1, 0)
            hi = jnp.minimum(x + 1, 15)
            at = lambda f, r: s_ref[f, r] if f < 5 else der[f - 5, r]
            rows.append(rate(
                lambda f: at(f, x), lambda f: at(f, lo), lambda f: at(f, hi),
                lambda f: pltpu.roll(at(f, x), 1, 0), lambda f: pltpu.roll(at(f, x), 15, 0),
                lambda f: pltpu.roll(at(f, x), 1, 1), lambda f: pltpu.roll(at(f, x), 127, 1), True))
        for f in range(5):
            for g in range(4):
                rates[f, 4 * g + xq] = rows[g][f]
            out = swap_blocks([rows[g][f] for g in range(4)], 1, 32, lane)
            for q in range(4):
                packed[q, f * 4 + xq] = out[q]
        return _

    lax.fori_loop(0, 4, column, 0)
    for r, m in enumerate((m0, m1, m2, m3)):
        q = me ^ r
        for f in range(5):
            for xq in (1, 2):
                m[2 * f + xq - 1] = packed[q, f * 4 + xq]
        for p in range(2):
            a0, a3 = packed[q, 8 * p], packed[q, 8 * p + 3]
            b0, b3 = packed[q, 8 * p + 4], packed[q, 8 * p + 7]
            m[10 + 3 * p] = jnp.where(lane < 32, b3, a0)
            m[11 + 3 * p] = jnp.where(lane >= 96, b0, a3)
            m[12 + 3 * p] = jnp.where(
                lane < 32, pltpu.roll(b3, 96, 1), jnp.where(lane < 96, b0, pltpu.roll(b3, 32, 1)))
        m[16] = packed[q, 16]
        m[17] = packed[q, 19]


def start_kernel(w_ref, slip_ref, _after, wq_ref, wz_ref, slipq_ref):
    me = lax.axis_index("node")
    sub, lane = iotas()
    for xq in range(4):
        for f in range(5):
            own = [w_ref[f, 4 * g + xq] for g in range(4)]
            wq_ref[f * 4 + xq] = pick(swap_blocks(own, 1, 32, lane), me)
    packs = [pack_z_edge(lambda f, xq: w_ref[f, 4 * g + xq], 2, lane) for g in range(4)]
    for side in range(2):
        wz_ref[side] = pick(swap_blocks([packs[g][side] for g in range(4)], 1, 32, lane), me)
    slipq_ref[...] = pack_y_edge(slip_ref[0], slip_ref[1], me, sub, lane)


def pack_y_edge(lower, upper, me, sub, lane):
    zero = jnp.zeros((16, 128), jnp.float32)
    tiles = swap_blocks([zero, lower, upper, zero], 0, 4, sub)
    return pick(swap_blocks(tiles, 1, 32, lane), me)


def slab_kernel(flag_hbm, s_hbm, w_hbm, up_ref, down_ref, slip_ref, rows, flags, sems):
    me = lax.axis_index("node")
    sub, lane = iotas()

    def run(up_ref, down_ref):
        copies = []
        for k, (ref, ys) in enumerate(((up_ref, (14, 15)), (down_ref, (0, 1)))):
            for r in range(2):
                copies.append(pltpu.make_async_copy(
                    s_hbm.at[:, :, ys[r], :], ref.at[:, pl.ds(16 * r, 16), :], sems.at[2 * k + r]))
            copies.append(pltpu.make_async_copy(w_hbm.at[:, :, (15, 0)[k], :], rows.at[k], sems.at[4 + k]))
        copies.append(pltpu.make_async_copy(flag_hbm, flags, sems.at[6]))
        for copy in copies:
            copy.start()
        copies[2].wait()
        copies[5].wait()
        for f in range(5):
            start = pack_y_edge(rows[1, f], rows[0, f], me, sub, lane)
            for ref, place in ((up_ref, 8), (down_ref, 4)):
                ref[f, pl.ds(32, 4), :] = start[place:place + 4]
                ref[f, pl.ds(36, 4), :] = jnp.zeros((4, 128), jnp.float32)
        for k in (0, 1, 3, 4, 6):
            copies[k].wait()

    run(up_ref, down_ref)

    slip_ref[...] = slip_of(flags[...])


def corner_kernel(slow_ref, shigh_ref, up_ref, down_ref):
    below, above = reads(slow_ref, shigh_ref)
    for ref, up in ((up_ref, True), (down_ref, False)):
        ref[pl.ds(10, 6), :] = jnp.zeros((6, 128), jnp.float32)
        for f in range(5):
            ref[pl.ds(f, 1), :] = ((below(f, pl.ds(31, 1))) if up else below(f, pl.ds(16, 1)))
            ref[pl.ds(5 + f, 1), :] = ((above(f, pl.ds(15, 1))) if up else above(f, pl.ds(0, 1)))


def fill_ext(ext, s_ref, tlow_ref, thigh_ref, t0, t7):
    lo, hi = reads(tlow_ref, thigh_ref)
    for f in range(5):
        first, last = s_ref[f, pl.ds(0, 16), :], s_ref[f, pl.ds(240, 16), :]
        ext[f, 0] = lo(f)
        ext[f, 1] = jnp.where(t0, first, lo(5 + f))
        ext[f, 2] = first
        ext[f, 3] = s_ref[f, pl.ds(16, 16), :]
        ext[f, 4] = s_ref[f, pl.ds(224, 16), :]
        ext[f, 5] = last
        ext[f, 6] = jnp.where(t7, last, hi(f))
        ext[f, 7] = hi(5 + f)


def inner_kernel(power_ref, s_ref, tlow_ref, thigh_ref, rates, out_ref, ext):
    _, t0, t7, _, _ = edges()
    sub, lane = iotas()
    fill_ext(ext, s_ref, tlow_ref, thigh_ref, t0, t7)
    ext[5], ext[6], ext[7] = derived(ext[0], ext[1], power_ref[0:1, :])

    def row(x):
        return rate(
            lambda f: ext[f, x], lambda f: ext[f, x - 1], lambda f: ext[f, x + 1],
            lambda f: pltpu.roll(ext[f, x], 1, 0), lambda f: pltpu.roll(ext[f, x], 15, 0),
            lambda f: pltpu.roll(ext[f, x], 1, 1), lambda f: pltpu.roll(ext[f, x], 127, 1), True)

    first, last = row(2), row(5)
    for f in range(5):
        for q in range(4):
            out_ref[q, f] = jnp.where(
                lane < 32, pltpu.roll(first[f], 32 * (4 - q) % 128, 1), pltpu.roll(last[f], 32 * (3 - q), 1))

    def at(g):
        def tile(f, xq):
            return first[f] if g + xq == 0 else last[f] if g + xq == 6 else rates[f, 4 * g + xq]

        return tile

    packs = [pack_z_edge(at(g), 2, lane) for g in range(4)]
    for side in range(2):
        out = swap_blocks([packs[g][side] for g in range(4)], 1, 32, lane)
        for q in range(4):
            out_ref[q, 5 + side] = out[q]


def edge_kernel(power_ref, s_ref, tlow_ref, thigh_ref, slow_ref, shigh_ref, clow_ref, chigh_ref, slip_ref,
                inner_ref, _a1, _a2, e0, e1, e2, e3, ext, yh, band, edge):
    me, t0, t7, s0, s7 = edges()
    sub, lane = iotas()
    power = power_ref[0:1, :]
    lo, hi = reads(tlow_ref, thigh_ref)
    corner_lo, corner_hi = reads(clow_ref, chigh_ref)
    below_row, above_row = reads(slow_ref, shigh_ref)
    fill_ext(ext, s_ref, tlow_ref, thigh_ref, t0, t7)
    ext[5], ext[6], ext[7] = derived(ext[0], ext[1], power)

    for side in range(2):
        ref = (below_row, above_row)[side]
        near, far = ((16, 0), (0, 16))[side]
        y, inward = ((0, 1), (15, 14))[side]
        wall = (s0, s7)[side]
        slip = slip_ref[side]
        slip_lo = lo(15, pl.ds(side, 1))
        slip_hi = hi(15, pl.ds(side, 1))
        for f in range(5):
            def ghost(value, flag):
                return -value if f == 3 else value * flag if f in (2, 4) else value

            mine = s_ref[f, pl.ds(y, 16, stride=16), :]
            yh[f, side, pl.ds(0, 16), :] = jnp.where(wall, ghost(mine, slip), ref(f, pl.ds(near, 16)))
            yh[f, side, pl.ds(16, 1), :] = jnp.where(
                wall, ghost(ext[f, 1, pl.ds(y, 1), :], slip_lo),
                jnp.where(t0, ref(f, pl.ds(near, 1)), corner_lo(pl.ds(5 * side + f, 1))))
            yh[f, side, pl.ds(17, 1), :] = jnp.where(
                wall, ghost(ext[f, 6, pl.ds(y, 1), :], slip_hi),
                jnp.where(t7, ref(f, pl.ds(near + 15, 1)), corner_hi(pl.ds(5 * side + f, 1))))
            yh[f, side, pl.ds(18, 6), :] = jnp.zeros((6, 128), jnp.float32)
            band[f, side, 0] = ref(f, pl.ds(far, 16))
            band[f, side, 1] = ref(f, pl.ds(near, 16))
            band[f, side, 2] = mine
            band[f, side, 3] = s_ref[f, pl.ds(inward, 16, stride=16), :]
        yh[5, side], yh[6, side], yh[7, side] = derived(yh[0, side], yh[1, side], power)
        band[5, side], band[6, side], band[7, side] = derived(band[0, side], band[1, side], power)

    def row(x, place):
        def below(f):
            return jnp.where(sub == 0, yh[f, 0, pl.ds(place, 1), :], pltpu.roll(ext[f, x], 1, 0))

        def above(f):
            return jnp.where(sub == 15, yh[f, 1, pl.ds(place, 1), :], pltpu.roll(ext[f, x], 15, 0))

        return rate(
            lambda f: ext[f, x], lambda f: ext[f, x - 1], lambda f: ext[f, x + 1], below, above,
            lambda f: pltpu.roll(ext[f, x], 1, 1), lambda f: pltpu.roll(ext[f, x], 127, 1), True)

    lower, upper = row(1, 16), row(6, 17)
    for f in range(5):
        for q in range(4):
            edge[q, f] = jnp.where(
                jnp.logical_or(lane < 32, lane >= 96), inner_ref[q, f],
                jnp.where(lane < 64, pltpu.roll(lower[f], (32 * (1 - q)) % 128, 1),
                          pltpu.roll(upper[f], (32 * (2 - q)) % 128, 1)))

    def band_rate(side, k):
        y = 0 if side == 0 else 15
        left = (lambda f: yh[f, side, pl.ds(16, 1), :]) if k == 1 else (lambda f: ext[f, 1, pl.ds(y, 1), :])
        right = (lambda f: yh[f, side, pl.ds(17, 1), :]) if k == 1 else (lambda f: ext[f, 6, pl.ds(y, 1), :])

        def before_x(f):
            return jnp.where(sub == 0, left(f), pltpu.roll(band[f, side, k], 1, 0))

        def after_x(f):
            return jnp.where(sub == 15, right(f), pltpu.roll(band[f, side, k], 15, 0))

        outer = (lambda f: band[f, side, 0]) if k == 1 else (lambda f: yh[f, side, pl.ds(0, 16), :])
        inner = lambda f: band[f, side, k + 1]
        before, after = (outer, inner) if side == 0 else (inner, outer)
        return rate(
            lambda f: band[f, side, k], before, after, before_x, after_x,
            lambda f: pltpu.roll(band[f, side, k], 1, 1), lambda f: pltpu.roll(band[f, side, k], 127, 1), False)

    rows = [band_rate(0, 2), band_rate(0, 1), band_rate(1, 1), band_rate(1, 2)]
    zero = jnp.zeros((16, 128), jnp.float32)
    beside = [[zero, zero] for q in range(4)]
    for f in range(5):
        out = swap_blocks(swap_blocks([r[f] for r in rows], 0, 4, sub), 1, 32, lane)
        for q in range(4):
            edge[q, 5 + f] = out[q]
            for xq in range(4):
                place = 4 * f + xq
                spot = jnp.logical_and(lane % 32 == place, sub % 4 == xq)
                for side, to, shift in ((0, (q + 1) % 4, (place + 97) % 128), (1, (q + 3) % 4, place)):
                    beside[to][side] = jnp.where(spot, pltpu.roll(out[q], shift, 1), beside[to][side])
    for q in range(4):
        for side in range(2):
            b = beside[q][side]
            low = b + pltpu.roll(b, 15, 0)
            low = low + pltpu.roll(low, 14, 0)
            high = b + pltpu.roll(b, 1, 0)
            high = high + pltpu.roll(high, 2, 0)
            edge[q, 10 + side] = jnp.where(sub == 0, low, jnp.where(sub == 15, high, inner_ref[q, 5 + side]))
    for r, e in enumerate((e0, e1, e2, e3)):
        e[...] = edge[me ^ r]


def start_tiles_kernel(tlow_ref, thigh_ref, slow_ref, shigh_ref, wq_ref, wz_ref, _after, wxy_ref):
    me = lax.axis_index("node")
    sub, lane = iotas()
    lo, hi = reads(tlow_ref, thigh_ref)
    below, above = reads(slow_ref, shigh_ref)
    for f in range(5):
        a = pltpu.roll(lo(10 + f), (5 - me) % 4 * 32, 1)
        b = pltpu.roll(hi(10 + f), (6 - me) % 4 * 32, 1)
        wxy_ref[f] = jnp.where(
            lane < 32, wq_ref[f * 4], jnp.where(lane < 64, a, jnp.where(lane < 96, b, wq_ref[f * 4 + 3])))
        wxy_ref[5 + f, pl.ds(4, 4), :] = below(f, pl.ds(32, 4))
        wxy_ref[5 + f, pl.ds(8, 4), :] = above(f, pl.ds(32, 4))
        for xq in range(4):
            wxy_ref[5 + f, pl.ds(xq, 1), :] = wq_ref[f * 4 + xq, pl.ds(0, 1), :]
            wxy_ref[5 + f, pl.ds(12 + xq, 1), :] = wq_ref[f * 4 + xq, pl.ds(15, 1), :]
    for side in range(2):
        wxy_ref[10 + side] = wz_ref[side]


def second_kernel(a2, a3, power_ref, a0, a1, b0, b1, b2, b3, wq_ref, wxy_ref, slipq_ref,
                  o0, o1, o2, o3, main, xh, yh, zh, rates, table):
    me, t0, t7, s0, s7 = edges()
    sub, lane = iotas()
    power = power_ref[0:1, :]
    slip = slipq_ref[...]
    at_lower = jnp.logical_and(jnp.logical_and(sub >= 4, sub < 8), s0)
    at_upper = jnp.logical_and(jnp.logical_and(sub >= 8, sub < 12), s7)
    arrived = ((a0, 0), (a1, 0), (a2, 0), (a3, 0))
    edge = ((b0, 0), (b1, 0), (b2, 0), (b3, 0))
    weights = relative_weights(me)
    for m in range(4):
        for r in range(4):
            table[m * 4 + r] = weights[m][r]

    def node(m, _):
        weight = [table[m * 4 + r] for r in range(4)]

        def mix(refs, k):
            out = None
            for r, (ref, base) in enumerate(refs):
                term = weight[r] * ref[base + k]
                out = term if out is None else out + term
            return out

        outer = {}
        for p in range(2):
            a0, a3, b = (mix(arrived, 10 + 3 * p + k) for k in range(3))
            outer[2 * p] = a0, a3
            outer[2 * p + 1] = jnp.where(lane < 96, b, a3), jnp.where(
                lane < 32, a0, jnp.where(lane < 64, pltpu.roll(b, 32, 1), pltpu.roll(b, 96, 1)))
        outer[4] = mix(arrived, 16), mix(arrived, 17)

        for f in range(5):
            xb = wxy_ref[f] + mix(edge, f)
            yb = wxy_ref[5 + f] + mix(edge, 5 + f)
            yh[f] = yb
            for xq in range(4):
                tile = wq_ref[f * 4 + xq] + (mix(arrived, 2 * f + xq - 1) if xq in (1, 2) else outer[f][xq // 3])
                if xq == 0:
                    tile = jnp.where(lane < 32, xb, tile)
                if xq == 3:
                    tile = jnp.where(lane >= 96, xb, tile)
                tile = jnp.where(sub == 0, yh[f, pl.ds(xq, 1), :], tile)
                tile = jnp.where(sub == 15, yh[f, pl.ds(12 + xq, 1), :], tile)
                main[f, xq] = tile
            xh[f] = jnp.where(
                lane < 64, jnp.where(t0, main[f, 0], pltpu.roll(xb, 96, 1)),
                jnp.where(t7, main[f, 3], pltpu.roll(xb, 32, 1)))
            lower, upper = pltpu.roll(yb, 4, 0), pltpu.roll(yb, 12, 0)
            if f == 3:
                lower, upper = -lower, -upper
            if f in (2, 4):
                lower, upper = lower * slip, upper * slip
            yh[f] = jnp.where(at_lower, lower, jnp.where(at_upper, upper, yb))
        for xq in range(4):
            main[5, xq], main[6, xq], main[7, xq] = derived(main[0, xq], main[1, xq], power)
        xh[5], xh[6], xh[7] = derived(xh[0], xh[1], power)
        yh[5], yh[6], yh[7] = derived(yh[0], yh[1], power)
        for side in range(2):
            z = wxy_ref[10 + side] + mix(edge, 10 + side)
            zh[0, side] = z
            q, eta, _s = derived(z, pltpu.roll(z, 124, 1), power)
            zh[1, side], zh[2, side] = q, eta
        for xq in range(4):
            def left(f):
                if xq > 0:
                    return main[f, xq - 1]
                return jnp.where(lane < 32, xh[f], pltpu.roll(main[f, 3], 32, 1))

            def right(f):
                if xq < 3:
                    return main[f, xq + 1]
                return jnp.where(lane >= 96, xh[f], pltpu.roll(main[f, 0], 96, 1))

            def below(f):
                return jnp.where(sub == 0, yh[f, pl.ds(4 + xq, 1), :], pltpu.roll(main[f, xq], 1, 0))

            def above(f):
                return jnp.where(sub == 15, yh[f, pl.ds(8 + xq, 1), :], pltpu.roll(main[f, xq], 15, 0))

            def spot(f):
                return (0, 4 * f + xq) if f < 5 else (f - 4, xq)

            def before(f):
                k, i = spot(f)
                return jnp.where(lane % 32 == 0, pltpu.roll(zh[k, 0], (128 - i) % 128, 1), pltpu.roll(main[f, xq], 1, 1))

            def after(f):
                k, i = spot(f)
                return jnp.where(lane % 32 == 31, pltpu.roll(zh[k, 1], 31 - i, 1), pltpu.roll(main[f, xq], 127, 1))

            out = rate(lambda f: main[f, xq], left, right, below, above, before, after, True)
            for f in range(5):
                rates[m, f * 4 + xq] = out[f]
        return _

    lax.fori_loop(0, 4, node, 0, unroll=2)

    def combine(k, _):
        have = [rates[r, k] for r in range(4)]
        for m, o in enumerate((o0, o1, o2, o3)):
            out = wq_ref[k]
            for r in range(4):
                out = out + weights[m][r] * have[r]
            o[k] = out
        return _

    lax.fori_loop(0, 20, combine, 0, unroll=4)


def last_kernel(r0, r1, r2, r3, out_hbm, quarter, out, sems):
    me = lax.axis_index("node")
    _, lane = iotas()
    def copy(f):
        return pltpu.make_async_copy(out.at[f], out_hbm.at[f], sems.at[f])

    def field(f, _):
        for r, ref in enumerate((r0, r1, r2, r3)):
            quarter[me ^ r, pl.ds(4 * f, 4)] = ref[pl.ds(4 * f, 4)]
        for xq in range(4):
            tiles = swap_blocks([quarter[q, 4 * f + xq] for q in range(4)], 1, 32, lane)
            for g in range(4):
                out[f, 4 * g + xq] = tiles[g]
        copy(f).start()
        return _

    lax.fori_loop(0, 5, field, 0)
    for f in range(5):
        copy(f).wait()


def tiles_of(n):
    return jax.ShapeDtypeStruct((n, 16, 128), jnp.float32)


def shards(start_state, iterate, wall_flags, reg_index):
    state = iterate[0]
    flat = state.reshape(5, 256, 128)
    params = pltpu.CompilerParams(vmem_limit_bytes=32 * 1024 * 1024)
    scratch = lambda *shape: pltpu.VMEM(shape + (16, 128), jnp.float32)
    shape = lambda *dims: jax.ShapeDtypeStruct(dims, jnp.float32)
    dma = lambda n: pltpu.SemaphoreType.DMA((n,))

    def call(kernel, ins, outs, scratch_shapes=(), place=VMEM):
        return pl.pallas_call(
            kernel, out_shape=outs, in_specs=ins, out_specs=[place] * len(outs),
            scratch_shapes=scratch_shapes, compiler_params=params,
            cost_estimate=pl.CostEstimate(flops=1, bytes_accessed=1, transcendentals=0))

    def neighbours(up, down, axis):
        size = lax.axis_size(axis)
        from_lower = lax.ppermute(up, axis, [(i, (i + 1) % size) for i in range(size)])
        from_upper = lax.ppermute(down, axis, [((i + 1) % size, i) for i in range(size)])
        return from_lower, from_upper

    def send(tiles, r):
        return lax.ppermute(tiles, "node", [(i, i ^ r) for i in range(4)])

    far = lambda x: pltpu.with_memory_space_constraint(x, pltpu.HBM)
    slab_near, slab_next, slip = call(
        slab_kernel, [HBM] * 3, [shape(5, 40, 128)] * 2 + [shape(2, 16, 128)],
        [scratch(2, 5), pltpu.VMEM((2, 16, 128), jnp.int32), dma(7)])(
        far(wall_flags), far(state), far(start_state))
    power = jnp.broadcast_to(0.2 + 0.05 * reg_index.astype(jnp.float32), (8, 128))
    slab = neighbours(slab_near, slab_next, "slab")

    m0, m1, m2, m3, rates = call(
        first_kernel, [VMEM, VMEM, ANY], [tiles_of(MAIN)] * 4 + [shape(5, 16, 16, 128)],
        [scratch(3, 16), scratch(4, 20)])(power, state, slip)
    a2, a3, a1 = send(m2, 2), send(m3, 3), send(m1, 1)

    tile = neighbours(*call(tile_kernel, [VMEM] * 3 + [ANY], [tiles_of(16)] * 2)(
        state, start_state, slip, m2), "tile")

    inner, = call(
        inner_kernel, [VMEM] * 5, [shape(4, 7, 16, 128)], [scratch(8, 8)])(power, flat, *tile, rates)

    corner = neighbours(*call(corner_kernel, [VMEM] * 2, [shape(16, 128)] * 2)(*slab), "tile")

    e0, e1, e2, e3 = call(
        edge_kernel, [VMEM] * 10 + [ANY] * 2, [tiles_of(EDGE)] * 4,
        [scratch(8, 8), pltpu.VMEM((8, 2, 24, 128), jnp.float32), scratch(8, 2, 4), scratch(4, EDGE)])(
        power, flat, *tile, *slab, *corner, slip, inner, a1, a2)
    b2, b3, b1 = send(e2, 2), send(e3, 3), send(e1, 1)

    wq, wz, slipq = call(
        start_kernel, [VMEM, VMEM, ANY], [tiles_of(20), tiles_of(2), shape(16, 128)])(start_state, slip, e2)
    wxy, = call(start_tiles_kernel, [VMEM] * 6 + [ANY], [tiles_of(EDGE)])(*tile, *slab, wq, wz, e2)

    outs = call(
        second_kernel, [VMEM] * 12, [tiles_of(20)] * 4,
        [scratch(8, 4), scratch(8), scratch(8), scratch(3, 2), scratch(4, 20), pltpu.SMEM((16,), jnp.float32)])(
        a2, a3, power, m0, a1, e0, b1, b2, b3, wq, wxy, slipq)
    back = {r: send(outs[r], r) for r in (2, 3, 1)}

    result, = call(
        last_kernel, [VMEM] * 4, [shape(5, 16, 16, 128)], [scratch(4, 20), scratch(5, 16), dma(5)], HBM)(
        outs[0], back[1], back[2], back[3])
    return result[None]


def solution(mesh):
    return jax.shard_map(
        shards,
        mesh=mesh,
        in_specs=(
            P(None, "tile", "slab", None),
            P("node", None, "tile", "slab", None),
            P(None, "tile", None),
            P(),
        ),
        out_specs=P("node", None, "tile", "slab", None),
        check_vma=False,
    )
```

```python
import jax
import jax.numpy as jnp
import numpy as np
from jax import lax
from jax.experimental import pallas as pl
from jax.experimental.pallas import tpu as pltpu
from jax.sharding import PartitionSpec as P

STEP = 0.2
MAIN = 18
EDGE = 12
VMEM = pl.BlockSpec(memory_space=pltpu.VMEM)
SMEM = pl.BlockSpec(memory_space=pltpu.SMEM)
ANY = pl.BlockSpec(memory_space=pl.ANY)
HBM = pl.BlockSpec(memory_space=pltpu.HBM)


def quadrature_table():
    points = [0.25, 0.5, 0.75, 1.0]
    table = np.zeros((4, 4))
    for column in range(4):
        coeffs = [1.0]
        divisor = 1.0
        for other in range(4):
            if other != column:
                other_point = points[other]
                widened = [0.0] * (len(coeffs) + 1)
                for power, value in enumerate(coeffs):
                    widened[power + 1] += value
                    widened[power] -= other_point * value
                coeffs = widened
                divisor *= points[column] - other_point
        for line_index in range(4):
            position = points[line_index]
            total = 0.0
            for power, value in enumerate(coeffs):
                total += value * position ** (power + 1) / (power + 1)
            table[line_index, column] = total / divisor
    return table


def relative_weights(me):
    table = np.asarray(quadrature_table(), np.float32) * np.float32(STEP)

    def entry(a, b):
        value = jnp.float32(table[3 ^ a, 3 ^ b])
        for node in range(3):
            value = jnp.where(me == node, jnp.float32(table[node ^ a, node ^ b]), value)
        return value

    return [[entry(a, b) for b in range(4)] for a in range(4)]


def iotas():
    sub = lax.broadcasted_iota(jnp.int32, (16, 128), 0)
    lane = lax.broadcasted_iota(jnp.int32, (16, 128), 1)
    return sub, lane


def derived(c, g, power):
    r = jnp.exp(power * jnp.log(g * g + 0.25))
    q = c * r
    eta = (0.08 + 0.2 * c + 0.496 * (c * c)) * r
    return q, eta, 0.5 * c * q


def rate(cen, lm, lp, sm, sp, zm, zp, lead_x):
    def diffs(f):
        dl = lp(f) - lm(f)
        ds = sp(f) - sm(f)
        return (dl, ds) if lead_x else (ds, dl)

    def grads(f):
        lo, hi, a, b, n, m = lm(f), lp(f), sm(f), sp(f), zm(f), zp(f)
        x, y = (hi - lo, b - a) if lead_x else (b - a, hi - lo)
        return x, y, m - n, (lo + hi) + (a + b) + (n + m)

    c, g, u, v, w, eta = cen(0), cen(1), cen(2), cen(3), cen(4), cen(6)
    hu, hv, hw = 0.5 * u, 0.5 * v, 0.5 * w
    qx, qy, qz, qsum = grads(5)
    cx, cy, cz, _ = grads(0)
    dc = 0.3 * c * (qsum - 6.0 * cen(5)) + (0.075 * qx - hu) * cx + (0.075 * qy - hv) * cy + (0.075 * qz - hw) * cz
    ex, ey, ez, _ = grads(6)
    ax, ay, az = 0.25 * ex - hu, 0.25 * ey - hv, 0.25 * ez - hw
    ux, uy, uz, usum = grads(2)
    du = eta * (usum - 6.0 * u) + ax * ux + ay * uy + az * uz + 0.5
    vx, vy, vz, vsum = grads(3)
    dv = eta * (vsum - 6.0 * v) + ax * vx + ay * vy + az * vz - 0.5 * diffs(7)[1]
    wx, wy, wz, wsum = grads(4)
    dw = eta * (wsum - 6.0 * w) + ax * wx + ay * wy + az * wz
    strain = uy * uy + wy * wy + vx * vx + vz * vz
    dg = jnp.sqrt(strain + 1.0) - 2.0 * g
    return dc, dg, du, dv, dw


def swap_blocks(tiles, axis, block, index):
    size = 4 * block
    low = index < 2 * block
    even = (index // block) % 2 == 0
    roll = lambda t, k: pltpu.roll(t, k, axis)
    a0, a1, a2, a3 = tiles
    lo0 = jnp.where(low, a0, roll(a2, 2 * block))
    hi0 = jnp.where(low, roll(a0, 2 * block), a2)
    lo1 = jnp.where(low, a1, roll(a3, 2 * block))
    hi1 = jnp.where(low, roll(a1, 2 * block), a3)
    out = []
    for p, q in ((lo0, lo1), (hi0, hi1)):
        out.append(jnp.where(even, p, roll(q, block)))
        out.append(jnp.where(even, roll(p, size - block), q))
    return out


def edges():
    me = lax.axis_index("node")
    t, s = lax.axis_index("tile"), lax.axis_index("slab")
    return me, t == 0, t == lax.axis_size("tile") - 1, s == 0, s == lax.axis_size("slab") - 1


def pick(tiles, me):
    out = tiles[3]
    for q in range(3):
        out = jnp.where(me == q, tiles[q], out)
    return out


def reads(*refs):
    return [lambda *at, ref=ref: ref[at] for ref in refs]


def pack_z_edge(row, sides, lane):
    left = right = jnp.zeros((16, 128), jnp.float32)
    for xq in range(4):
        for f in range(5):
            place = 4 * f + xq
            spot = lane % 32 == place
            tile = row(f, xq)
            left = jnp.where(spot, pltpu.roll(tile, place + 1, 1), left)
            right = jnp.where(spot, pltpu.roll(tile, (place + 96) % 128, 1), right)
    return left, right


def slip_of(flags):
    return 1.0 - 2.0 * flags.astype(jnp.float32)


def tile_kernel(s_ref, w_ref, _after, up_ref, down_ref):
    me = lax.axis_index("node")
    _, lane = iotas()
    for ref, rows, x in ((up_ref, (14, 15), 15), (down_ref, (0, 1), 0)):
        for f in range(5):
            ref[f] = s_ref[f, rows[0]]
            ref[5 + f] = s_ref[f, rows[1]]
        own = [pltpu.roll(w_ref[f, x], (f + 4 - me) % 4 * 32, 1) for f in range(5)]
        ref[10] = jnp.where(lane < 32, own[0], jnp.where(lane < 64, own[1], jnp.where(lane < 96, own[2], own[3])))
        ref[11] = own[4]
        ref[12] = own[4]


def first_kernel(power_ref, s_ref, _after, m0, m1, m2, m3, rates, der, packed):
    me = lax.axis_index("node")
    sub, lane = iotas()
    power = power_ref[0:1, :]

    def derive(k, _):
        x = pl.ds(4 * k, 4)
        der[0, x], der[1, x], der[2, x] = derived(s_ref[0, x], s_ref[1, x], power)
        return _

    lax.fori_loop(0, 4, derive, 0)

    def column(xq, _):
        rows = []
        for g in range(4):
            x = 4 * g + xq
            lo = jnp.maximum(x - 1, 0)
            hi = jnp.minimum(x + 1, 15)
            at = lambda f, r: s_ref[f, r] if f < 5 else der[f - 5, r]
            rows.append(rate(
                lambda f: at(f, x), lambda f: at(f, lo), lambda f: at(f, hi),
                lambda f: pltpu.roll(at(f, x), 1, 0), lambda f: pltpu.roll(at(f, x), 15, 0),
                lambda f: pltpu.roll(at(f, x), 1, 1), lambda f: pltpu.roll(at(f, x), 127, 1), True))
        for f in range(5):
            for g in range(4):
                rates[f, 4 * g + xq] = rows[g][f]
            out = swap_blocks([rows[g][f] for g in range(4)], 1, 32, lane)
            for q in range(4):
                packed[q, f * 4 + xq] = out[q]
        return _

    lax.fori_loop(0, 4, column, 0)
    for r, m in enumerate((m0, m1, m2, m3)):
        q = me ^ r

        def put(k, tile):
            m[pl.ds(14 * k + 1, 14), :] = tile[1:15]

        m[pl.ds(0, 1), :] = jnp.zeros((1, 128), jnp.float32)
        m[pl.ds(14 * MAIN + 1, 3), :] = jnp.zeros((3, 128), jnp.float32)
        for f in range(5):
            for xq in (1, 2):
                put(2 * f + xq - 1, packed[q, f * 4 + xq])
        for p in range(2):
            a0, a3 = packed[q, 8 * p], packed[q, 8 * p + 3]
            b0, b3 = packed[q, 8 * p + 4], packed[q, 8 * p + 7]
            put(10 + 3 * p, jnp.where(lane < 32, b3, a0))
            put(11 + 3 * p, jnp.where(lane >= 96, b0, a3))
            put(12 + 3 * p, jnp.where(
                lane < 32, pltpu.roll(b3, 96, 1), jnp.where(lane < 96, b0, pltpu.roll(b3, 32, 1))))
        put(16, packed[q, 16])
        put(17, packed[q, 19])


def start_kernel(w_ref, slip_ref, _after, wq_ref, wz_ref, slipq_ref):
    me = lax.axis_index("node")
    sub, lane = iotas()
    for xq in range(4):
        for f in range(5):
            own = [w_ref[f, 4 * g + xq] for g in range(4)]
            wq_ref[f * 4 + xq] = pick(swap_blocks(own, 1, 32, lane), me)
    packs = [pack_z_edge(lambda f, xq: w_ref[f, 4 * g + xq], 2, lane) for g in range(4)]
    for side in range(2):
        wz_ref[side] = pick(swap_blocks([packs[g][side] for g in range(4)], 1, 32, lane), me)
    slipq_ref[...] = pack_y_edge(slip_ref[0], slip_ref[1], me, sub, lane)


def pack_y_edge(lower, upper, me, sub, lane):
    zero = jnp.zeros((16, 128), jnp.float32)
    tiles = swap_blocks([zero, lower, upper, zero], 0, 4, sub)
    return pick(swap_blocks(tiles, 1, 32, lane), me)


def slab_kernel(flag_hbm, s_hbm, w_hbm, up_ref, down_ref, slip_ref, rows, flags, sems):
    me = lax.axis_index("node")
    sub, lane = iotas()

    def run(up_ref, down_ref):
        copies = []
        for k, (ref, ys) in enumerate(((up_ref, (14, 15)), (down_ref, (0, 1)))):
            for r in range(2):
                copies.append(pltpu.make_async_copy(
                    s_hbm.at[:, :, ys[r], :], ref.at[:, pl.ds(16 * r, 16), :], sems.at[2 * k + r]))
            copies.append(pltpu.make_async_copy(w_hbm.at[:, :, (15, 0)[k], :], rows.at[k], sems.at[4 + k]))
        copies.append(pltpu.make_async_copy(flag_hbm, flags, sems.at[6]))
        for copy in copies:
            copy.start()
        copies[2].wait()
        copies[5].wait()
        for f in range(5):
            start = pack_y_edge(rows[1, f], rows[0, f], me, sub, lane)
            for ref, place in ((up_ref, 8), (down_ref, 4)):
                ref[f, pl.ds(32, 4), :] = start[place:place + 4]
                ref[f, pl.ds(36, 4), :] = jnp.zeros((4, 128), jnp.float32)
        for k in (0, 1, 3, 4, 6):
            copies[k].wait()

    run(up_ref, down_ref)

    slip_ref[...] = slip_of(flags[...])


def corner_kernel(slow_ref, shigh_ref, slip_ref, up_ref, down_ref):
    below, above = reads(slow_ref, shigh_ref)
    for ref, up in ((up_ref, True), (down_ref, False)):
        for side in range(2):
            ref[pl.ds(10 + side, 1), :] = slip_ref[side, pl.ds(15 if up else 0, 1), :]
        ref[pl.ds(12, 4), :] = jnp.zeros((4, 128), jnp.float32)
        for f in range(5):
            ref[pl.ds(f, 1), :] = ((below(f, pl.ds(31, 1))) if up else below(f, pl.ds(16, 1)))
            ref[pl.ds(5 + f, 1), :] = ((above(f, pl.ds(15, 1))) if up else above(f, pl.ds(0, 1)))


def fill_ext(ext, s_ref, tlow_ref, thigh_ref, t0, t7):
    lo, hi = reads(tlow_ref, thigh_ref)
    for f in range(5):
        first, last = s_ref[f, pl.ds(0, 16), :], s_ref[f, pl.ds(240, 16), :]
        ext[f, 0] = lo(f)
        ext[f, 1] = jnp.where(t0, first, lo(5 + f))
        ext[f, 2] = first
        ext[f, 3] = s_ref[f, pl.ds(16, 16), :]
        ext[f, 4] = s_ref[f, pl.ds(224, 16), :]
        ext[f, 5] = last
        ext[f, 6] = jnp.where(t7, last, hi(f))
        ext[f, 7] = hi(5 + f)


def inner_kernel(power_ref, s_ref, tlow_ref, thigh_ref, rates, out_ref, ext):
    _, t0, t7, _, _ = edges()
    sub, lane = iotas()
    fill_ext(ext, s_ref, tlow_ref, thigh_ref, t0, t7)
    ext[5], ext[6], ext[7] = derived(ext[0], ext[1], power_ref[0:1, :])

    def row(x):
        return rate(
            lambda f: ext[f, x], lambda f: ext[f, x - 1], lambda f: ext[f, x + 1],
            lambda f: pltpu.roll(ext[f, x], 1, 0), lambda f: pltpu.roll(ext[f, x], 15, 0),
            lambda f: pltpu.roll(ext[f, x], 1, 1), lambda f: pltpu.roll(ext[f, x], 127, 1), True)

    first, last = row(2), row(5)
    for f in range(5):
        for q in range(4):
            out_ref[q, f] = jnp.where(
                lane < 32, pltpu.roll(first[f], 32 * (4 - q) % 128, 1), pltpu.roll(last[f], 32 * (3 - q), 1))

    def at(g):
        def tile(f, xq):
            return first[f] if g + xq == 0 else last[f] if g + xq == 6 else rates[f, 4 * g + xq]

        return tile

    packs = [pack_z_edge(at(g), 2, lane) for g in range(4)]
    for side in range(2):
        out = swap_blocks([packs[g][side] for g in range(4)], 1, 32, lane)
        for q in range(4):
            out_ref[q, 5 + side] = out[q]


def edge_kernel(power_ref, s_ref, slow_ref, shigh_ref, clow_ref, chigh_ref, slip_ref,
                inner_ref, ext, _a1, _a2, e0, e1, e2, e3, yh, band, edge):
    me, t0, t7, s0, s7 = edges()
    sub, lane = iotas()
    power = power_ref[0:1, :]
    corner_lo, corner_hi = reads(clow_ref, chigh_ref)
    below_row, above_row = reads(slow_ref, shigh_ref)

    for side in range(2):
        ref = (below_row, above_row)[side]
        near, far = ((16, 0), (0, 16))[side]
        y, inward = ((0, 1), (15, 14))[side]
        wall = (s0, s7)[side]
        slip = slip_ref[side]
        slip_lo = corner_lo(pl.ds(10 + side, 1))
        slip_hi = corner_hi(pl.ds(10 + side, 1))
        for f in range(5):
            def ghost(value, flag):
                return -value if f == 3 else value * flag if f in (2, 4) else value

            mine = s_ref[f, pl.ds(y, 16, stride=16), :]
            yh[f, side, pl.ds(0, 16), :] = jnp.where(wall, ghost(mine, slip), ref(f, pl.ds(near, 16)))
            yh[f, side, pl.ds(16, 1), :] = jnp.where(
                wall, ghost(ext[f, 1, pl.ds(y, 1), :], slip_lo),
                jnp.where(t0, ref(f, pl.ds(near, 1)), corner_lo(pl.ds(5 * side + f, 1))))
            yh[f, side, pl.ds(17, 1), :] = jnp.where(
                wall, ghost(ext[f, 6, pl.ds(y, 1), :], slip_hi),
                jnp.where(t7, ref(f, pl.ds(near + 15, 1)), corner_hi(pl.ds(5 * side + f, 1))))
            yh[f, side, pl.ds(18, 6), :] = jnp.zeros((6, 128), jnp.float32)
            band[f, side, 0] = ref(f, pl.ds(far, 16))
            band[f, side, 1] = ref(f, pl.ds(near, 16))
            band[f, side, 2] = mine
            band[f, side, 3] = s_ref[f, pl.ds(inward, 16, stride=16), :]
        yh[5, side], yh[6, side], yh[7, side] = derived(yh[0, side], yh[1, side], power)
        band[5, side], band[6, side], band[7, side] = derived(band[0, side], band[1, side], power)

    def row(x, place):
        def below(f):
            return jnp.where(sub == 0, yh[f, 0, pl.ds(place, 1), :], pltpu.roll(ext[f, x], 1, 0))

        def above(f):
            return jnp.where(sub == 15, yh[f, 1, pl.ds(place, 1), :], pltpu.roll(ext[f, x], 15, 0))

        return rate(
            lambda f: ext[f, x], lambda f: ext[f, x - 1], lambda f: ext[f, x + 1], below, above,
            lambda f: pltpu.roll(ext[f, x], 1, 1), lambda f: pltpu.roll(ext[f, x], 127, 1), True)

    lower, upper = row(1, 16), row(6, 17)
    for f in range(5):
        for q in range(4):
            edge[q, f] = jnp.where(
                jnp.logical_or(lane < 32, lane >= 96), inner_ref[q, f],
                jnp.where(lane < 64, pltpu.roll(lower[f], (32 * (1 - q)) % 128, 1),
                          pltpu.roll(upper[f], (32 * (2 - q)) % 128, 1)))

    def band_rate(side, k):
        y = 0 if side == 0 else 15
        left = (lambda f: yh[f, side, pl.ds(16, 1), :]) if k == 1 else (lambda f: ext[f, 1, pl.ds(y, 1), :])
        right = (lambda f: yh[f, side, pl.ds(17, 1), :]) if k == 1 else (lambda f: ext[f, 6, pl.ds(y, 1), :])

        def before_x(f):
            return jnp.where(sub == 0, left(f), pltpu.roll(band[f, side, k], 1, 0))

        def after_x(f):
            return jnp.where(sub == 15, right(f), pltpu.roll(band[f, side, k], 15, 0))

        outer = (lambda f: band[f, side, 0]) if k == 1 else (lambda f: yh[f, side, pl.ds(0, 16), :])
        inner = lambda f: band[f, side, k + 1]
        before, after = (outer, inner) if side == 0 else (inner, outer)
        return rate(
            lambda f: band[f, side, k], before, after, before_x, after_x,
            lambda f: pltpu.roll(band[f, side, k], 1, 1), lambda f: pltpu.roll(band[f, side, k], 127, 1), False)

    rows = [band_rate(0, 2), band_rate(0, 1), band_rate(1, 1), band_rate(1, 2)]
    zero = jnp.zeros((16, 128), jnp.float32)
    beside = [[zero, zero] for q in range(4)]
    for f in range(5):
        out = swap_blocks(swap_blocks([r[f] for r in rows], 0, 4, sub), 1, 32, lane)
        for q in range(4):
            edge[q, 5 + f] = out[q]
            for xq in range(4):
                place = 4 * f + xq
                spot = jnp.logical_and(lane % 32 == place, sub % 4 == xq)
                for side, to, shift in ((0, (q + 1) % 4, (place + 97) % 128), (1, (q + 3) % 4, place)):
                    beside[to][side] = jnp.where(spot, pltpu.roll(out[q], shift, 1), beside[to][side])
    for q in range(4):
        for side in range(2):
            b = beside[q][side]
            low = b + pltpu.roll(b, 15, 0)
            low = low + pltpu.roll(low, 14, 0)
            high = b + pltpu.roll(b, 1, 0)
            high = high + pltpu.roll(high, 2, 0)
            edge[q, 10 + side] = jnp.where(sub == 0, low, jnp.where(sub == 15, high, inner_ref[q, 5 + side]))
    for r, e in enumerate((e0, e1, e2, e3)):
        e[...] = edge[me ^ r]


def start_tiles_kernel(tlow_ref, thigh_ref, slow_ref, shigh_ref, wq_ref, wz_ref, _after, wxy_ref):
    me = lax.axis_index("node")
    sub, lane = iotas()
    lo, hi = reads(tlow_ref, thigh_ref)
    below, above = reads(slow_ref, shigh_ref)
    for f in range(5):
        a = pltpu.roll(lo(10 + f // 4), (5 - f % 4) % 4 * 32, 1)
        b = pltpu.roll(hi(10 + f // 4), (6 - f % 4) % 4 * 32, 1)
        wxy_ref[f] = jnp.where(
            lane < 32, wq_ref[f * 4], jnp.where(lane < 64, a, jnp.where(lane < 96, b, wq_ref[f * 4 + 3])))
        wxy_ref[5 + f, pl.ds(4, 4), :] = below(f, pl.ds(32, 4))
        wxy_ref[5 + f, pl.ds(8, 4), :] = above(f, pl.ds(32, 4))
        for xq in range(4):
            wxy_ref[5 + f, pl.ds(xq, 1), :] = wq_ref[f * 4 + xq, pl.ds(0, 1), :]
            wxy_ref[5 + f, pl.ds(12 + xq, 1), :] = wq_ref[f * 4 + xq, pl.ds(15, 1), :]
    for side in range(2):
        wxy_ref[10 + side] = wz_ref[side]


def second_kernel(a2, a3, power_ref, a0, a1, b0, b1, b2, b3, wq_ref, wxy_ref, slipq_ref,
                  o0, o1, o2, o3, main, xh, yh, zh, rates, table):
    me, t0, t7, s0, s7 = edges()
    sub, lane = iotas()
    power = power_ref[0:1, :]
    slip = slipq_ref[...]
    at_lower = jnp.logical_and(jnp.logical_and(sub >= 4, sub < 8), s0)
    at_upper = jnp.logical_and(jnp.logical_and(sub >= 8, sub < 12), s7)
    arrived, edge = (a0, a1, a2, a3), (b0, b1, b2, b3)
    weights = relative_weights(me)
    for m in range(4):
        for r in range(4):
            table[m * 4 + r] = weights[m][r]

    def node(m, _):
        weight = [table[m * 4 + r] for r in range(4)]

        def mix(refs, k):
            out = None
            for r, ref in enumerate(refs):
                term = weight[r] * (ref[pl.ds(14 * k, 16), :] if refs is arrived else ref[k])
                out = term if out is None else out + term
            return out

        outer = {}
        for p in range(2):
            a0, a3, b = (mix(arrived, 10 + 3 * p + k) for k in range(3))
            outer[2 * p] = a0, a3
            outer[2 * p + 1] = jnp.where(lane < 96, b, a3), jnp.where(
                lane < 32, a0, jnp.where(lane < 64, pltpu.roll(b, 32, 1), pltpu.roll(b, 96, 1)))
        outer[4] = mix(arrived, 16), mix(arrived, 17)

        for f in range(5):
            xb = wxy_ref[f] + mix(edge, f)
            yb = wxy_ref[5 + f] + mix(edge, 5 + f)
            yh[f] = yb
            for xq in range(4):
                tile = wq_ref[f * 4 + xq] + (mix(arrived, 2 * f + xq - 1) if xq in (1, 2) else outer[f][xq // 3])
                if xq == 0:
                    tile = jnp.where(lane < 32, xb, tile)
                if xq == 3:
                    tile = jnp.where(lane >= 96, xb, tile)
                tile = jnp.where(sub == 0, yh[f, pl.ds(xq, 1), :], tile)
                tile = jnp.where(sub == 15, yh[f, pl.ds(12 + xq, 1), :], tile)
                main[f, xq] = tile
            xh[f] = jnp.where(
                lane < 64, jnp.where(t0, main[f, 0], pltpu.roll(xb, 96, 1)),
                jnp.where(t7, main[f, 3], pltpu.roll(xb, 32, 1)))
            lower, upper = pltpu.roll(yb, 4, 0), pltpu.roll(yb, 12, 0)
            if f == 3:
                lower, upper = -lower, -upper
            if f in (2, 4):
                lower, upper = lower * slip, upper * slip
            yh[f] = jnp.where(at_lower, lower, jnp.where(at_upper, upper, yb))
        for xq in range(4):
            main[5, xq], main[6, xq], main[7, xq] = derived(main[0, xq], main[1, xq], power)
        xh[5], xh[6], xh[7] = derived(xh[0], xh[1], power)
        yh[5], yh[6], yh[7] = derived(yh[0], yh[1], power)
        for side in range(2):
            z = wxy_ref[10 + side] + mix(edge, 10 + side)
            zh[0, side] = z
            q, eta, _s = derived(z, pltpu.roll(z, 124, 1), power)
            zh[1, side], zh[2, side] = q, eta
        for xq in range(4):
            def left(f):
                if xq > 0:
                    return main[f, xq - 1]
                return jnp.where(lane < 32, xh[f], pltpu.roll(main[f, 3], 32, 1))

            def right(f):
                if xq < 3:
                    return main[f, xq + 1]
                return jnp.where(lane >= 96, xh[f], pltpu.roll(main[f, 0], 96, 1))

            def below(f):
                return jnp.where(sub == 0, yh[f, pl.ds(4 + xq, 1), :], pltpu.roll(main[f, xq], 1, 0))

            def above(f):
                return jnp.where(sub == 15, yh[f, pl.ds(8 + xq, 1), :], pltpu.roll(main[f, xq], 15, 0))

            def spot(f):
                return (0, 4 * f + xq) if f < 5 else (f - 4, xq)

            def before(f):
                k, i = spot(f)
                return jnp.where(lane % 32 == 0, pltpu.roll(zh[k, 0], (128 - i) % 128, 1), pltpu.roll(main[f, xq], 1, 1))

            def after(f):
                k, i = spot(f)
                return jnp.where(lane % 32 == 31, pltpu.roll(zh[k, 1], 31 - i, 1), pltpu.roll(main[f, xq], 127, 1))

            out = rate(lambda f: main[f, xq], left, right, below, above, before, after, True)
            for f in range(5):
                rates[m, f * 4 + xq] = out[f]
        return _

    lax.fori_loop(0, 4, node, 0, unroll=2)

    def combine(k, _):
        have = [rates[r, k] for r in range(4)]
        for m, o in enumerate((o0, o1, o2, o3)):
            out = wq_ref[k]
            for r in range(4):
                out = out + weights[m][r] * have[r]
            o[k] = out
        return _

    lax.fori_loop(0, 20, combine, 0, unroll=4)


def last_kernel(r2, r3, r1, r0, out_hbm, quarter, out, sems):
    me = lax.axis_index("node")
    _, lane = iotas()
    def copy(f):
        return pltpu.make_async_copy(out.at[f], out_hbm.at[f], sems.at[f])

    def field(f, _):
        for r, ref in enumerate((r0, r1, r2, r3)):
            quarter[me ^ r, pl.ds(4 * f, 4)] = ref[pl.ds(4 * f, 4)]
        for xq in range(4):
            tiles = swap_blocks([quarter[q, 4 * f + xq] for q in range(4)], 1, 32, lane)
            for g in range(4):
                out[f, 4 * g + xq] = tiles[g]
        copy(f).start()
        return _

    lax.fori_loop(0, 5, field, 0)
    for f in range(5):
        copy(f).wait()


def tiles_of(n):
    return jax.ShapeDtypeStruct((n, 16, 128), jnp.float32)


def shards(start_state, iterate, wall_flags, reg_index):
    state = iterate[0]
    flat = state.reshape(5, 256, 128)
    params = pltpu.CompilerParams(vmem_limit_bytes=32 * 1024 * 1024)
    scratch = lambda *shape: pltpu.VMEM(shape + (16, 128), jnp.float32)
    shape = lambda *dims: jax.ShapeDtypeStruct(dims, jnp.float32)
    dma = lambda n: pltpu.SemaphoreType.DMA((n,))

    def call(kernel, ins, outs, scratch_shapes=(), place=VMEM):
        return pl.pallas_call(
            kernel, out_shape=outs, in_specs=ins, out_specs=[place] * len(outs),
            scratch_shapes=scratch_shapes, compiler_params=params,
            cost_estimate=pl.CostEstimate(flops=1, bytes_accessed=1, transcendentals=0))

    def neighbours(up, down, axis):
        size = lax.axis_size(axis)
        from_lower = lax.ppermute(up, axis, [(i, (i + 1) % size) for i in range(size)])
        from_upper = lax.ppermute(down, axis, [((i + 1) % size, i) for i in range(size)])
        return from_lower, from_upper

    def send(tiles, r):
        return lax.ppermute(tiles, "node", [(i, i ^ r) for i in range(4)])

    far = lambda x: pltpu.with_memory_space_constraint(x, pltpu.HBM)
    slab_near, slab_next, slip = call(
        slab_kernel, [HBM] * 3, [shape(5, 40, 128)] * 2 + [shape(2, 16, 128)],
        [scratch(2, 5), pltpu.VMEM((2, 16, 128), jnp.int32), dma(7)])(
        far(wall_flags), far(state), far(start_state))
    power = jnp.broadcast_to(0.2 + 0.05 * reg_index.astype(jnp.float32), (8, 128))
    slab = neighbours(slab_near, slab_next, "slab")

    m0, m1, m2, m3, rates = call(
        first_kernel, [VMEM, VMEM, ANY], [shape(256, 128)] * 4 + [shape(5, 16, 16, 128)],
        [scratch(3, 16), scratch(4, 20)])(power, state, slip)
    a2, a3, a1 = send(m2, 2), send(m3, 3), send(m1, 1)

    tile = neighbours(*call(tile_kernel, [VMEM] * 2 + [ANY], [tiles_of(13)] * 2)(
        state, start_state, m2), "tile")

    inner, ext = call(
        inner_kernel, [VMEM] * 5, [shape(4, 7, 16, 128), shape(8, 8, 16, 128)])(power, flat, *tile, rates)

    corner = neighbours(*call(corner_kernel, [VMEM] * 3, [shape(16, 128)] * 2)(*slab, slip), "tile")

    e0, e1, e2, e3 = call(
        edge_kernel, [VMEM] * 9 + [ANY] * 2, [tiles_of(EDGE)] * 4,
        [pltpu.VMEM((8, 2, 24, 128), jnp.float32), scratch(8, 2, 4), scratch(4, EDGE)])(
        power, flat, *slab, *corner, slip, inner, ext, a1, a2)
    b2, b3, b1 = send(e2, 2), send(e3, 3), send(e1, 1)

    wq, wz, slipq = call(
        start_kernel, [VMEM, VMEM, ANY], [tiles_of(20), tiles_of(2), shape(16, 128)])(start_state, slip, e2)
    wxy, = call(start_tiles_kernel, [VMEM] * 6 + [ANY], [tiles_of(EDGE)])(*tile, *slab, wq, wz, e2)

    outs = call(
        second_kernel, [VMEM] * 12, [tiles_of(20)] * 4,
        [scratch(8, 4), scratch(8), scratch(8), scratch(3, 2), scratch(4, 20), pltpu.SMEM((16,), jnp.float32)])(
        a2, a3, power, m0, a1, e0, b1, b2, b3, wq, wxy, slipq)
    back = {r: send(outs[r], r) for r in (2, 3, 1)}

    result, = call(
        last_kernel, [VMEM] * 4, [shape(5, 16, 16, 128)], [scratch(4, 20), scratch(5, 16), dma(5)], HBM)(
        back[2], back[3], back[1], outs[0])
    return result[None]


def solution(mesh):
    return jax.shard_map(
        shards,
        mesh=mesh,
        in_specs=(
            P(None, "tile", "slab", None),
            P("node", None, "tile", "slab", None),
            P(None, "tile", None),
            P(),
        ),
        out_specs=P("node", None, "tile", "slab", None),
        check_vma=False,
    )
```

```python
import jax
import jax.numpy as jnp
import numpy as np
from jax import lax
from jax.experimental import pallas as pl
from jax.experimental.pallas import tpu as pltpu
from jax.sharding import PartitionSpec as P

STEP = 0.2
MAIN = 18
EDGE = 12
VMEM = pl.BlockSpec(memory_space=pltpu.VMEM)
SMEM = pl.BlockSpec(memory_space=pltpu.SMEM)
ANY = pl.BlockSpec(memory_space=pl.ANY)
HBM = pl.BlockSpec(memory_space=pltpu.HBM)


def quadrature_table():
    points = [0.25, 0.5, 0.75, 1.0]
    table = np.zeros((4, 4))
    for column in range(4):
        coeffs = [1.0]
        divisor = 1.0
        for other in range(4):
            if other != column:
                other_point = points[other]
                widened = [0.0] * (len(coeffs) + 1)
                for power, value in enumerate(coeffs):
                    widened[power + 1] += value
                    widened[power] -= other_point * value
                coeffs = widened
                divisor *= points[column] - other_point
        for line_index in range(4):
            position = points[line_index]
            total = 0.0
            for power, value in enumerate(coeffs):
                total += value * position ** (power + 1) / (power + 1)
            table[line_index, column] = total / divisor
    return table


def relative_weights(me):
    table = np.asarray(quadrature_table(), np.float32) * np.float32(STEP)

    def entry(a, b):
        value = jnp.float32(table[3 ^ a, 3 ^ b])
        for node in range(3):
            value = jnp.where(me == node, jnp.float32(table[node ^ a, node ^ b]), value)
        return value

    return [[entry(a, b) for b in range(4)] for a in range(4)]


def iotas():
    sub = lax.broadcasted_iota(jnp.int32, (16, 128), 0)
    lane = lax.broadcasted_iota(jnp.int32, (16, 128), 1)
    return sub, lane


def derived(c, g, power):
    r = jnp.exp(power * jnp.log(g * g + 0.25))
    q = c * r
    eta = (0.08 + 0.2 * c + 0.496 * (c * c)) * r
    return q, eta, 0.5 * c * q


def rate(cen, lm, lp, sm, sp, zm, zp, lead_x):
    def diffs(f):
        dl = lp(f) - lm(f)
        ds = sp(f) - sm(f)
        return (dl, ds) if lead_x else (ds, dl)

    def grads(f):
        lo, hi, a, b, n, m = lm(f), lp(f), sm(f), sp(f), zm(f), zp(f)
        x, y = (hi - lo, b - a) if lead_x else (b - a, hi - lo)
        return x, y, m - n, (lo + hi) + (a + b) + (n + m)

    c, g, u, v, w, eta = cen(0), cen(1), cen(2), cen(3), cen(4), cen(6)
    hu, hv, hw = 0.5 * u, 0.5 * v, 0.5 * w
    qx, qy, qz, qsum = grads(5)
    cx, cy, cz, _ = grads(0)
    dc = 0.3 * c * (qsum - 6.0 * cen(5)) + (0.075 * qx - hu) * cx + (0.075 * qy - hv) * cy + (0.075 * qz - hw) * cz
    ex, ey, ez, _ = grads(6)
    ax, ay, az = 0.25 * ex - hu, 0.25 * ey - hv, 0.25 * ez - hw
    ux, uy, uz, usum = grads(2)
    du = eta * (usum - 6.0 * u) + ax * ux + ay * uy + az * uz + 0.5
    vx, vy, vz, vsum = grads(3)
    dv = eta * (vsum - 6.0 * v) + ax * vx + ay * vy + az * vz - 0.5 * diffs(7)[1]
    wx, wy, wz, wsum = grads(4)
    dw = eta * (wsum - 6.0 * w) + ax * wx + ay * wy + az * wz
    strain = uy * uy + wy * wy + vx * vx + vz * vz
    dg = jnp.sqrt(strain + 1.0) - 2.0 * g
    return dc, dg, du, dv, dw


def swap_blocks(tiles, axis, block, index):
    size = 4 * block
    low = index < 2 * block
    even = (index // block) % 2 == 0
    roll = lambda t, k: pltpu.roll(t, k, axis)
    a0, a1, a2, a3 = tiles
    lo0 = jnp.where(low, a0, roll(a2, 2 * block))
    hi0 = jnp.where(low, roll(a0, 2 * block), a2)
    lo1 = jnp.where(low, a1, roll(a3, 2 * block))
    hi1 = jnp.where(low, roll(a1, 2 * block), a3)
    out = []
    for p, q in ((lo0, lo1), (hi0, hi1)):
        out.append(jnp.where(even, p, roll(q, block)))
        out.append(jnp.where(even, roll(p, size - block), q))
    return out


def edges():
    me = lax.axis_index("node")
    t, s = lax.axis_index("tile"), lax.axis_index("slab")
    return me, t == 0, t == lax.axis_size("tile") - 1, s == 0, s == lax.axis_size("slab") - 1


def pick(tiles, me):
    out = tiles[3]
    for q in range(3):
        out = jnp.where(me == q, tiles[q], out)
    return out


def reads(*refs):
    return [lambda *at, ref=ref: ref[at] for ref in refs]


def pack_z_edge(row, sides, lane):
    left = right = jnp.zeros((16, 128), jnp.float32)
    for xq in range(4):
        for f in range(5):
            place = 4 * f + xq
            spot = lane % 32 == place
            tile = row(f, xq)
            left = jnp.where(spot, pltpu.roll(tile, place + 1, 1), left)
            right = jnp.where(spot, pltpu.roll(tile, (place + 96) % 128, 1), right)
    return left, right


def slip_of(flags):
    return 1.0 - 2.0 * flags.astype(jnp.float32)


def tile_kernel(s_ref, w_ref, _after, up_ref, down_ref):
    me = lax.axis_index("node")
    _, lane = iotas()
    for ref, rows, x in ((up_ref, (14, 15), 15), (down_ref, (0, 1), 0)):
        for f in range(5):
            ref[f] = s_ref[f, rows[0]]
            ref[5 + f] = s_ref[f, rows[1]]
        own = [pltpu.roll(w_ref[f, x], (f + 4 - me) % 4 * 32, 1) for f in range(5)]
        ref[10] = jnp.where(lane < 32, own[0], jnp.where(lane < 64, own[1], jnp.where(lane < 96, own[2], own[3])))
        ref[11] = own[4]
        ref[12] = own[4]


def first_kernel(power_ref, s_ref, _after, m0, m1, m2, m3, rates, der, packed):
    me = lax.axis_index("node")
    sub, lane = iotas()
    power = power_ref[0:1, :]

    def derive(k, _):
        x = pl.ds(4 * k, 4)
        der[0, x], der[1, x], der[2, x] = derived(s_ref[0, x], s_ref[1, x], power)
        return _

    lax.fori_loop(0, 4, derive, 0)

    def column(xq, _):
        rows = []
        for g in range(4):
            x = 4 * g + xq
            lo = jnp.maximum(x - 1, 0)
            hi = jnp.minimum(x + 1, 15)
            at = lambda f, r: s_ref[f, r] if f < 5 else der[f - 5, r]
            rows.append(rate(
                lambda f: at(f, x), lambda f: at(f, lo), lambda f: at(f, hi),
                lambda f: pltpu.roll(at(f, x), 1, 0), lambda f: pltpu.roll(at(f, x), 15, 0),
                lambda f: pltpu.roll(at(f, x), 1, 1), lambda f: pltpu.roll(at(f, x), 127, 1), True))
        for f in range(5):
            for g in range(4):
                rates[f, 4 * g + xq] = rows[g][f]
            out = swap_blocks([rows[g][f] for g in range(4)], 1, 32, lane)
            for q in range(4):
                packed[q, f * 4 + xq] = out[q]
        return _

    lax.fori_loop(0, 4, column, 0)
    for r, m in enumerate((m0, m1, m2, m3)):
        q = me ^ r

        def put(k, tile):
            m[pl.ds(14 * k + 1, 14), :] = tile[1:15]

        m[pl.ds(0, 1), :] = jnp.zeros((1, 128), jnp.float32)
        m[pl.ds(14 * MAIN + 1, 3), :] = jnp.zeros((3, 128), jnp.float32)
        for f in range(5):
            for xq in (1, 2):
                put(2 * f + xq - 1, packed[q, f * 4 + xq])
        for p in range(2):
            a0, a3 = packed[q, 8 * p], packed[q, 8 * p + 3]
            b0, b3 = packed[q, 8 * p + 4], packed[q, 8 * p + 7]
            put(10 + 3 * p, jnp.where(lane < 32, b3, a0))
            put(11 + 3 * p, jnp.where(lane >= 96, b0, a3))
            put(12 + 3 * p, jnp.where(
                lane < 32, pltpu.roll(b3, 96, 1), jnp.where(lane < 96, b0, pltpu.roll(b3, 32, 1))))
        put(16, packed[q, 16])
        put(17, packed[q, 19])


def start_kernel(w_ref, slip_ref, _after, wq_ref, wz_ref, slipq_ref):
    me = lax.axis_index("node")
    sub, lane = iotas()
    for xq in range(4):
        for f in range(5):
            own = [w_ref[f, 4 * g + xq] for g in range(4)]
            wq_ref[f * 4 + xq] = pick(swap_blocks(own, 1, 32, lane), me)
    packs = [pack_z_edge(lambda f, xq: w_ref[f, 4 * g + xq], 2, lane) for g in range(4)]
    for side in range(2):
        wz_ref[side] = pick(swap_blocks([packs[g][side] for g in range(4)], 1, 32, lane), me)
    slipq_ref[...] = pack_y_edge(slip_ref[0], slip_ref[1], me, sub, lane)


def pack_y_edge(lower, upper, me, sub, lane):
    zero = jnp.zeros((16, 128), jnp.float32)
    tiles = swap_blocks([zero, lower, upper, zero], 0, 4, sub)
    return pick(swap_blocks(tiles, 1, 32, lane), me)


def slab_kernel(flag_hbm, s_hbm, w_hbm, up_ref, down_ref, slip_ref, rows, flags, sems):
    me = lax.axis_index("node")
    sub, lane = iotas()

    def run(up_ref, down_ref):
        copies = []
        for k, (ref, ys) in enumerate(((up_ref, (14, 15)), (down_ref, (0, 1)))):
            for r in range(2):
                copies.append(pltpu.make_async_copy(
                    s_hbm.at[:, :, ys[r], :], ref.at[:, pl.ds(16 * r, 16), :], sems.at[2 * k + r]))
            copies.append(pltpu.make_async_copy(w_hbm.at[:, :, (15, 0)[k], :], rows.at[k], sems.at[4 + k]))
        copies.append(pltpu.make_async_copy(flag_hbm, flags, sems.at[6]))
        for copy in copies:
            copy.start()
        copies[2].wait()
        copies[5].wait()
        for f in range(5):
            start = pack_y_edge(rows[1, f], rows[0, f], me, sub, lane)
            for ref, place in ((up_ref, 8), (down_ref, 4)):
                ref[f, pl.ds(32, 4), :] = start[place:place + 4]
                ref[f, pl.ds(36, 4), :] = jnp.zeros((4, 128), jnp.float32)
        for k in (0, 1, 3, 4, 6):
            copies[k].wait()

    run(up_ref, down_ref)

    slip_ref[...] = slip_of(flags[...])


def corner_kernel(slow_ref, shigh_ref, slip_ref, up_ref, down_ref):
    below, above = reads(slow_ref, shigh_ref)
    for ref, up in ((up_ref, True), (down_ref, False)):
        for side in range(2):
            ref[pl.ds(10 + side, 1), :] = slip_ref[side, pl.ds(15 if up else 0, 1), :]
        ref[pl.ds(12, 4), :] = jnp.zeros((4, 128), jnp.float32)
        for f in range(5):
            ref[pl.ds(f, 1), :] = ((below(f, pl.ds(31, 1))) if up else below(f, pl.ds(16, 1)))
            ref[pl.ds(5 + f, 1), :] = ((above(f, pl.ds(15, 1))) if up else above(f, pl.ds(0, 1)))


def fill_ext(ext, s_ref, tlow_ref, thigh_ref, t0, t7):
    lo, hi = reads(tlow_ref, thigh_ref)
    for f in range(5):
        first, last = s_ref[f, pl.ds(0, 16), :], s_ref[f, pl.ds(240, 16), :]
        ext[f, 0] = lo(f)
        ext[f, 1] = jnp.where(t0, first, lo(5 + f))
        ext[f, 2] = first
        ext[f, 3] = s_ref[f, pl.ds(16, 16), :]
        ext[f, 4] = s_ref[f, pl.ds(224, 16), :]
        ext[f, 5] = last
        ext[f, 6] = jnp.where(t7, last, hi(f))
        ext[f, 7] = hi(5 + f)


def inner_kernel(power_ref, s_ref, tlow_ref, thigh_ref, rates, out_ref, ext):
    _, t0, t7, _, _ = edges()
    sub, lane = iotas()
    fill_ext(ext, s_ref, tlow_ref, thigh_ref, t0, t7)
    ext[5], ext[6], ext[7] = derived(ext[0], ext[1], power_ref[0:1, :])

    def row(x):
        return rate(
            lambda f: ext[f, x], lambda f: ext[f, x - 1], lambda f: ext[f, x + 1],
            lambda f: pltpu.roll(ext[f, x], 1, 0), lambda f: pltpu.roll(ext[f, x], 15, 0),
            lambda f: pltpu.roll(ext[f, x], 1, 1), lambda f: pltpu.roll(ext[f, x], 127, 1), True)

    first, last = row(2), row(5)
    for f in range(5):
        for q in range(4):
            out_ref[q, f] = jnp.where(
                lane < 32, pltpu.roll(first[f], 32 * (4 - q) % 128, 1), pltpu.roll(last[f], 32 * (3 - q), 1))

    def at(g):
        def tile(f, xq):
            return first[f] if g + xq == 0 else last[f] if g + xq == 6 else rates[f, 4 * g + xq]

        return tile

    packs = [pack_z_edge(at(g), 2, lane) for g in range(4)]
    for side in range(2):
        out = swap_blocks([packs[g][side] for g in range(4)], 1, 32, lane)
        for q in range(4):
            out_ref[q, 5 + side] = out[q]


def edge_kernel(power_ref, s_ref, slow_ref, shigh_ref, clow_ref, chigh_ref, slip_ref,
                inner_ref, ext, e0, e1, e2, e3, yh, band, edge):
    me, t0, t7, s0, s7 = edges()
    sub, lane = iotas()
    power = power_ref[0:1, :]
    corner_lo, corner_hi = reads(clow_ref, chigh_ref)
    below_row, above_row = reads(slow_ref, shigh_ref)

    for side in range(2):
        ref = (below_row, above_row)[side]
        near, far = ((16, 0), (0, 16))[side]
        y, inward = ((0, 1), (15, 14))[side]
        wall = (s0, s7)[side]
        slip = slip_ref[side]
        slip_lo = corner_lo(pl.ds(10 + side, 1))
        slip_hi = corner_hi(pl.ds(10 + side, 1))
        for f in range(5):
            def ghost(value, flag):
                return -value if f == 3 else value * flag if f in (2, 4) else value

            mine = s_ref[f, pl.ds(y, 16, stride=16), :]
            yh[f, side, pl.ds(0, 16), :] = jnp.where(wall, ghost(mine, slip), ref(f, pl.ds(near, 16)))
            yh[f, side, pl.ds(16, 1), :] = jnp.where(
                wall, ghost(ext[f, 1, pl.ds(y, 1), :], slip_lo),
                jnp.where(t0, ref(f, pl.ds(near, 1)), corner_lo(pl.ds(5 * side + f, 1))))
            yh[f, side, pl.ds(17, 1), :] = jnp.where(
                wall, ghost(ext[f, 6, pl.ds(y, 1), :], slip_hi),
                jnp.where(t7, ref(f, pl.ds(near + 15, 1)), corner_hi(pl.ds(5 * side + f, 1))))
            yh[f, side, pl.ds(18, 6), :] = jnp.zeros((6, 128), jnp.float32)
            band[f, side, 0] = ref(f, pl.ds(far, 16))
            band[f, side, 1] = ref(f, pl.ds(near, 16))
            band[f, side, 2] = mine
            band[f, side, 3] = s_ref[f, pl.ds(inward, 16, stride=16), :]
        yh[5, side], yh[6, side], yh[7, side] = derived(yh[0, side], yh[1, side], power)
        band[5, side], band[6, side], band[7, side] = derived(band[0, side], band[1, side], power)

    def row(x, place):
        def below(f):
            return jnp.where(sub == 0, yh[f, 0, pl.ds(place, 1), :], pltpu.roll(ext[f, x], 1, 0))

        def above(f):
            return jnp.where(sub == 15, yh[f, 1, pl.ds(place, 1), :], pltpu.roll(ext[f, x], 15, 0))

        return rate(
            lambda f: ext[f, x], lambda f: ext[f, x - 1], lambda f: ext[f, x + 1], below, above,
            lambda f: pltpu.roll(ext[f, x], 1, 1), lambda f: pltpu.roll(ext[f, x], 127, 1), True)

    lower, upper = row(1, 16), row(6, 17)
    for f in range(5):
        for q in range(4):
            edge[q, f] = jnp.where(
                jnp.logical_or(lane < 32, lane >= 96), inner_ref[q, f],
                jnp.where(lane < 64, pltpu.roll(lower[f], (32 * (1 - q)) % 128, 1),
                          pltpu.roll(upper[f], (32 * (2 - q)) % 128, 1)))

    def band_rate(side, k):
        y = 0 if side == 0 else 15
        left = (lambda f: yh[f, side, pl.ds(16, 1), :]) if k == 1 else (lambda f: ext[f, 1, pl.ds(y, 1), :])
        right = (lambda f: yh[f, side, pl.ds(17, 1), :]) if k == 1 else (lambda f: ext[f, 6, pl.ds(y, 1), :])

        def before_x(f):
            return jnp.where(sub == 0, left(f), pltpu.roll(band[f, side, k], 1, 0))

        def after_x(f):
            return jnp.where(sub == 15, right(f), pltpu.roll(band[f, side, k], 15, 0))

        outer = (lambda f: band[f, side, 0]) if k == 1 else (lambda f: yh[f, side, pl.ds(0, 16), :])
        inner = lambda f: band[f, side, k + 1]
        before, after = (outer, inner) if side == 0 else (inner, outer)
        return rate(
            lambda f: band[f, side, k], before, after, before_x, after_x,
            lambda f: pltpu.roll(band[f, side, k], 1, 1), lambda f: pltpu.roll(band[f, side, k], 127, 1), False)

    rows = [band_rate(0, 2), band_rate(0, 1), band_rate(1, 1), band_rate(1, 2)]
    zero = jnp.zeros((16, 128), jnp.float32)
    beside = [[zero, zero] for q in range(4)]
    for f in range(5):
        out = swap_blocks(swap_blocks([r[f] for r in rows], 0, 4, sub), 1, 32, lane)
        for q in range(4):
            edge[q, 5 + f] = out[q]
            for xq in range(4):
                place = 4 * f + xq
                spot = jnp.logical_and(lane % 32 == place, sub % 4 == xq)
                for side, to, shift in ((0, (q + 1) % 4, (place + 97) % 128), (1, (q + 3) % 4, place)):
                    beside[to][side] = jnp.where(spot, pltpu.roll(out[q], shift, 1), beside[to][side])
    for q in range(4):
        for side in range(2):
            b = beside[q][side]
            low = b + pltpu.roll(b, 15, 0)
            low = low + pltpu.roll(low, 14, 0)
            high = b + pltpu.roll(b, 1, 0)
            high = high + pltpu.roll(high, 2, 0)
            edge[q, 10 + side] = jnp.where(sub == 0, low, jnp.where(sub == 15, high, inner_ref[q, 5 + side]))
    for r, e in enumerate((e0, e1, e2, e3)):
        e[...] = edge[me ^ r]


def start_tiles_kernel(tlow_ref, thigh_ref, slow_ref, shigh_ref, wq_ref, wz_ref, _after, wxy_ref):
    me = lax.axis_index("node")
    sub, lane = iotas()
    lo, hi = reads(tlow_ref, thigh_ref)
    below, above = reads(slow_ref, shigh_ref)
    for f in range(5):
        a = pltpu.roll(lo(10 + f // 4), (5 - f % 4) % 4 * 32, 1)
        b = pltpu.roll(hi(10 + f // 4), (6 - f % 4) % 4 * 32, 1)
        wxy_ref[f] = jnp.where(
            lane < 32, wq_ref[f * 4], jnp.where(lane < 64, a, jnp.where(lane < 96, b, wq_ref[f * 4 + 3])))
        wxy_ref[5 + f, pl.ds(4, 4), :] = below(f, pl.ds(32, 4))
        wxy_ref[5 + f, pl.ds(8, 4), :] = above(f, pl.ds(32, 4))
        for xq in range(4):
            wxy_ref[5 + f, pl.ds(xq, 1), :] = wq_ref[f * 4 + xq, pl.ds(0, 1), :]
            wxy_ref[5 + f, pl.ds(12 + xq, 1), :] = wq_ref[f * 4 + xq, pl.ds(15, 1), :]
    for side in range(2):
        wxy_ref[10 + side] = wz_ref[side]


def second_kernel(a2, a3, power_ref, a0, a1, b0, b1, b2, b3, wq_ref, wxy_ref, slipq_ref,
                  o0, o1, o2, o3, main, xh, yh, zh, rates, table):
    me, t0, t7, s0, s7 = edges()
    sub, lane = iotas()
    power = power_ref[0:1, :]
    slip = slipq_ref[...]
    at_lower = jnp.logical_and(jnp.logical_and(sub >= 4, sub < 8), s0)
    at_upper = jnp.logical_and(jnp.logical_and(sub >= 8, sub < 12), s7)
    arrived, edge = (a0, a1, a2, a3), (b0, b1, b2, b3)
    weights = relative_weights(me)
    for m in range(4):
        for r in range(4):
            table[m * 4 + r] = weights[m][r]

    def node(m, _):
        weight = [table[m * 4 + r] for r in range(4)]

        def mix(refs, k):
            out = None
            for r, ref in enumerate(refs):
                term = weight[r] * (ref[pl.ds(14 * k, 16), :] if refs is arrived else ref[k])
                out = term if out is None else out + term
            return out

        outer = {}
        for p in range(2):
            a0, a3, b = (mix(arrived, 10 + 3 * p + k) for k in range(3))
            outer[2 * p] = a0, a3
            outer[2 * p + 1] = jnp.where(lane < 96, b, a3), jnp.where(
                lane < 32, a0, jnp.where(lane < 64, pltpu.roll(b, 32, 1), pltpu.roll(b, 96, 1)))
        outer[4] = mix(arrived, 16), mix(arrived, 17)

        for f in range(5):
            xb = wxy_ref[f] + mix(edge, f)
            yb = wxy_ref[5 + f] + mix(edge, 5 + f)
            yh[f] = yb
            for xq in range(4):
                tile = wq_ref[f * 4 + xq] + (mix(arrived, 2 * f + xq - 1) if xq in (1, 2) else outer[f][xq // 3])
                if xq == 0:
                    tile = jnp.where(lane < 32, xb, tile)
                if xq == 3:
                    tile = jnp.where(lane >= 96, xb, tile)
                tile = jnp.where(sub == 0, yh[f, pl.ds(xq, 1), :], tile)
                tile = jnp.where(sub == 15, yh[f, pl.ds(12 + xq, 1), :], tile)
                main[f, xq] = tile
            xh[f] = jnp.where(
                lane < 64, jnp.where(t0, main[f, 0], pltpu.roll(xb, 96, 1)),
                jnp.where(t7, main[f, 3], pltpu.roll(xb, 32, 1)))
            lower, upper = pltpu.roll(yb, 4, 0), pltpu.roll(yb, 12, 0)
            if f == 3:
                lower, upper = -lower, -upper
            if f in (2, 4):
                lower, upper = lower * slip, upper * slip
            yh[f] = jnp.where(at_lower, lower, jnp.where(at_upper, upper, yb))
        for xq in range(4):
            main[5, xq], main[6, xq], main[7, xq] = derived(main[0, xq], main[1, xq], power)
        xh[5], xh[6], xh[7] = derived(xh[0], xh[1], power)
        yh[5], yh[6], yh[7] = derived(yh[0], yh[1], power)
        for side in range(2):
            z = wxy_ref[10 + side] + mix(edge, 10 + side)
            zh[0, side] = z
            q, eta, _s = derived(z, pltpu.roll(z, 124, 1), power)
            zh[1, side], zh[2, side] = q, eta
        for xq in range(4):
            def left(f):
                if xq > 0:
                    return main[f, xq - 1]
                return jnp.where(lane < 32, xh[f], pltpu.roll(main[f, 3], 32, 1))

            def right(f):
                if xq < 3:
                    return main[f, xq + 1]
                return jnp.where(lane >= 96, xh[f], pltpu.roll(main[f, 0], 96, 1))

            def below(f):
                return jnp.where(sub == 0, yh[f, pl.ds(4 + xq, 1), :], pltpu.roll(main[f, xq], 1, 0))

            def above(f):
                return jnp.where(sub == 15, yh[f, pl.ds(8 + xq, 1), :], pltpu.roll(main[f, xq], 15, 0))

            def spot(f):
                return (0, 4 * f + xq) if f < 5 else (f - 4, xq)

            def before(f):
                k, i = spot(f)
                return jnp.where(lane % 32 == 0, pltpu.roll(zh[k, 0], (128 - i) % 128, 1), pltpu.roll(main[f, xq], 1, 1))

            def after(f):
                k, i = spot(f)
                return jnp.where(lane % 32 == 31, pltpu.roll(zh[k, 1], 31 - i, 1), pltpu.roll(main[f, xq], 127, 1))

            out = rate(lambda f: main[f, xq], left, right, below, above, before, after, True)
            for f in range(5):
                rates[m, f * 4 + xq] = out[f]
        return _

    lax.fori_loop(0, 4, node, 0, unroll=2)

    def combine(k, _):
        have = [rates[r, k] for r in range(4)]
        for m, o in enumerate((o0, o1, o2, o3)):
            out = wq_ref[k]
            for r in range(4):
                out = out + weights[m][r] * have[r]
            o[k] = out
        return _

    lax.fori_loop(0, 20, combine, 0, unroll=4)


def last_kernel(r2, r3, r1, r0, out_hbm, quarter, out, sems):
    me = lax.axis_index("node")
    _, lane = iotas()
    def copy(f):
        return pltpu.make_async_copy(out.at[f], out_hbm.at[f], sems.at[f])

    def field(f, _):
        for r, ref in enumerate((r0, r1, r2, r3)):
            quarter[me ^ r, pl.ds(4 * f, 4)] = ref[pl.ds(4 * f, 4)]
        for xq in range(4):
            tiles = swap_blocks([quarter[q, 4 * f + xq] for q in range(4)], 1, 32, lane)
            for g in range(4):
                out[f, 4 * g + xq] = tiles[g]
        copy(f).start()
        return _

    lax.fori_loop(0, 5, field, 0)
    for f in range(5):
        copy(f).wait()


def tiles_of(n):
    return jax.ShapeDtypeStruct((n, 16, 128), jnp.float32)


def shards(start_state, iterate, wall_flags, reg_index):
    state = iterate[0]
    flat = state.reshape(5, 256, 128)
    params = pltpu.CompilerParams(vmem_limit_bytes=32 * 1024 * 1024)
    scratch = lambda *shape: pltpu.VMEM(shape + (16, 128), jnp.float32)
    shape = lambda *dims: jax.ShapeDtypeStruct(dims, jnp.float32)
    dma = lambda n: pltpu.SemaphoreType.DMA((n,))

    def call(kernel, ins, outs, scratch_shapes=(), place=VMEM):
        return pl.pallas_call(
            kernel, out_shape=outs, in_specs=ins, out_specs=[place] * len(outs),
            scratch_shapes=scratch_shapes, compiler_params=params,
            cost_estimate=pl.CostEstimate(flops=1, bytes_accessed=1, transcendentals=0))

    def neighbours(up, down, axis):
        size = lax.axis_size(axis)
        from_lower = lax.ppermute(up, axis, [(i, (i + 1) % size) for i in range(size)])
        from_upper = lax.ppermute(down, axis, [((i + 1) % size, i) for i in range(size)])
        return from_lower, from_upper

    def send(tiles, r):
        return lax.ppermute(tiles, "node", [(i, i ^ r) for i in range(4)])

    far = lambda x: pltpu.with_memory_space_constraint(x, pltpu.HBM)
    slab_near, slab_next, slip = call(
        slab_kernel, [HBM] * 3, [shape(5, 40, 128)] * 2 + [shape(2, 16, 128)],
        [scratch(2, 5), pltpu.VMEM((2, 16, 128), jnp.int32), dma(7)])(
        far(wall_flags), far(state), far(start_state))
    power = jnp.broadcast_to(0.2 + 0.05 * reg_index.astype(jnp.float32), (8, 128))
    slab = neighbours(slab_near, slab_next, "slab")

    m0, m1, m2, m3, rates = call(
        first_kernel, [VMEM, VMEM, ANY], [shape(256, 128)] * 4 + [shape(5, 16, 16, 128)],
        [scratch(3, 16), scratch(4, 20)])(power, state, slip)
    a2, a3, a1 = send(m2, 2), send(m3, 3), send(m1, 1)

    tile = neighbours(*call(tile_kernel, [VMEM] * 2 + [ANY], [tiles_of(13)] * 2)(
        state, start_state, m2), "tile")

    inner, ext = call(
        inner_kernel, [VMEM] * 5, [shape(4, 7, 16, 128), shape(8, 8, 16, 128)])(power, flat, *tile, rates)

    corner = neighbours(*call(corner_kernel, [VMEM] * 3, [shape(16, 128)] * 2)(*slab, slip), "tile")

    e0, e1, e2, e3 = call(
        edge_kernel, [VMEM] * 9, [tiles_of(EDGE)] * 4,
        [pltpu.VMEM((8, 2, 24, 128), jnp.float32), scratch(8, 2, 4), scratch(4, EDGE)])(
        power, flat, *slab, *corner, slip, inner, ext)
    b2, b3, b1 = send(e2, 2), send(e3, 3), send(e1, 1)

    wq, wz, slipq = call(
        start_kernel, [VMEM, VMEM, ANY], [tiles_of(20), tiles_of(2), shape(16, 128)])(start_state, slip, e2)
    wxy, = call(start_tiles_kernel, [VMEM] * 6 + [ANY], [tiles_of(EDGE)])(*tile, *slab, wq, wz, e2)

    outs = call(
        second_kernel, [VMEM] * 12, [tiles_of(20)] * 4,
        [scratch(8, 4), scratch(8), scratch(8), scratch(3, 2), scratch(4, 20), pltpu.SMEM((16,), jnp.float32)])(
        a2, a3, power, m0, a1, e0, b1, b2, b3, wq, wxy, slipq)
    back = {r: send(outs[r], r) for r in (2, 3, 1)}

    result, = call(
        last_kernel, [VMEM] * 4, [shape(5, 16, 16, 128)], [scratch(4, 20), scratch(5, 16), dma(5)], HBM)(
        back[2], back[3], back[1], outs[0])
    return result[None]


def solution(mesh):
    return jax.shard_map(
        shards,
        mesh=mesh,
        in_specs=(
            P(None, "tile", "slab", None),
            P("node", None, "tile", "slab", None),
            P(None, "tile", None),
            P(),
        ),
        out_specs=P("node", None, "tile", "slab", None),
        check_vma=False,
    )
```

```python
import jax
import jax.numpy as jnp
import numpy as np
from jax import lax
from jax.experimental import pallas as pl
from jax.experimental.pallas import tpu as pltpu
from jax.sharding import PartitionSpec as P

STEP = 0.2
MAIN = 18
EDGE = 12
VMEM = pl.BlockSpec(memory_space=pltpu.VMEM)
SMEM = pl.BlockSpec(memory_space=pltpu.SMEM)
ANY = pl.BlockSpec(memory_space=pl.ANY)
HBM = pl.BlockSpec(memory_space=pltpu.HBM)


def quadrature_table():
    points = [0.25, 0.5, 0.75, 1.0]
    table = np.zeros((4, 4))
    for column in range(4):
        coeffs = [1.0]
        divisor = 1.0
        for other in range(4):
            if other != column:
                other_point = points[other]
                widened = [0.0] * (len(coeffs) + 1)
                for power, value in enumerate(coeffs):
                    widened[power + 1] += value
                    widened[power] -= other_point * value
                coeffs = widened
                divisor *= points[column] - other_point
        for line_index in range(4):
            position = points[line_index]
            total = 0.0
            for power, value in enumerate(coeffs):
                total += value * position ** (power + 1) / (power + 1)
            table[line_index, column] = total / divisor
    return table


def relative_weights(me):
    table = np.asarray(quadrature_table(), np.float32) * np.float32(STEP)

    def entry(a, b):
        value = jnp.float32(table[3 ^ a, 3 ^ b])
        for node in range(3):
            value = jnp.where(me == node, jnp.float32(table[node ^ a, node ^ b]), value)
        return value

    return [[entry(a, b) for b in range(4)] for a in range(4)]


def iotas():
    sub = lax.broadcasted_iota(jnp.int32, (16, 128), 0)
    lane = lax.broadcasted_iota(jnp.int32, (16, 128), 1)
    return sub, lane


def derived(c, g, power):
    r = jnp.exp(power * jnp.log(g * g + 0.25))
    q = c * r
    eta = (0.08 + 0.2 * c + 0.496 * (c * c)) * r
    return q, eta, 0.5 * c * q


def rate(cen, lm, lp, sm, sp, zm, zp, lead_x):
    def diffs(f):
        dl = lp(f) - lm(f)
        ds = sp(f) - sm(f)
        return (dl, ds) if lead_x else (ds, dl)

    def grads(f):
        lo, hi, a, b, n, m = lm(f), lp(f), sm(f), sp(f), zm(f), zp(f)
        x, y = (hi - lo, b - a) if lead_x else (b - a, hi - lo)
        return x, y, m - n, (lo + hi) + (a + b) + (n + m)

    c, g, u, v, w, eta = cen(0), cen(1), cen(2), cen(3), cen(4), cen(6)
    hu, hv, hw = 0.5 * u, 0.5 * v, 0.5 * w
    qx, qy, qz, qsum = grads(5)
    cx, cy, cz, _ = grads(0)
    dc = 0.3 * c * (qsum - 6.0 * cen(5)) + (0.075 * qx - hu) * cx + (0.075 * qy - hv) * cy + (0.075 * qz - hw) * cz
    ex, ey, ez, _ = grads(6)
    ax, ay, az = 0.25 * ex - hu, 0.25 * ey - hv, 0.25 * ez - hw
    ux, uy, uz, usum = grads(2)
    du = eta * (usum - 6.0 * u) + ax * ux + ay * uy + az * uz + 0.5
    vx, vy, vz, vsum = grads(3)
    dv = eta * (vsum - 6.0 * v) + ax * vx + ay * vy + az * vz - 0.5 * diffs(7)[1]
    wx, wy, wz, wsum = grads(4)
    dw = eta * (wsum - 6.0 * w) + ax * wx + ay * wy + az * wz
    strain = uy * uy + wy * wy + vx * vx + vz * vz
    dg = jnp.sqrt(strain + 1.0) - 2.0 * g
    return dc, dg, du, dv, dw


def swap_blocks(tiles, axis, block, index):
    size = 4 * block
    low = index < 2 * block
    even = (index // block) % 2 == 0
    roll = lambda t, k: pltpu.roll(t, k, axis)
    a0, a1, a2, a3 = tiles
    lo0 = jnp.where(low, a0, roll(a2, 2 * block))
    hi0 = jnp.where(low, roll(a0, 2 * block), a2)
    lo1 = jnp.where(low, a1, roll(a3, 2 * block))
    hi1 = jnp.where(low, roll(a1, 2 * block), a3)
    out = []
    for p, q in ((lo0, lo1), (hi0, hi1)):
        out.append(jnp.where(even, p, roll(q, block)))
        out.append(jnp.where(even, roll(p, size - block), q))
    return out


def edges():
    me = lax.axis_index("node")
    t, s = lax.axis_index("tile"), lax.axis_index("slab")
    return me, t == 0, t == lax.axis_size("tile") - 1, s == 0, s == lax.axis_size("slab") - 1


def pick(tiles, me):
    out = tiles[3]
    for q in range(3):
        out = jnp.where(me == q, tiles[q], out)
    return out


def reads(*refs):
    return [lambda *at, ref=ref: ref[at] for ref in refs]


def pack_z_edge(row, sides, lane):
    left = right = jnp.zeros((16, 128), jnp.float32)
    for xq in range(4):
        for f in range(5):
            place = 4 * f + xq
            spot = lane % 32 == place
            tile = row(f, xq)
            left = jnp.where(spot, pltpu.roll(tile, place + 1, 1), left)
            right = jnp.where(spot, pltpu.roll(tile, (place + 96) % 128, 1), right)
    return left, right


def slip_of(flags):
    return 1.0 - 2.0 * flags.astype(jnp.float32)


def tile_kernel(s_ref, w_ref, _after, up_ref, down_ref):
    me = lax.axis_index("node")
    _, lane = iotas()
    for ref, rows, x in ((up_ref, (14, 15), 15), (down_ref, (0, 1), 0)):
        for f in range(5):
            ref[f] = s_ref[f, rows[0]]
            ref[5 + f] = s_ref[f, rows[1]]
        own = [pltpu.roll(w_ref[f, x], (f + 4 - me) % 4 * 32, 1) for f in range(5)]
        ref[10] = jnp.where(lane < 32, own[0], jnp.where(lane < 64, own[1], jnp.where(lane < 96, own[2], own[3])))
        ref[11] = own[4]
        ref[12] = own[4]


def first_kernel(power_ref, s_ref, _after, m0, m1, m2, m3, rates, der, packed):
    me = lax.axis_index("node")
    sub, lane = iotas()
    power = power_ref[0:1, :]

    def derive(k, _):
        x = pl.ds(4 * k, 4)
        der[0, x], der[1, x], der[2, x] = derived(s_ref[0, x], s_ref[1, x], power)
        return _

    lax.fori_loop(0, 4, derive, 0)

    def column(xq, _):
        rows = []
        for g in range(4):
            x = 4 * g + xq
            lo = jnp.maximum(x - 1, 0)
            hi = jnp.minimum(x + 1, 15)
            at = lambda f, r: s_ref[f, r] if f < 5 else der[f - 5, r]
            rows.append(rate(
                lambda f: at(f, x), lambda f: at(f, lo), lambda f: at(f, hi),
                lambda f: pltpu.roll(at(f, x), 1, 0), lambda f: pltpu.roll(at(f, x), 15, 0),
                lambda f: pltpu.roll(at(f, x), 1, 1), lambda f: pltpu.roll(at(f, x), 127, 1), True))
        for f in range(5):
            for g in range(4):
                rates[f, 4 * g + xq] = rows[g][f]
            out = swap_blocks([rows[g][f] for g in range(4)], 1, 32, lane)
            for q in range(4):
                packed[q, f * 4 + xq] = out[q]
        return _

    lax.fori_loop(0, 4, column, 0)
    for r, m in enumerate((m0, m1, m2, m3)):
        q = me ^ r

        def put(k, tile):
            m[pl.ds(14 * k + 1, 14), :] = tile[1:15]

        m[pl.ds(0, 1), :] = jnp.zeros((1, 128), jnp.float32)
        m[pl.ds(14 * MAIN + 1, 3), :] = jnp.zeros((3, 128), jnp.float32)
        for f in range(5):
            for xq in (1, 2):
                put(2 * f + xq - 1, packed[q, f * 4 + xq])
        for p in range(2):
            a0, a3 = packed[q, 8 * p], packed[q, 8 * p + 3]
            b0, b3 = packed[q, 8 * p + 4], packed[q, 8 * p + 7]
            put(10 + 3 * p, jnp.where(lane < 32, b3, a0))
            put(11 + 3 * p, jnp.where(lane >= 96, b0, a3))
            put(12 + 3 * p, jnp.where(
                lane < 32, pltpu.roll(b3, 96, 1), jnp.where(lane < 96, b0, pltpu.roll(b3, 32, 1))))
        put(16, packed[q, 16])
        put(17, packed[q, 19])


def start_kernel(w_ref, slip_ref, _after, wq_ref, wz_ref, slipq_ref):
    me = lax.axis_index("node")
    sub, lane = iotas()
    for xq in range(4):
        for f in range(5):
            own = [w_ref[f, 4 * g + xq] for g in range(4)]
            wq_ref[f * 4 + xq] = pick(swap_blocks(own, 1, 32, lane), me)
    packs = [pack_z_edge(lambda f, xq: w_ref[f, 4 * g + xq], 2, lane) for g in range(4)]
    for side in range(2):
        wz_ref[side] = pick(swap_blocks([packs[g][side] for g in range(4)], 1, 32, lane), me)
    slipq_ref[...] = pack_y_edge(slip_ref[0], slip_ref[1], me, sub, lane)


def pack_y_edge(lower, upper, me, sub, lane):
    zero = jnp.zeros((16, 128), jnp.float32)
    tiles = swap_blocks([zero, lower, upper, zero], 0, 4, sub)
    return pick(swap_blocks(tiles, 1, 32, lane), me)


def slab_kernel(flag_hbm, s_hbm, w_hbm, up_ref, down_ref, slip_ref, rows, flags, sems):
    me = lax.axis_index("node")
    sub, lane = iotas()

    def run(up_ref, down_ref):
        copies = []
        for k, (ref, ys) in enumerate(((up_ref, (14, 15)), (down_ref, (0, 1)))):
            for r in range(2):
                copies.append(pltpu.make_async_copy(
                    s_hbm.at[:, :, ys[r], :], ref.at[:, pl.ds(16 * r, 16), :], sems.at[2 * k + r]))
            copies.append(pltpu.make_async_copy(w_hbm.at[:, :, (15, 0)[k], :], rows.at[k], sems.at[4 + k]))
        copies.append(pltpu.make_async_copy(flag_hbm, flags, sems.at[6]))
        for copy in copies:
            copy.start()
        copies[2].wait()
        copies[5].wait()
        for f in range(5):
            start = pack_y_edge(rows[1, f], rows[0, f], me, sub, lane)
            for ref, place in ((up_ref, 8), (down_ref, 4)):
                ref[f, pl.ds(32, 4), :] = start[place:place + 4]
                ref[f, pl.ds(36, 4), :] = jnp.zeros((4, 128), jnp.float32)
        for k in (0, 1, 3, 4, 6):
            copies[k].wait()

    run(up_ref, down_ref)

    slip_ref[...] = slip_of(flags[...])


def corner_kernel(slow_ref, shigh_ref, slip_ref, up_ref, down_ref):
    below, above = reads(slow_ref, shigh_ref)
    for ref, up in ((up_ref, True), (down_ref, False)):
        for side in range(2):
            ref[pl.ds(10 + side, 1), :] = slip_ref[side, pl.ds(15 if up else 0, 1), :]
        ref[pl.ds(12, 4), :] = jnp.zeros((4, 128), jnp.float32)
        for f in range(5):
            ref[pl.ds(f, 1), :] = ((below(f, pl.ds(31, 1))) if up else below(f, pl.ds(16, 1)))
            ref[pl.ds(5 + f, 1), :] = ((above(f, pl.ds(15, 1))) if up else above(f, pl.ds(0, 1)))


def fill_ext(ext, s_ref, tlow_ref, thigh_ref, t0, t7):
    lo, hi = reads(tlow_ref, thigh_ref)
    for f in range(5):
        first, last = s_ref[f, pl.ds(0, 16), :], s_ref[f, pl.ds(240, 16), :]
        ext[f, 0] = lo(f)
        ext[f, 1] = jnp.where(t0, first, lo(5 + f))
        ext[f, 2] = first
        ext[f, 3] = s_ref[f, pl.ds(16, 16), :]
        ext[f, 4] = s_ref[f, pl.ds(224, 16), :]
        ext[f, 5] = last
        ext[f, 6] = jnp.where(t7, last, hi(f))
        ext[f, 7] = hi(5 + f)


def inner_kernel(power_ref, s_ref, tlow_ref, thigh_ref, rates, out_ref, ext):
    _, t0, t7, _, _ = edges()
    sub, lane = iotas()
    fill_ext(ext, s_ref, tlow_ref, thigh_ref, t0, t7)
    ext[5], ext[6], ext[7] = derived(ext[0], ext[1], power_ref[0:1, :])

    def row(x):
        return rate(
            lambda f: ext[f, x], lambda f: ext[f, x - 1], lambda f: ext[f, x + 1],
            lambda f: pltpu.roll(ext[f, x], 1, 0), lambda f: pltpu.roll(ext[f, x], 15, 0),
            lambda f: pltpu.roll(ext[f, x], 1, 1), lambda f: pltpu.roll(ext[f, x], 127, 1), True)

    first, last = row(2), row(5)
    for f in range(5):
        for q in range(4):
            out_ref[q, f] = jnp.where(
                lane < 32, pltpu.roll(first[f], 32 * (4 - q) % 128, 1), pltpu.roll(last[f], 32 * (3 - q), 1))

    def at(g):
        def tile(f, xq):
            return first[f] if g + xq == 0 else last[f] if g + xq == 6 else rates[f, 4 * g + xq]

        return tile

    packs = [pack_z_edge(at(g), 2, lane) for g in range(4)]
    for side in range(2):
        out = swap_blocks([packs[g][side] for g in range(4)], 1, 32, lane)
        for q in range(4):
            out_ref[q, 5 + side] = out[q]


def edge_kernel(power_ref, s_ref, slow_ref, shigh_ref, clow_ref, chigh_ref, slip_ref,
                inner_ref, ext, e0, e1, e2, e3, yh, band, edge):
    me, t0, t7, s0, s7 = edges()
    sub, lane = iotas()
    power = power_ref[0:1, :]
    corner_lo, corner_hi = reads(clow_ref, chigh_ref)
    below_row, above_row = reads(slow_ref, shigh_ref)

    for side in range(2):
        ref = (below_row, above_row)[side]
        near, far = ((16, 0), (0, 16))[side]
        y, inward = ((0, 1), (15, 14))[side]
        wall = (s0, s7)[side]
        slip = slip_ref[side]
        slip_lo = corner_lo(pl.ds(10 + side, 1))
        slip_hi = corner_hi(pl.ds(10 + side, 1))
        for f in range(5):
            def ghost(value, flag):
                return -value if f == 3 else value * flag if f in (2, 4) else value

            mine = s_ref[f, pl.ds(y, 16, stride=16), :]
            yh[f, side, pl.ds(0, 16), :] = jnp.where(wall, ghost(mine, slip), ref(f, pl.ds(near, 16)))
            yh[f, side, pl.ds(16, 1), :] = jnp.where(
                wall, ghost(ext[f, 1, pl.ds(y, 1), :], slip_lo),
                jnp.where(t0, ref(f, pl.ds(near, 1)), corner_lo(pl.ds(5 * side + f, 1))))
            yh[f, side, pl.ds(17, 1), :] = jnp.where(
                wall, ghost(ext[f, 6, pl.ds(y, 1), :], slip_hi),
                jnp.where(t7, ref(f, pl.ds(near + 15, 1)), corner_hi(pl.ds(5 * side + f, 1))))
            yh[f, side, pl.ds(18, 6), :] = jnp.zeros((6, 128), jnp.float32)
            band[f, side, 0] = ref(f, pl.ds(far, 16))
            band[f, side, 1] = ref(f, pl.ds(near, 16))
            band[f, side, 2] = mine
            band[f, side, 3] = s_ref[f, pl.ds(inward, 16, stride=16), :]
        yh[5, side], yh[6, side], yh[7, side] = derived(yh[0, side], yh[1, side], power)
        band[5, side], band[6, side], band[7, side] = derived(band[0, side], band[1, side], power)

    def row(x, place):
        def below(f):
            return jnp.where(sub == 0, yh[f, 0, pl.ds(place, 1), :], pltpu.roll(ext[f, x], 1, 0))

        def above(f):
            return jnp.where(sub == 15, yh[f, 1, pl.ds(place, 1), :], pltpu.roll(ext[f, x], 15, 0))

        return rate(
            lambda f: ext[f, x], lambda f: ext[f, x - 1], lambda f: ext[f, x + 1], below, above,
            lambda f: pltpu.roll(ext[f, x], 1, 1), lambda f: pltpu.roll(ext[f, x], 127, 1), True)

    lower, upper = row(1, 16), row(6, 17)
    for f in range(5):
        for q in range(4):
            edge[q, f] = jnp.where(
                jnp.logical_or(lane < 32, lane >= 96), inner_ref[q, f],
                jnp.where(lane < 64, pltpu.roll(lower[f], (32 * (1 - q)) % 128, 1),
                          pltpu.roll(upper[f], (32 * (2 - q)) % 128, 1)))

    def band_rate(side, k):
        y = 0 if side == 0 else 15
        left = (lambda f: yh[f, side, pl.ds(16, 1), :]) if k == 1 else (lambda f: ext[f, 1, pl.ds(y, 1), :])
        right = (lambda f: yh[f, side, pl.ds(17, 1), :]) if k == 1 else (lambda f: ext[f, 6, pl.ds(y, 1), :])

        def before_x(f):
            return jnp.where(sub == 0, left(f), pltpu.roll(band[f, side, k], 1, 0))

        def after_x(f):
            return jnp.where(sub == 15, right(f), pltpu.roll(band[f, side, k], 15, 0))

        outer = (lambda f: band[f, side, 0]) if k == 1 else (lambda f: yh[f, side, pl.ds(0, 16), :])
        inner = lambda f: band[f, side, k + 1]
        before, after = (outer, inner) if side == 0 else (inner, outer)
        return rate(
            lambda f: band[f, side, k], before, after, before_x, after_x,
            lambda f: pltpu.roll(band[f, side, k], 1, 1), lambda f: pltpu.roll(band[f, side, k], 127, 1), False)

    rows = [band_rate(0, 2), band_rate(0, 1), band_rate(1, 1), band_rate(1, 2)]
    zero = jnp.zeros((16, 128), jnp.float32)
    beside = [[zero, zero] for q in range(4)]
    for f in range(5):
        out = swap_blocks(swap_blocks([r[f] for r in rows], 0, 4, sub), 1, 32, lane)
        for q in range(4):
            edge[q, 5 + f] = out[q]
            for xq in range(4):
                place = 4 * f + xq
                spot = jnp.logical_and(lane % 32 == place, sub % 4 == xq)
                for side, to, shift in ((0, (q + 1) % 4, (place + 97) % 128), (1, (q + 3) % 4, place)):
                    beside[to][side] = jnp.where(spot, pltpu.roll(out[q], shift, 1), beside[to][side])
    for q in range(4):
        for side in range(2):
            b = beside[q][side]
            low = b + pltpu.roll(b, 15, 0)
            low = low + pltpu.roll(low, 14, 0)
            high = b + pltpu.roll(b, 1, 0)
            high = high + pltpu.roll(high, 2, 0)
            edge[q, 10 + side] = jnp.where(sub == 0, low, jnp.where(sub == 15, high, inner_ref[q, 5 + side]))
    for r, e in enumerate((e0, e1, e2, e3)):
        e[...] = edge[me ^ r]


def start_tiles_kernel(tlow_ref, thigh_ref, slow_ref, shigh_ref, wq_ref, wz_ref, _after, wxy_ref):
    me = lax.axis_index("node")
    sub, lane = iotas()
    lo, hi = reads(tlow_ref, thigh_ref)
    below, above = reads(slow_ref, shigh_ref)
    for f in range(5):
        a = pltpu.roll(lo(10 + f // 4), (5 - f % 4) % 4 * 32, 1)
        b = pltpu.roll(hi(10 + f // 4), (6 - f % 4) % 4 * 32, 1)
        wxy_ref[f] = jnp.where(
            lane < 32, wq_ref[f * 4], jnp.where(lane < 64, a, jnp.where(lane < 96, b, wq_ref[f * 4 + 3])))
        wxy_ref[5 + f, pl.ds(4, 4), :] = below(f, pl.ds(32, 4))
        wxy_ref[5 + f, pl.ds(8, 4), :] = above(f, pl.ds(32, 4))
        for xq in range(4):
            wxy_ref[5 + f, pl.ds(xq, 1), :] = wq_ref[f * 4 + xq, pl.ds(0, 1), :]
            wxy_ref[5 + f, pl.ds(12 + xq, 1), :] = wq_ref[f * 4 + xq, pl.ds(15, 1), :]
    for side in range(2):
        wxy_ref[10 + side] = wz_ref[side]


def second_kernel(a2, a3, power_ref, a0, a1, b0, b1, b2, b3, wq_ref, wxy_ref, slipq_ref,
                  o0, o1, o2, o3, main, xh, yh, zh, rates, table):
    me, t0, t7, s0, s7 = edges()
    sub, lane = iotas()
    power = power_ref[0:1, :]
    slip = slipq_ref[...]
    at_lower = jnp.logical_and(jnp.logical_and(sub >= 4, sub < 8), s0)
    at_upper = jnp.logical_and(jnp.logical_and(sub >= 8, sub < 12), s7)
    arrived, edge = (a0, a1, a2, a3), (b0, b1, b2, b3)
    weights = relative_weights(me)
    for m in range(4):
        for r in range(4):
            table[m * 4 + r] = weights[m][r]

    def node(m, _):
        weight = [table[m * 4 + r] for r in range(4)]

        def mix(refs, k):
            out = None
            for r, ref in enumerate(refs):
                term = weight[r] * (ref[pl.ds(14 * k, 16), :] if refs is arrived else ref[k])
                out = term if out is None else out + term
            return out

        outer = {}
        for p in range(2):
            a0, a3, b = (mix(arrived, 10 + 3 * p + k) for k in range(3))
            outer[2 * p] = a0, a3
            outer[2 * p + 1] = jnp.where(lane < 96, b, a3), jnp.where(
                lane < 32, a0, jnp.where(lane < 64, pltpu.roll(b, 32, 1), pltpu.roll(b, 96, 1)))
        outer[4] = mix(arrived, 16), mix(arrived, 17)

        for f in range(5):
            xb = wxy_ref[f] + mix(edge, f)
            yb = wxy_ref[5 + f] + mix(edge, 5 + f)
            yh[f] = yb
            for xq in range(4):
                tile = wq_ref[f * 4 + xq] + (mix(arrived, 2 * f + xq - 1) if xq in (1, 2) else outer[f][xq // 3])
                if xq == 0:
                    tile = jnp.where(lane < 32, xb, tile)
                if xq == 3:
                    tile = jnp.where(lane >= 96, xb, tile)
                tile = jnp.where(sub == 0, yh[f, pl.ds(xq, 1), :], tile)
                tile = jnp.where(sub == 15, yh[f, pl.ds(12 + xq, 1), :], tile)
                main[f, xq] = tile
            xh[f] = jnp.where(
                lane < 64, jnp.where(t0, main[f, 0], pltpu.roll(xb, 96, 1)),
                jnp.where(t7, main[f, 3], pltpu.roll(xb, 32, 1)))
            lower, upper = pltpu.roll(yb, 4, 0), pltpu.roll(yb, 12, 0)
            if f == 3:
                lower, upper = -lower, -upper
            if f in (2, 4):
                lower, upper = lower * slip, upper * slip
            yh[f] = jnp.where(at_lower, lower, jnp.where(at_upper, upper, yb))
        for xq in range(4):
            main[5, xq], main[6, xq], main[7, xq] = derived(main[0, xq], main[1, xq], power)
        xh[5], xh[6], xh[7] = derived(xh[0], xh[1], power)
        yh[5], yh[6], yh[7] = derived(yh[0], yh[1], power)
        for side in range(2):
            z = wxy_ref[10 + side] + mix(edge, 10 + side)
            zh[0, side] = z
            q, eta, _s = derived(z, pltpu.roll(z, 124, 1), power)
            zh[1, side], zh[2, side] = q, eta
        for xq in range(4):
            def left(f):
                if xq > 0:
                    return main[f, xq - 1]
                return jnp.where(lane < 32, xh[f], pltpu.roll(main[f, 3], 32, 1))

            def right(f):
                if xq < 3:
                    return main[f, xq + 1]
                return jnp.where(lane >= 96, xh[f], pltpu.roll(main[f, 0], 96, 1))

            def below(f):
                return jnp.where(sub == 0, yh[f, pl.ds(4 + xq, 1), :], pltpu.roll(main[f, xq], 1, 0))

            def above(f):
                return jnp.where(sub == 15, yh[f, pl.ds(8 + xq, 1), :], pltpu.roll(main[f, xq], 15, 0))

            def spot(f):
                return (0, 4 * f + xq) if f < 5 else (f - 4, xq)

            def before(f):
                k, i = spot(f)
                return jnp.where(lane % 32 == 0, pltpu.roll(zh[k, 0], (128 - i) % 128, 1), pltpu.roll(main[f, xq], 1, 1))

            def after(f):
                k, i = spot(f)
                return jnp.where(lane % 32 == 31, pltpu.roll(zh[k, 1], 31 - i, 1), pltpu.roll(main[f, xq], 127, 1))

            out = rate(lambda f: main[f, xq], left, right, below, above, before, after, True)
            for f in range(5):
                rates[m, f * 4 + xq] = out[f]
        return _

    lax.fori_loop(0, 4, node, 0, unroll=4)

    def combine(k, _):
        have = [rates[r, k] for r in range(4)]
        for m, o in enumerate((o0, o1, o2, o3)):
            out = wq_ref[k]
            for r in range(4):
                out = out + weights[m][r] * have[r]
            o[k] = out
        return _

    lax.fori_loop(0, 20, combine, 0, unroll=4)


def last_kernel(r2, r3, r1, r0, out_hbm, quarter, out, sems):
    me = lax.axis_index("node")
    _, lane = iotas()
    def copy(f):
        return pltpu.make_async_copy(out.at[f], out_hbm.at[f], sems.at[f])

    def field(f, _):
        for r, ref in enumerate((r0, r1, r2, r3)):
            quarter[me ^ r, pl.ds(4 * f, 4)] = ref[pl.ds(4 * f, 4)]
        for xq in range(4):
            tiles = swap_blocks([quarter[q, 4 * f + xq] for q in range(4)], 1, 32, lane)
            for g in range(4):
                out[f, 4 * g + xq] = tiles[g]
        copy(f).start()
        return _

    lax.fori_loop(0, 5, field, 0)
    for f in range(5):
        copy(f).wait()


def tiles_of(n):
    return jax.ShapeDtypeStruct((n, 16, 128), jnp.float32)


def shards(start_state, iterate, wall_flags, reg_index):
    state = iterate[0]
    flat = state.reshape(5, 256, 128)
    params = pltpu.CompilerParams(vmem_limit_bytes=32 * 1024 * 1024)
    scratch = lambda *shape: pltpu.VMEM(shape + (16, 128), jnp.float32)
    shape = lambda *dims: jax.ShapeDtypeStruct(dims, jnp.float32)
    dma = lambda n: pltpu.SemaphoreType.DMA((n,))

    def call(kernel, ins, outs, scratch_shapes=(), place=VMEM):
        return pl.pallas_call(
            kernel, out_shape=outs, in_specs=ins, out_specs=[place] * len(outs),
            scratch_shapes=scratch_shapes, compiler_params=params,
            cost_estimate=pl.CostEstimate(flops=1, bytes_accessed=1, transcendentals=0))

    def neighbours(up, down, axis):
        size = lax.axis_size(axis)
        from_lower = lax.ppermute(up, axis, [(i, (i + 1) % size) for i in range(size)])
        from_upper = lax.ppermute(down, axis, [((i + 1) % size, i) for i in range(size)])
        return from_lower, from_upper

    def send(tiles, r):
        return lax.ppermute(tiles, "node", [(i, i ^ r) for i in range(4)])

    far = lambda x: pltpu.with_memory_space_constraint(x, pltpu.HBM)
    slab_near, slab_next, slip = call(
        slab_kernel, [HBM] * 3, [shape(5, 40, 128)] * 2 + [shape(2, 16, 128)],
        [scratch(2, 5), pltpu.VMEM((2, 16, 128), jnp.int32), dma(7)])(
        far(wall_flags), far(state), far(start_state))
    power = jnp.broadcast_to(0.2 + 0.05 * reg_index.astype(jnp.float32), (8, 128))
    slab = neighbours(slab_near, slab_next, "slab")

    m0, m1, m2, m3, rates = call(
        first_kernel, [VMEM, VMEM, ANY], [shape(256, 128)] * 4 + [shape(5, 16, 16, 128)],
        [scratch(3, 16), scratch(4, 20)])(power, state, slip)
    a2, a3, a1 = send(m2, 2), send(m3, 3), send(m1, 1)

    tile = neighbours(*call(tile_kernel, [VMEM] * 2 + [ANY], [tiles_of(13)] * 2)(
        state, start_state, m2), "tile")

    inner, ext = call(
        inner_kernel, [VMEM] * 5, [shape(4, 7, 16, 128), shape(8, 8, 16, 128)])(power, flat, *tile, rates)

    corner = neighbours(*call(corner_kernel, [VMEM] * 3, [shape(16, 128)] * 2)(*slab, slip), "tile")

    e0, e1, e2, e3 = call(
        edge_kernel, [VMEM] * 9, [tiles_of(EDGE)] * 4,
        [pltpu.VMEM((8, 2, 24, 128), jnp.float32), scratch(8, 2, 4), scratch(4, EDGE)])(
        power, flat, *slab, *corner, slip, inner, ext)
    b2, b3, b1 = send(e2, 2), send(e3, 3), send(e1, 1)

    wq, wz, slipq = call(
        start_kernel, [VMEM, VMEM, ANY], [tiles_of(20), tiles_of(2), shape(16, 128)])(start_state, slip, e2)
    wxy, = call(start_tiles_kernel, [VMEM] * 6 + [ANY], [tiles_of(EDGE)])(*tile, *slab, wq, wz, e2)

    outs = call(
        second_kernel, [VMEM] * 12, [tiles_of(20)] * 4,
        [scratch(8, 4), scratch(8), scratch(8), scratch(3, 2), scratch(4, 20), pltpu.SMEM((16,), jnp.float32)])(
        a2, a3, power, m0, a1, e0, b1, b2, b3, wq, wxy, slipq)
    back = {r: send(outs[r], r) for r in (2, 3, 1)}

    result, = call(
        last_kernel, [VMEM] * 4, [shape(5, 16, 16, 128)], [scratch(4, 20), scratch(5, 16), dma(5)], HBM)(
        back[2], back[3], back[1], outs[0])
    return result[None]


def solution(mesh):
    return jax.shard_map(
        shards,
        mesh=mesh,
        in_specs=(
            P(None, "tile", "slab", None),
            P("node", None, "tile", "slab", None),
            P(None, "tile", None),
            P(),
        ),
        out_specs=P("node", None, "tile", "slab", None),
        check_vma=False,
    )
```
